32 devices in a mesh: dp: 4 (over x, core), seq: 8 (over z, y).
Axes of the slice: x: 2, y: 2, z: 4, core: 2. Of those that a mesh axis runs over, the one named last changes fastest.
Arguments:
- activations: bfloat16 [2, 4, 64, 256, 384], P(None, 'dp', 'seq'), may hold values from -11 to 11
- cotangent: bfloat16 [2, 4, 64, 256, 384], P(None, 'dp', None, 'seq'), may hold values from -11 to 11
- lengths: int32 [2, 4], P(None, 'dp'), may hold values from 64 to 256, as said below
- weight_in: float32 [2, 384, 3072], P(None, 'seq'), may hold values from -0.4375 to 0.4375
- weight_out: float32 [2, 384, 2048], P(None, 'seq')
- weight_small: float32 [2, 384, 10], P(None, 'seq')
- first_in: float32 [2, 384, 3072], P(None, 'seq')
- first_out: float32 [2, 384, 2048], P(None, 'seq')
- first_small: float32 [2, 384, 10], P(None, 'seq')
- second_in: float32 [2, 384, 3072], P(None, 'seq')
- second_out: float32 [2, 384, 2048], P(None, 'seq')
- second_small: float32 [2, 384, 10], P(None, 'seq')
Outputs:
- block_output: bfloat16 [2, 4, 64, 256, 384], P(None, 'dp', None, 'seq')
- input_grad: float32 [2, 4, 64, 256, 384], P(None, 'dp', 'seq')
- grad_norm: float32 [], replicated
- new_weight_in: float32 [2, 384, 3072], P(None, 'seq')
- new_weight_out: float32 [2, 384, 2048], P(None, 'seq')
- new_weight_small: float32 [2, 384, 10], P(None, 'seq')
- new_first_in: float32 [2, 384, 3072], P(None, 'seq')
- new_first_out: float32 [2, 384, 2048], P(None, 'seq')
- new_first_small: float32 [2, 384, 10], P(None, 'seq')
- new_second_in: float32 [2, 384, 3072], P(None, 'seq')
- new_second_out: float32 [2, 384, 2048], P(None, 'seq')
- new_second_small: float32 [2, 384, 10], P(None, 'seq')
- copy_weight_in: bfloat16 [2, 384, 3072], P(None, 'seq')
- copy_weight_out: bfloat16 [2, 384, 2048], P(None, 'seq')
- copy_weight_small: bfloat16 [2, 384, 10], P(None, 'seq')
The draws below stay inside these ranges and needn't reach their ends.
Inputs may be any that keep to these rules, and one draw needn't show every extreme that they name: lengths[m, c] counts the valid frames of clip c in micro-batch m; frames from it on are padding. For every clip index c some micro-batch has length 256.
All inputs are finite; a program needn't handle non-finite values.
Results may differ from the reference program's by a relative error of at most 0.03.
The reference program's roundings to bfloat16 on the way count: a program that leaves them out, or rounds other values in their place, can miss the bound.
Values may be sent and summed in bfloat16 or wider, within the bound.
A program may use at most 576 MiB of HBM per device.

```python
import math
import jax
import jax.numpy as jnp
from jax import lax

D = 384
HEAD_COUNT = 8
HEAD_DIM = 64
FF = 1536
INNER_WIDTH = 512
BANDS = 64
FRAMES = 256
MICRO = 2
STEP = 10
CLIPS = 4


CLIP_NORM = 1.0


def feature_profile(top_scale):
    return jnp.exp(jnp.linspace(0.0, math.log(top_scale), D))


def clipped_entry():
    total_params = 2 * D * (3 * INNER_WIDTH + FF) + 2 * D * (INNER_WIDTH + FF) + 2 * D * (HEAD_COUNT + 2)
    return CLIP_NORM / math.sqrt(total_params)


def first_state(key, columns, boost):
    base_draw = jax.random.normal(key, (2, D, columns), jnp.float32)
    return 0.1 / 0.9 * boost * clipped_entry() * jnp.clip(base_draw, -5.0, 5.0)


def second_state(key, columns, boost):
    spread = jnp.exp(jax.random.uniform(key, (2, D, columns), jnp.float32, math.log(0.5), math.log(8.0)))
    return 0.001 / 0.999 * (boost * clipped_entry()) ** 2 * spread


def draw_activations(key, part):
    key = jax.random.fold_in(key, 1)
    full_shape = (MICRO, CLIPS, BANDS, FRAMES, D)
    base_draw = jnp.clip(jax.random.normal(key, full_shape, jnp.float32), -6.0, 6.0)
    top_scale = 1.73
    return (base_draw * feature_profile(top_scale)).astype(jnp.bfloat16)


def draw_cotangent(key, part):
    key = jax.random.fold_in(key, 2)
    full_shape = (MICRO, CLIPS, BANDS, FRAMES, D)
    base_draw = jnp.clip(jax.random.normal(key, full_shape, jnp.float32), -6.0, 6.0)
    top_scale = 1.73
    return (base_draw * feature_profile(top_scale)).astype(jnp.bfloat16)


def draw_lengths(key, part):
    key = jax.random.fold_in(key, 3)
    base_key, pick_key = jax.random.split(key)
    drawn = jax.random.randint(base_key, (MICRO, CLIPS), FRAMES // 4, FRAMES + 1)
    chosen = jax.random.randint(pick_key, (CLIPS,), 0, MICRO)
    full_rows = jnp.arange(MICRO)[:, None] == chosen[None, :]
    return jnp.where(full_rows, FRAMES, drawn).astype(jnp.int32)


def draw_weight_out(key, part):
    key = jax.random.fold_in(key, 4)
    base_draw = jnp.clip(jax.random.normal(key, (2, D, INNER_WIDTH + FF), jnp.float32), -5.0, 5.0)
    column = jnp.arange(INNER_WIDTH + FF)
    spread = jnp.where(column < INNER_WIDTH, 4.0 / math.sqrt(INNER_WIDTH), 1.4 / math.sqrt(FF))
    return base_draw * spread


def draw_weight_small(key, part):
    key = jax.random.fold_in(key, 5)
    gate_key, gain_key = jax.random.split(key)
    gate_part = jnp.clip(jax.random.normal(gate_key, (2, D, HEAD_COUNT + 2), jnp.float32), -5.0, 5.0) * (1.5 / math.sqrt(D))
    gain_part = jax.random.uniform(gain_key, (2, D, HEAD_COUNT + 2), jnp.float32, 0.6, 1.4)
    column = jnp.arange(HEAD_COUNT + 2)
    return jnp.where(column < HEAD_COUNT, gate_part, gain_part)


def draw_first_in(key, part):
    key = jax.random.fold_in(key, 6)
    return first_state(key, 3 * INNER_WIDTH + FF, 1.0)


def draw_first_out(key, part):
    key = jax.random.fold_in(key, 7)
    return first_state(key, INNER_WIDTH + FF, 1.0)


def draw_first_small(key, part):
    key = jax.random.fold_in(key, 8)
    return first_state(key, HEAD_COUNT + 2, 5.0)


def draw_second_in(key, part):
    key = jax.random.fold_in(key, 9)
    return second_state(key, 3 * INNER_WIDTH + FF, 1.0)


def draw_second_out(key, part):
    key = jax.random.fold_in(key, 10)
    return second_state(key, INNER_WIDTH + FF, 1.0)


def draw_second_small(key, part):
    key = jax.random.fold_in(key, 11)
    return second_state(key, HEAD_COUNT + 2, 5.0)


def block_levels(stream_key, shape, shards, least, top_value):
    factor_of = 1.0
    for dim, blocks in shards:
        draws = jax.random.uniform(jax.random.fold_in(jax.random.fold_in(stream_key, 6), dim), (blocks,), jnp.float32, least / len(shards), top_value / len(shards))
        factor_of = factor_of * jnp.repeat(jnp.exp(draws), shape[dim] // blocks).reshape((-1,) + (1,) * (len(shape) - 1 - dim))
    return factor_of


def normal_values(rng, shape, deviation, reach, cuts=(), kind=jnp.bfloat16):
    values = deviation * jax.random.normal(rng, shape, jnp.float32)
    if cuts:
        values = values * block_levels(rng, shape, cuts, -0.22, 0.18)
    return jnp.clip(values, -reach, reach).astype(kind)


def setup_inputs(seed: int = 0) -> dict:
    key_of = jax.random.split(jax.random.key(seed), 13)
    return {
        "activations": draw_activations(jax.random.fold_in(key_of[12], 71), 0),
        "cotangent": draw_cotangent(jax.random.fold_in(key_of[12], 71), 0),
        "lengths": draw_lengths(jax.random.fold_in(key_of[12], 71), 0),
        "weight_in": normal_values(key_of[3], (2, D, 3 * INNER_WIDTH + FF), (D // 2) ** -0.5, 0.4375, ((1, 8),), jnp.float32),
        "weight_out": draw_weight_out(jax.random.fold_in(key_of[12], 71), 0),
        "weight_small": draw_weight_small(jax.random.fold_in(key_of[12], 71), 0),
        "first_in": draw_first_in(jax.random.fold_in(key_of[12], 71), 0),
        "first_out": draw_first_out(jax.random.fold_in(key_of[12], 71), 0),
        "first_small": draw_first_small(jax.random.fold_in(key_of[12], 71), 0),
        "second_in": draw_second_in(jax.random.fold_in(key_of[12], 71), 0),
        "second_out": draw_second_out(jax.random.fold_in(key_of[12], 71), 0),
        "second_small": draw_second_small(jax.random.fold_in(key_of[12], 71), 0),
    }


EPS_NORM = 1e-06
BETA_ONE = 0.9
BETA_TWO = 0.999
ADAM_EPS = 1e-08
DECAY = 0.1
RATE_MATRIX = 0.1
RATE_GATE = 0.1
RATE_GAIN = 0.5
CLIP_NORM = 1.0
PRECISE_MATMUL = lax.Precision.HIGHEST
MASKED = -1e+30

@jax.custom_vjp
def low(v):
    return lax.optimization_barrier(v.astype(jnp.bfloat16)).astype(jnp.float32)

@jax.custom_vjp
def lowered_backward(v):
    return v

def low_keep(v):
    return (low(v), None)

def low_pass(kept, grad):
    return (grad,)

def back_keep(v):
    return (v, None)

def back_low(kept, grad):
    return (low(grad),)
low.defvjp(low_keep, low_pass)
lowered_backward.defvjp(back_keep, back_low)

def rounded(values):
    return lax.optimization_barrier(values.astype(jnp.bfloat16)).astype(jnp.float32)

def rotary_tables(positions, head_width):
    half_width = head_width // 2
    inverse = 10000.0 ** (-(jnp.arange(half_width, dtype=jnp.float32) * 2.0 / head_width))
    angles = jnp.arange(positions, dtype=jnp.float32)[:, None] * inverse[None, :]
    return (jnp.cos(angles), jnp.sin(angles))

def rotate(tensor, cosine, sine_part):
    half_width = tensor.shape[-1] // 2
    leading = tensor[..., :half_width]
    trailing = tensor[..., half_width:]
    cos_wide = cosine[:, None, :]
    sin_wide = sine_part[:, None, :]
    return jnp.concatenate([leading * cos_wide - trailing * sin_wide, trailing * cos_wide + leading * sin_wide], axis=-1)

def rms_norm(values, gain_row):
    return values * lax.rsqrt(lax.optimization_barrier(jnp.mean(values * values, axis=-1, keepdims=True)) + EPS_NORM) * gain_row

def attend_group(block_args):
    queries, key_part, value_part, key_valid = block_args
    scale = queries.shape[-1] ** (-0.5)
    scores = lowered_backward(jnp.einsum('gqhe,gkhe->ghqk', queries, key_part, precision=PRECISE_MATMUL) * scale)
    scores = jnp.where(key_valid[:, None, None, :] > 0, scores, MASKED)
    attn_probs = low(jax.nn.softmax(scores, axis=-1))
    return jnp.einsum('ghqk,gkhe->gqhe', attn_probs, value_part, precision=PRECISE_MATMUL)

def attention(queries, key_part, value_part, key_valid):
    seq_count, length = (queries.shape[0], queries.shape[1])
    group_size = math.gcd(seq_count, max(1, 1024 // length))

    def to_groups(tensor):
        return tensor.reshape((seq_count // group_size, group_size) + tensor.shape[1:])
    result = lax.map(jax.checkpoint(attend_group), (to_groups(queries), to_groups(key_part), to_groups(value_part), to_groups(key_valid)))
    return result.reshape(queries.shape)

def sublayer(residual_state, layer_input_weight, layer_output_weight, layer_small_weight, key_valid, cosine, sine_part):
    seq_count, length, model_width = residual_state.shape
    shape_heads = (seq_count, length, HEAD_COUNT, HEAD_DIM)
    normed_rows = low(rms_norm(residual_state, layer_small_weight[:, HEAD_COUNT]))
    projected_rows = jnp.einsum('zka,ao->zko', normed_rows, layer_input_weight[:, :3 * INNER_WIDTH], precision=PRECISE_MATMUL)
    queries = low(rotate(lowered_backward(projected_rows[..., :INNER_WIDTH]).reshape(shape_heads), cosine, sine_part))
    key_part = low(rotate(lowered_backward(projected_rows[..., INNER_WIDTH:2 * INNER_WIDTH]).reshape(shape_heads), cosine, sine_part))
    value_part = low(lowered_backward(projected_rows[..., 2 * INNER_WIDTH:]).reshape(shape_heads))
    gate_sigmoid = jax.nn.sigmoid(jnp.einsum('cvj,jn->cvn', normed_rows, layer_small_weight[:, :HEAD_COUNT], precision=PRECISE_MATMUL))
    attended = lowered_backward(attention(queries, key_part, value_part, key_valid))
    gated_output = low((attended * gate_sigmoid[..., None]).reshape(seq_count, length, INNER_WIDTH))
    middle_state = residual_state + lowered_backward(jnp.einsum('qxi,bi->qxb', gated_output, layer_output_weight[:, :INNER_WIDTH], precision=PRECISE_MATMUL))
    normed_feedforward = low(rms_norm(middle_state, layer_small_weight[:, HEAD_COUNT + 1]))
    hidden_rows = lowered_backward(jnp.einsum('zka,ao->zko', normed_feedforward, layer_input_weight[:, 3 * INNER_WIDTH:], precision=PRECISE_MATMUL))
    activated_hidden = low(jax.nn.gelu(hidden_rows, approximate=False))
    return middle_state + lowered_backward(jnp.einsum('zui,ai->zua', activated_hidden, layer_output_weight[:, INNER_WIDTH:], precision=PRECISE_MATMUL))

def clip_forward(residual_state, weights, valid_frames, time_tables, band_tables):
    layer_input_weight, layer_output_weight, layer_small_weight = weights
    time_valid = jnp.broadcast_to(valid_frames[None, :], (BANDS, FRAMES))
    middle_state = sublayer(residual_state, layer_input_weight[0], layer_output_weight[0], layer_small_weight[0], time_valid, time_tables[0], time_tables[1])
    middle_state = lowered_backward(low(middle_state))
    across = jnp.swapaxes(middle_state, 0, 1)
    band_valid = jnp.ones((FRAMES, BANDS), jnp.float32)
    final = sublayer(across, layer_input_weight[1], layer_output_weight[1], layer_small_weight[1], band_valid, band_tables[0], band_tables[1])
    return jnp.swapaxes(final, 0, 1) * valid_frames[None, :, None]

def adam_step(master, gradient, first_old, second_old, learn_rate):
    first_new = BETA_ONE * first_old + (1.0 - BETA_ONE) * gradient
    second_new = BETA_TWO * second_old + (1.0 - BETA_TWO) * gradient * gradient
    first_hat = first_new / (1.0 - BETA_ONE ** STEP)
    second_hat = second_new / (1.0 - BETA_TWO ** STEP)
    updated = master - learn_rate * (first_hat / (jnp.sqrt(second_hat) + ADAM_EPS) + DECAY * master)
    return (updated, first_new, second_new)

def reference(activations, cotangent, lengths, weight_in, weight_out, weight_small, first_in, first_out, first_small, second_in, second_out, second_small):
    masters = (weight_in, weight_out, weight_small)
    working = tuple((rounded(master) for master in masters))
    time_tables = rotary_tables(FRAMES, HEAD_DIM)
    band_tables = rotary_tables(BANDS, HEAD_DIM)

    def one_clip(totals, clip_item):
        residual_state, back_grad, frame_count = clip_item
        valid_frames = (jnp.arange(FRAMES) < frame_count).astype(jnp.float32)

        def forward(stream_in, weights):
            return clip_forward(stream_in, weights, valid_frames, time_tables, band_tables)
        output, pullback = jax.vjp(forward, residual_state.astype(jnp.float32), working)
        d_stream, d_weights = pullback(back_grad.astype(jnp.float32))
        totals = jax.tree.map(jnp.add, totals, d_weights)
        return (totals, (output.astype(jnp.bfloat16), d_stream))
    zeros = tuple((jnp.zeros(master.shape, jnp.float32) for master in masters))
    clip_shape = (MICRO * CLIPS, BANDS, FRAMES, D)
    grads, (outputs, d_inputs) = lax.scan(one_clip, zeros, (activations.reshape(clip_shape), cotangent.reshape(clip_shape), lengths.reshape(MICRO * CLIPS)))
    block_output = outputs.reshape(activations.shape)
    input_grad = d_inputs.reshape(activations.shape)
    grad_norm = jnp.sqrt(sum((jnp.sum(gradient * gradient) for gradient in grads)))
    factor = jnp.minimum(1.0, CLIP_NORM / (grad_norm + 1e-06))
    small_rate = jnp.where(jnp.arange(HEAD_COUNT + 2) < HEAD_COUNT, RATE_GATE, RATE_GAIN)
    new_in = adam_step(weight_in, grads[0] * factor, first_in, second_in, RATE_MATRIX)
    new_out = adam_step(weight_out, grads[1] * factor, first_out, second_out, RATE_MATRIX)
    new_small = adam_step(weight_small, grads[2] * factor, first_small, second_small, small_rate)
    return (block_output, input_grad, grad_norm, new_in[0], new_out[0], new_small[0], new_in[1], new_out[1], new_small[1], new_in[2], new_out[2], new_small[2], new_in[0].astype(jnp.bfloat16), new_out[0].astype(jnp.bfloat16), new_small[0].astype(jnp.bfloat16))
```

```python
from functools import partial
import math

import jax
import jax.numpy as jnp
from jax import lax
from jax.experimental import pallas as pl
from jax.experimental.pallas import tpu as pltpu
from jax.sharding import PartitionSpec as P

HEAD_COUNT = 8
HEAD_DIM = 64
INNER_WIDTH = 512
STEP = 10
EPS_NORM = 1e-06
BETA_ONE = 0.9
BETA_TWO = 0.999
ADAM_EPS = 1e-08
DECAY = 0.1
RATE_MATRIX = 0.1
RATE_GATE = 0.1
RATE_GAIN = 0.5
CLIP_NORM = 1.0
MASKED = -1e30

BF = jnp.bfloat16
F32 = jnp.float32
GROUP = 256
BLOCK = 256
LANES = 128
LOG2E = 1.4426950408889634
SCORE_EXP = LOG2E / math.sqrt(HEAD_DIM)
SQRT_HALF = math.sqrt(0.5)
GAUSS = 1.0 / math.sqrt(2.0 * math.pi)
VMEM_LIMIT = 60 * 2**20


def nn(a, b):
    return lax.dot_general(a, b, (((1,), (0,)), ((), ())), preferred_element_type=F32)


def nt(a, b):
    return lax.dot_general(a, b, (((1,), (1,)), ((), ())), preferred_element_type=F32)


def tn(a, b):
    return lax.dot_general(a, b, (((0,), (0,)), ((), ())), preferred_element_type=F32)


def iota(shape, dim):
    return lax.broadcasted_iota(jnp.int32, shape, dim)


def split_rows(rows):
    high = rows.astype(BF)
    rest = (rows - high.astype(F32)).astype(BF)
    return jnp.concatenate([high, rest], axis=0)


def head_lanes():
    shape = (2 * HEAD_COUNT, INNER_WIDTH)
    return (iota(shape, 1) // HEAD_DIM == iota(shape, 0) % HEAD_COUNT).astype(F32).astype(BF)


def inverse_rms(rows):
    return lax.rsqrt(jnp.mean(rows * rows, axis=-1, keepdims=True) + EPS_NORM)


def norm_back(rows, gain, grad):
    inverse = inverse_rms(rows)
    unit = rows * inverse
    scaled = grad * gain
    d_rows = inverse * (scaled - unit * jnp.mean(scaled * unit, axis=-1, keepdims=True))
    return d_rows, jnp.sum(grad * unit, axis=0, keepdims=True)


def half_lanes(h):
    return (iota((BLOCK, GROUP), 1) % LANES) // (HEAD_DIM // 2) == h


def whole_lanes(h):
    return iota((BLOCK, GROUP), 1) // HEAD_DIM == h


def picked(mask, tensor):
    return jnp.where(mask, tensor, jnp.zeros_like(tensor))


def group_slice(g):
    return slice(g * GROUP, (g + 1) * GROUP)


def forward_block(x, w_ref, small, cos, sin, key_mask, keep, rows, item, width_ff):
    gate_weight, gain_attn, gain_ff = small
    normed = (x * inverse_rms(x) * gain_attn).astype(BF)
    if "normed" in keep:
        keep["normed"][rows, :] = normed
    gate_rows = jax.nn.sigmoid(nt(gate_weight, normed))
    keep["gate"][item] = gate_rows
    half = GROUP // 2
    for g in range(2):
        for part, name in ((0, "q"), (1, "k")):
            start = part * INNER_WIDTH + g * GROUP
            t = nn(normed, w_ref[:, start : start + GROUP])
            a, b = t[:, :half], t[:, half:]
            keep[name][rows, g * GROUP : g * GROUP + half] = (a * cos - b * sin).astype(BF)
            keep[name][rows, g * GROUP + half : (g + 1) * GROUP] = (b * cos + a * sin).astype(BF)
        start = 2 * INNER_WIDTH + g * GROUP
        keep["v"][rows, group_slice(g)] = nn(normed, w_ref[:, start : start + GROUP]).astype(BF)
    gate = tn(split_rows(gate_rows), head_lanes())
    for g in range(2):
        lanes = group_slice(g)
        queries, keys = keep["q"][rows, lanes], keep["k"][rows, lanes]
        values = keep["v"][rows, lanes]
        attended = None
        for h in range(4):
            scores = nt(picked(half_lanes(h), keys), queries)
            scores = jnp.where(key_mask, scores, MASKED)
            peak = jnp.max(scores, axis=0, keepdims=True)
            terms = jnp.exp2((scores - peak) * SCORE_EXP)
            probs = (terms * (1.0 / jnp.sum(terms, axis=0, keepdims=True))).astype(BF)
            keep["probs"][item, g * 4 + h] = probs
            part = tn(probs, picked(whole_lanes(h), values))
            attended = part if attended is None else attended + part
        keep["gated"][rows, lanes] = (attended * gate[:, lanes]).astype(BF)
    out_start = 3 * INNER_WIDTH + width_ff
    middle = x + nt(keep["gated"][rows, :], w_ref[:, out_start : out_start + INNER_WIDTH])
    keep["middle"][rows, :] = middle
    normed_ff = (middle * inverse_rms(middle) * gain_ff).astype(BF)
    if "normed_ff" in keep:
        keep["normed_ff"][rows, :] = normed_ff
    result = middle
    for c in range(width_ff // GROUP):
        up = 3 * INNER_WIDTH + c * GROUP
        down = out_start + INNER_WIDTH + c * GROUP
        hidden = nn(normed_ff, w_ref[:, up : up + GROUP])
        cumulative = 0.5 + 0.5 * lax.erf(hidden * SQRT_HALF)
        activated = (hidden * cumulative).astype(BF)
        density = jnp.exp2(hidden * hidden * (-0.5 * LOG2E)) * GAUSS
        keep["act"][rows, group_slice(c)] = activated
        keep["slope"][rows, group_slice(c)] = (cumulative + hidden * density).astype(BF)
        result = result + nt(activated, w_ref[:, down : down + GROUP])
    return result


def backward_block(d_out, x, w_ref, small, cos, sin, keep, work, sums, rows, item, width_ff):
    gate_weight, gain_attn, gain_ff = small
    branch = d_out.astype(BF)
    work["branch"][rows, :] = branch
    out_start = 3 * INNER_WIDTH + width_ff
    d_normed_ff = None
    for c in range(width_ff // GROUP):
        up = 3 * INNER_WIDTH + c * GROUP
        down = out_start + INNER_WIDTH + c * GROUP
        d_act = nn(branch, w_ref[:, down : down + GROUP])
        d_hidden = (d_act * keep["slope"][rows, group_slice(c)].astype(F32)).astype(BF)
        work["d_hidden"][rows, group_slice(c)] = d_hidden
        part = nt(d_hidden, w_ref[:, up : up + GROUP])
        d_normed_ff = part if d_normed_ff is None else d_normed_ff + part
    middle = keep["middle"][rows, :]
    d_rows, d_gain_ff = norm_back(middle, gain_ff, d_normed_ff)
    d_middle = d_out + d_rows
    attn_back = d_middle.astype(BF)
    work["attn_back"][rows, :] = attn_back
    gate_rows = keep["gate"][item]
    lanes_of = head_lanes()
    gate = tn(split_rows(gate_rows), lanes_of)
    d_gated = nn(attn_back, w_ref[:, out_start : out_start + INNER_WIDTH])
    product = d_gated * keep["gated"][rows, :].astype(F32)
    high = product.astype(BF)
    rest = (product - high.astype(F32)).astype(BF)
    delta_rows = (nt(lanes_of, high) + nt(lanes_of, rest))[:HEAD_COUNT]
    d_logit = split_rows(delta_rows * (1.0 - gate_rows))
    d_attended = (d_gated * gate).astype(BF)
    half = GROUP // 2
    scale = HEAD_DIM**-0.5
    for g in range(2):
        lanes = group_slice(g)
        queries, keys = keep["q"][rows, lanes], keep["k"][rows, lanes]
        values, d_att = keep["v"][rows, lanes], d_attended[:, lanes]
        d_query = d_keys = d_values = None
        for h in range(4):
            halves, wholes = half_lanes(h), whole_lanes(h)
            key_h = picked(halves, keys)
            probs = keep["probs"][item, g * 4 + h]
            d_probs = nt(picked(wholes, values), d_att)
            delta = delta_rows[g * 4 + h : g * 4 + h + 1, :]
            d_scores = (probs.astype(F32) * (d_probs - delta)).astype(BF)
            part_v = nn(probs, picked(wholes, d_att))
            part_k = nn(d_scores, picked(halves, queries))
            part_q = tn(d_scores, key_h)
            if h == 0:
                d_query, d_keys, d_values = part_q, part_k, part_v
            else:
                d_query, d_keys, d_values = d_query + part_q, d_keys + part_k, d_values + part_v
        for start, t in ((0, d_query), (INNER_WIDTH, d_keys)):
            t = t * scale
            a, b = t[:, :half], t[:, half:]
            start = start + g * GROUP
            work["d_proj"][rows, start : start + half] = (a * cos + b * sin).astype(BF)
            work["d_proj"][rows, start + half : start + GROUP] = (b * cos - a * sin).astype(BF)
        start = 2 * INNER_WIDTH + g * GROUP
        work["d_proj"][rows, start : start + GROUP] = d_values.astype(BF)
    twice = jnp.concatenate([gate_weight, gate_weight], axis=0)
    d_normed = tn(d_logit, twice)
    for c in range(3 * INNER_WIDTH // INNER_WIDTH):
        part = slice(c * INNER_WIDTH, (c + 1) * INNER_WIDTH)
        d_normed = d_normed + nt(work["d_proj"][rows, part], w_ref[:, part])
    d_rows, d_gain_attn = norm_back(x, gain_attn, d_normed)
    d_gate = nn(d_logit, work["normed"][rows, :])
    sums[0:HEAD_COUNT, :] += d_gate[:HEAD_COUNT] + d_gate[HEAD_COUNT:]
    sums[HEAD_COUNT : HEAD_COUNT + 1, :] += d_gain_attn
    sums[HEAD_COUNT + 1 : HEAD_COUNT + 2, :] += d_gain_ff
    return d_middle + d_rows


def weight_sums(total, work, keep, width_ff):
    out_start = 3 * INNER_WIDTH + width_ff
    pairs = (
        (work["normed"], work["d_proj"], 0),
        (work["normed_ff"], work["d_hidden"], 3 * INNER_WIDTH),
        (work["attn_back"], keep["gated"], out_start),
        (work["branch"], keep["act"], out_start + INNER_WIDTH),
    )
    for left, right, start in pairs:
        turned = left[...].T
        for c in range(right.shape[-1] // INNER_WIDTH):
            part = slice(start + c * INNER_WIDTH, start + (c + 1) * INNER_WIDTH)
            total[:, part] += nn(turned, right[:, c * INNER_WIDTH : (c + 1) * INNER_WIDTH])


def small_parts(small_ref):
    gate_weight = small_ref[0:HEAD_COUNT, :].astype(BF)
    return (
        gate_weight,
        small_ref[HEAD_COUNT : HEAD_COUNT + 1, :],
        small_ref[HEAD_COUNT + 1 : HEAD_COUNT + 2, :],
    )


def finish_sums(total, sums, out_ref):
    width = total.shape[1] - LANES
    model = total.shape[0]
    out_ref[:, :width] = total[:, :width].astype(out_ref.dtype)
    tall = jnp.concatenate([sums[...], jnp.zeros((LANES - sums.shape[0], model), F32)], axis=0)
    out_ref[:, width:] = tall.T.astype(out_ref.dtype)


def start_sums(total, sums, before_ref, arrival):
    sums[...] = jnp.zeros_like(sums)
    if before_ref is None:
        total[...] = jnp.zeros_like(total)
    else:
        pltpu.make_async_copy(before_ref, total, arrival).start()


def await_sums(total, sums, before_ref, arrival):
    if before_ref is not None:
        width = total.shape[1] - LANES
        pltpu.make_async_copy(before_ref, total, arrival).wait()
        sums[...] += total[:, width:].T[: sums.shape[0]]


SAVED = ("q", "k", "v", "gate", "probs", "gated", "middle", "act", "slope")


def time_forward_kernel(width_ff, len_ref, x_ref, w_ref, small_ref, cos_ref, sin_ref, out_ref, *saved):
    keep = dict(zip(SAVED, saved))
    keys = iota((BLOCK, BLOCK), 0) < len_ref[0]
    x = x_ref[0].astype(F32)
    out = forward_block(
        x, w_ref, small_parts(small_ref), cos_ref[...], sin_ref[...], keys, keep, slice(None), 0, width_ff
    )
    parts, unused, frames, model = out_ref.shape
    out_ref[:, 0] = out.reshape(parts, frames, model).astype(BF)


def time_backward_kernel(width_ff, chained, per_step, *refs):
    x_ref, d_ref, w_ref, small_ref, cos_ref, sin_ref = refs[:6]
    keep = dict(zip(SAVED, refs[6:15]))
    refs = refs[15:]
    before = refs[0] if chained else None
    dx_ref, grad_ref = refs[1:3] if chained else refs[:2]
    total, sums, normed, normed_ff, d_hidden, attn_back, branch, d_proj, arrival = refs[-9:]
    work = dict(
        normed=normed, normed_ff=normed_ff, d_hidden=d_hidden, attn_back=attn_back, branch=branch, d_proj=d_proj
    )
    step = pl.program_id(0)

    @pl.when(step == 0)
    def _():
        start_sums(total, sums, before, arrival)

    small = small_parts(small_ref)

    def one(i, carry):
        rows = pl.ds(pl.multiple_of(i * BLOCK, BLOCK), BLOCK)
        x = x_ref[i].astype(F32)
        work["normed"][rows, :] = (x * inverse_rms(x) * small[1]).astype(BF)
        middle = keep["middle"][rows, :]
        work["normed_ff"][rows, :] = (middle * inverse_rms(middle) * small[2]).astype(BF)
        d_out = d_ref[:, i].astype(F32).reshape(BLOCK, x.shape[1])
        dx_ref[i] = backward_block(
            d_out, x, w_ref, small, cos_ref[...], sin_ref[...], keep, work, sums, rows, i, width_ff
        )
        return carry

    lax.fori_loop(0, per_step, one, 0)
    if chained:

        @pl.when(step == 0)
        def _():
            await_sums(total, sums, before, arrival)

    weight_sums(total, work, keep, width_ff)

    @pl.when(step == pl.num_programs(0) - 1)
    def _():
        finish_sums(total, sums, grad_ref)


def gather_rows(ref, strides, factors):
    return jnp.concatenate(
        [
            jnp.concatenate([ref[p, s, :] * f for p in range(ref.shape[0])], axis=1)
            for s, f in zip(strides, factors)
        ],
        axis=0,
    )


def band_kernel(width_ff, chained, info_ref, *refs):
    x_ref, d_ref, w_ref, small_ref, cos_ref, sin_ref = refs[:6]
    refs = refs[6:]
    before = refs[0] if chained else None
    out_ref, back_ref, grad_ref = refs[1:4] if chained else refs[:3]
    scratch = refs[-20:]
    keep = dict(zip(SAVED, scratch[:9]))
    total, sums, normed, normed_ff, d_hidden, attn_back, branch, d_proj, arrival, rows_a, rows_b = scratch[9:]
    work = dict(
        normed=normed, normed_ff=normed_ff, d_hidden=d_hidden, attn_back=attn_back, branch=branch, d_proj=d_proj
    )
    keep.update(normed=normed, normed_ff=normed_ff)
    step = pl.program_id(0)
    bands, frames, model = x_ref.shape
    together = BLOCK // bands
    pieces = model // LANES

    @pl.when(step == 0)
    def _():
        start_sums(total, sums, before, arrival)

    small = small_parts(small_ref)
    for p in range(pieces):
        lanes = slice(p * LANES, (p + 1) * LANES)
        rows_a[p] = x_ref[:, :, lanes].astype(F32).reshape(bands * frames, LANES)
        rows_b[p] = d_ref[:, :, lanes].astype(F32).reshape(bands * frames, LANES)
    same = iota((BLOCK, BLOCK), 0) // bands == iota((BLOCK, BLOCK), 1) // bands
    first = info_ref[1] + step * frames

    def one(j, carry):
        rows = pl.ds(pl.multiple_of(j * BLOCK, BLOCK), BLOCK)
        strides = [pl.ds(j * together + f, bands, stride=frames) for f in range(together)]
        valid = [
            (first + j * together + f < info_ref[0]).astype(F32) for f in range(together)
        ]
        x = gather_rows(rows_a, strides, [1.0] * together)
        d_out = gather_rows(rows_b, strides, valid)
        out = forward_block(
            x, w_ref, small, cos_ref[...], sin_ref[...], same, keep, rows, j, width_ff
        )
        for f in range(together):
            for p in range(pieces):
                part = out[f * bands : (f + 1) * bands, p * LANES : (p + 1) * LANES]
                rows_a[p, strides[f], :] = part * valid[f]
        back = backward_block(
            d_out, x, w_ref, small, cos_ref[...], sin_ref[...], keep, work, sums, rows, j, width_ff
        )
        for f in range(together):
            for p in range(pieces):
                part = back[f * bands : (f + 1) * bands, p * LANES : (p + 1) * LANES]
                rows_b[p, strides[f], :] = part
        return carry

    lax.fori_loop(0, frames // together, one, 0)
    for p in range(pieces):
        lanes = slice(p * LANES, (p + 1) * LANES)
        out_ref[:, :, lanes] = rows_a[p].reshape(bands, frames, LANES).astype(BF)
        back_ref[:, :, lanes] = rows_b[p].reshape(bands, frames, LANES).astype(BF)
    if chained:

        @pl.when(step == 0)
        def _():
            await_sums(total, sums, before, arrival)

    weight_sums(total, work, keep, width_ff)

    @pl.when(step == pl.num_programs(0) - 1)
    def _():
        finish_sums(total, sums, grad_ref)


def whole(shape):
    return pl.BlockSpec(shape, lambda *i: (0,) * len(shape), pipeline_mode=pl.Buffered(1))


def params(**more):
    return pltpu.CompilerParams(vmem_limit_bytes=VMEM_LIMIT, **more)


def rotary_tables(positions):
    half_width = HEAD_DIM // 2
    inverse = 10000.0 ** (-(jnp.arange(half_width, dtype=F32) * 2.0 / HEAD_DIM))
    angles = jnp.arange(positions, dtype=F32)[:, None] * inverse[None, :]
    angles = jnp.tile(angles, (BLOCK // positions, LANES // half_width))
    return (jnp.cos(angles), jnp.sin(angles))


def saved_shapes(tokens, items, model, width_ff):
    return (
        ((tokens, INNER_WIDTH), BF),
        ((tokens, INNER_WIDTH), BF),
        ((tokens, INNER_WIDTH), BF),
        ((items, HEAD_COUNT, BLOCK), F32),
        ((items, HEAD_COUNT, BLOCK, BLOCK), BF),
        ((tokens, INNER_WIDTH), BF),
        ((tokens, model), F32),
        ((tokens, width_ff), BF),
        ((tokens, width_ff), BF),
    )


def saved_specs(tokens, items, model, width_ff):
    return [
        pl.BlockSpec(shape, lambda i, *s, n=len(shape): (i,) + (0,) * (n - 1))
        for shape, kind in saved_shapes(tokens, items, model, width_ff)
    ]


def work_shapes(tokens, model, width_ff, columns):
    return [
        pltpu.VMEM((model, columns), F32),
        pltpu.VMEM((2 * HEAD_COUNT, model), F32),
        pltpu.VMEM((tokens, model), BF),
        pltpu.VMEM((tokens, model), BF),
        pltpu.VMEM((tokens, width_ff), BF),
        pltpu.VMEM((tokens, model), BF),
        pltpu.VMEM((tokens, model), BF),
        pltpu.VMEM((tokens, 3 * INNER_WIDTH), BF),
        pltpu.SemaphoreType.DMA,
    ]


def time_forward(x, length, weights, small, tables, parts, width_ff):
    seqs, frames, model = x.shape
    tokens = seqs * frames
    shapes = saved_shapes(tokens, seqs, model, width_ff)
    out = jax.ShapeDtypeStruct((parts, seqs, frames // parts, model), BF)
    return pl.pallas_call(
        partial(time_forward_kernel, width_ff),
        grid_spec=pltpu.PrefetchScalarGridSpec(
            num_scalar_prefetch=1,
            grid=(seqs,),
            in_specs=[
                pl.BlockSpec((1, frames, model), lambda i, s: (i, 0, 0)),
                whole(weights.shape),
                whole(small.shape),
                whole(tables[0].shape),
                whole(tables[1].shape),
            ],
            out_specs=[
                pl.BlockSpec((parts, 1, frames // parts, model), lambda i, s: (0, i, 0, 0)),
                *saved_specs(frames, 1, model, width_ff),
            ],
        ),
        out_shape=[out, *(jax.ShapeDtypeStruct(s, k) for s, k in shapes)],
        compiler_params=params(),
        cost_estimate=pl.CostEstimate(
            flops=int(tokens * 5e6), bytes_accessed=tokens * 15000, transcendentals=tokens * 5000
        ),
        name="time_forward",
    )(length, x, weights, small, *tables)


def time_backward(x, d_out, weights, small, tables, saved, before, kind, width_ff):
    seqs, frames, model = x.shape
    tokens = seqs * frames
    parts, unused, part_frames, unused_model = d_out.shape
    per_step = 2 if seqs % 2 == 0 else 1
    columns = weights.shape[1]
    chained = before is not None
    ins = [x, d_out, weights, small, *tables, *saved] + ([before] if chained else [])
    return pl.pallas_call(
        partial(time_backward_kernel, width_ff, chained, per_step),
        grid=(seqs // per_step,),
        in_specs=[
            pl.BlockSpec((per_step, frames, model), lambda i: (i, 0, 0)),
            pl.BlockSpec((parts, per_step, part_frames, model), lambda i: (0, i, 0, 0)),
            whole(weights.shape),
            whole(small.shape),
            whole(tables[0].shape),
            whole(tables[1].shape),
            *saved_specs(per_step * frames, per_step, model, width_ff),
        ]
        + ([pl.BlockSpec(memory_space=pl.ANY)] if chained else []),
        out_specs=[
            pl.BlockSpec((per_step, frames, model), lambda i: (i, 0, 0)),
            whole((model, columns)),
        ],
        out_shape=[
            jax.ShapeDtypeStruct(x.shape, F32),
            jax.ShapeDtypeStruct((model, columns), kind),
        ],
        scratch_shapes=work_shapes(per_step * frames, model, width_ff, columns),
        compiler_params=params(),
        cost_estimate=pl.CostEstimate(
            flops=int(tokens * 9e6), bytes_accessed=tokens * 18000, transcendentals=0
        ),
        name="time_backward",
    )(*ins)


def band_both(x, d_out, info, weights, small, tables, before, kind, width_ff):
    bands, frames, model = x.shape
    tokens = bands * frames
    chunk = math.gcd(frames, 16)
    step_tokens = bands * chunk
    columns = weights.shape[1]
    chained = before is not None
    ins = [info, x, d_out, weights, small, *tables] + ([before] if chained else [])
    rows = pl.BlockSpec((bands, chunk, model), lambda i, s: (0, i, 0))
    saved = [
        pltpu.VMEM(s, k) for s, k in saved_shapes(step_tokens, step_tokens // BLOCK, model, width_ff)
    ]
    return pl.pallas_call(
        partial(band_kernel, width_ff, chained),
        grid_spec=pltpu.PrefetchScalarGridSpec(
            num_scalar_prefetch=1,
            grid=(frames // chunk,),
            in_specs=[
                rows,
                rows,
                whole(weights.shape),
                whole(small.shape),
                whole(tables[0].shape),
                whole(tables[1].shape),
            ]
            + ([pl.BlockSpec(memory_space=pl.ANY)] if chained else []),
            out_specs=[rows, rows, whole((model, columns))],
            scratch_shapes=saved
            + work_shapes(step_tokens, model, width_ff, columns)
            + [pltpu.VMEM((model // LANES, step_tokens, LANES), F32)] * 2,
        ),
        out_shape=[
            jax.ShapeDtypeStruct(x.shape, BF),
            jax.ShapeDtypeStruct(x.shape, BF),
            jax.ShapeDtypeStruct((model, columns), kind),
        ],
        compiler_params=params(),
        cost_estimate=pl.CostEstimate(
            flops=int(tokens * 14e6), bytes_accessed=tokens * 8000, transcendentals=tokens * 5000
        ),
        name="band_both",
    )(*ins)


def rotary_order(columns):
    lead = columns.shape[:-1]
    split = columns.reshape(lead + (-1, 4, 2, HEAD_DIM // 2))
    return jnp.swapaxes(split, -3, -2).reshape(columns.shape)


def head_order(columns):
    lead = columns.shape[:-1]
    split = columns.reshape(lead + (-1, 2, 4, HEAD_DIM // 2))
    return jnp.swapaxes(split, -3, -2).reshape(columns.shape)


def adam_step(master, gradient, first_old, second_old, learn_rate):
    first_new = BETA_ONE * first_old + (1.0 - BETA_ONE) * gradient
    second_new = BETA_TWO * second_old + (1.0 - BETA_TWO) * gradient * gradient
    first_hat = first_new / (1.0 - BETA_ONE**STEP)
    second_hat = second_new / (1.0 - BETA_TWO**STEP)
    updated = master - learn_rate * (first_hat / (jnp.sqrt(second_hat) + ADAM_EPS) + DECAY * master)
    return (updated, first_new, second_new)


def body(
    activations,
    cotangent,
    lengths,
    weight_in,
    weight_out,
    weight_small,
    first_in,
    first_out,
    first_small,
    second_in,
    second_out,
    second_small,
):
    parts = lax.axis_size("seq")
    micro, unused, band_dev, frames, model = activations.shape
    bands, frame_dev = cotangent.shape[2], cotangent.shape[3]
    turned = 2 * INNER_WIDTH
    width_in, width_out = weight_in.shape[2], weight_out.shape[2]
    width_ff = width_in - 3 * INNER_WIDTH
    small_width = weight_small.shape[2]
    full = []
    for layer in range(2):
        packed = jnp.concatenate(
            [
                rotary_order(weight_in[layer, :, :turned].astype(BF)),
                weight_in[layer, :, turned:].astype(BF),
                weight_out[layer].astype(BF),
                jnp.pad(weight_small[layer].astype(BF), ((0, 0), (0, LANES - small_width))),
            ],
            axis=1,
        )
        full.append(lax.all_gather(packed, "seq", axis=0, tiled=True))
    small = [
        jnp.pad(w[:, width_in + width_out :].T[:small_width].astype(F32), ((0, 16 - small_width), (0, 0)))
        for w in full
    ]
    time_tables, band_tables = rotary_tables(frames), rotary_tables(bands)
    frame_base = lax.axis_index("seq") * frame_dev

    def exchange(tensor):
        return lax.all_to_all(tensor, "seq", split_axis=0, concat_axis=0, tiled=True)

    streams, saves = [], []
    for m in range(micro):
        out, *saved = time_forward(
            activations[m, 0], lengths[m], full[0], small[0], time_tables, parts, width_ff
        )
        saves.append(saved)
        streams.append(exchange(out).reshape(bands, frame_dev, model))
    outputs, backs, grad_band = [], [], None
    for m in range(micro):
        info = jnp.concatenate([lengths[m], frame_base[None].astype(jnp.int32)])
        kind = BF if m == micro - 1 else F32
        out, back, grad_band = band_both(
            streams[m], cotangent[m, 0], info, full[1], small[1], band_tables, grad_band, kind, width_ff
        )
        outputs.append(out)
        backs.append(exchange(back.reshape(parts, band_dev, frame_dev, model)))
    sum_band = lax.psum(grad_band, ("dp", "seq"))
    d_inputs, grad_time = [], None
    for m in range(micro):
        kind = BF if m == micro - 1 else F32
        d_input, grad_time = time_backward(
            activations[m, 0], backs[m], full[0], small[0], time_tables, saves[m], grad_time, kind, width_ff
        )
        d_inputs.append(d_input)
    sum_time = lax.psum(grad_time, ("dp", "seq"))
    shard_width = weight_in.shape[1]
    shard_start = lax.axis_index("seq") * shard_width
    squares = 0.0
    shards = []
    for total in (sum_time, sum_band):
        squares = squares + jnp.sum(jnp.square(total.astype(F32)))
        shard = lax.dynamic_slice_in_dim(total, shard_start, shard_width, 0).astype(F32)
        shards.append(
            (
                jnp.concatenate([head_order(shard[:, :turned]), shard[:, turned:width_in]], axis=1),
                shard[:, width_in : width_in + width_out],
                shard[:, width_in + width_out : width_in + width_out + small_width],
            )
        )
    shards = tuple(jnp.stack([shards[0][s], shards[1][s]]) for s in range(3))
    grad_norm = jnp.sqrt(squares)
    factor = jnp.minimum(1.0, CLIP_NORM / (grad_norm + 1e-06))
    small_rate = jnp.where(jnp.arange(small_width) < HEAD_COUNT, RATE_GATE, RATE_GAIN)
    new_in = adam_step(weight_in, shards[0] * factor, first_in, second_in, RATE_MATRIX)
    new_out = adam_step(weight_out, shards[1] * factor, first_out, second_out, RATE_MATRIX)
    new_small = adam_step(weight_small, shards[2] * factor, first_small, second_small, small_rate)
    return (
        jnp.stack(outputs)[:, None],
        jnp.stack(d_inputs)[:, None],
        grad_norm,
        new_in[0],
        new_out[0],
        new_small[0],
        new_in[1],
        new_out[1],
        new_small[1],
        new_in[2],
        new_out[2],
        new_small[2],
        new_in[0].astype(BF),
        new_out[0].astype(BF),
        new_small[0].astype(BF),
    )


def solution(mesh):
    by_seq = P(None, "seq", None)
    by_band = P(None, "dp", "seq", None, None)
    by_frame = P(None, "dp", None, "seq", None)
    return jax.shard_map(
        body,
        mesh=mesh,
        in_specs=(by_band, by_frame, P(None, "dp")) + (by_seq,) * 9,
        out_specs=(by_frame, by_band, P()) + (by_seq,) * 12,
        check_vma=False,
    )
```

```python
from functools import partial
import math

import jax
import jax.numpy as jnp
from jax import lax
from jax.experimental import pallas as pl
from jax.experimental.pallas import tpu as pltpu
from jax.sharding import PartitionSpec as P

HEAD_COUNT = 8
HEAD_DIM = 64
INNER_WIDTH = 512
STEP = 10
EPS_NORM = 1e-06
BETA_ONE = 0.9
BETA_TWO = 0.999
ADAM_EPS = 1e-08
DECAY = 0.1
RATE_MATRIX = 0.1
RATE_GATE = 0.1
RATE_GAIN = 0.5
CLIP_NORM = 1.0
MASKED = -1e30

BF = jnp.bfloat16
F32 = jnp.float32
GROUP = 256
BLOCK = 256
LANES = 128
SMALL_LANES = 2 * LANES
LOG2E = 1.4426950408889634
SCORE_EXP = LOG2E / math.sqrt(HEAD_DIM)
SQRT_HALF = math.sqrt(0.5)
GAUSS = 1.0 / math.sqrt(2.0 * math.pi)
VMEM_LIMIT = 60 * 2**20


def nn(a, b):
    return lax.dot_general(a, b, (((1,), (0,)), ((), ())), preferred_element_type=F32)


def nt(a, b):
    return lax.dot_general(a, b, (((1,), (1,)), ((), ())), preferred_element_type=F32)


def tn(a, b):
    return lax.dot_general(a, b, (((0,), (0,)), ((), ())), preferred_element_type=F32)


def iota(shape, dim):
    return lax.broadcasted_iota(jnp.int32, shape, dim)


def split_rows(rows):
    high = rows.astype(BF)
    rest = (rows - high.astype(F32)).astype(BF)
    return jnp.concatenate([high, rest], axis=0)


def head_lanes():
    shape = (2 * HEAD_COUNT, INNER_WIDTH)
    return (iota(shape, 1) // HEAD_DIM == iota(shape, 0) % HEAD_COUNT).astype(F32).astype(BF)


def inverse_rms(rows):
    return lax.rsqrt(jnp.mean(rows * rows, axis=-1, keepdims=True) + EPS_NORM)


def norm_back(rows, gain, grad):
    inverse = inverse_rms(rows)
    unit = rows * inverse
    scaled = grad * gain
    d_rows = inverse * (scaled - unit * jnp.mean(scaled * unit, axis=-1, keepdims=True))
    return d_rows, jnp.sum(grad * unit, axis=0, keepdims=True)


def half_lanes(h):
    return (iota((BLOCK, GROUP), 1) % LANES) // (HEAD_DIM // 2) == h


def whole_lanes(h):
    return iota((BLOCK, GROUP), 1) // HEAD_DIM == h


def picked(mask, tensor):
    return jnp.where(mask, tensor, jnp.zeros_like(tensor))


def group_slice(g):
    return slice(g * GROUP, (g + 1) * GROUP)


def forward_block(x, w_ref, small, cos, sin, key_mask, keep, rows, item, width_ff):
    gate_weight, gain_attn, gain_ff = small
    normed = (x * inverse_rms(x) * gain_attn).astype(BF)
    if "normed" in keep:
        keep["normed"][rows, :] = normed
    gate_rows = jax.nn.sigmoid(nt(gate_weight, normed))
    keep["gate"][item] = gate_rows
    half = GROUP // 2
    for g in range(2):
        for part, name in ((0, "q"), (1, "k")):
            start = part * INNER_WIDTH + g * GROUP
            t = nn(normed, w_ref[:, start : start + GROUP])
            a, b = t[:, :half], t[:, half:]
            keep[name][rows, g * GROUP : g * GROUP + half] = (a * cos - b * sin).astype(BF)
            keep[name][rows, g * GROUP + half : (g + 1) * GROUP] = (b * cos + a * sin).astype(BF)
        start = 2 * INNER_WIDTH + g * GROUP
        keep["v"][rows, group_slice(g)] = nn(normed, w_ref[:, start : start + GROUP]).astype(BF)
    gate = tn(split_rows(gate_rows), head_lanes())
    for g in range(2):
        lanes = group_slice(g)
        queries, keys = keep["q"][rows, lanes], keep["k"][rows, lanes]
        values = keep["v"][rows, lanes]
        attended = None
        for h in range(4):
            scores = nt(picked(half_lanes(h), keys), queries)
            scores = jnp.where(key_mask, scores, MASKED)
            peak = jnp.max(scores, axis=0, keepdims=True)
            terms = jnp.exp2((scores - peak) * SCORE_EXP)
            probs = (terms * (1.0 / jnp.sum(terms, axis=0, keepdims=True))).astype(BF)
            keep["probs"][item, g * 4 + h] = probs
            part = tn(probs, picked(whole_lanes(h), values))
            attended = part if attended is None else attended + part
        keep["gated"][rows, lanes] = (attended * gate[:, lanes]).astype(BF)
    out_start = 3 * INNER_WIDTH + width_ff
    middle = x + nt(keep["gated"][rows, :], w_ref[:, out_start : out_start + INNER_WIDTH])
    keep["middle"][rows, :] = middle
    normed_ff = (middle * inverse_rms(middle) * gain_ff).astype(BF)
    if "normed_ff" in keep:
        keep["normed_ff"][rows, :] = normed_ff
    result = middle
    for c in range(width_ff // GROUP):
        up = 3 * INNER_WIDTH + c * GROUP
        down = out_start + INNER_WIDTH + c * GROUP
        hidden = nn(normed_ff, w_ref[:, up : up + GROUP])
        cumulative = 0.5 + 0.5 * lax.erf(hidden * SQRT_HALF)
        activated = (hidden * cumulative).astype(BF)
        density = jnp.exp2(hidden * hidden * (-0.5 * LOG2E)) * GAUSS
        keep["act"][rows, group_slice(c)] = activated
        keep["slope"][rows, group_slice(c)] = (cumulative + hidden * density).astype(BF)
        result = result + nt(activated, w_ref[:, down : down + GROUP])
    return result


def backward_block(d_out, x, w_ref, small, cos, sin, keep, work, sums, rows, item, width_ff):
    gate_weight, gain_attn, gain_ff = small
    branch = d_out.astype(BF)
    work["branch"][rows, :] = branch
    out_start = 3 * INNER_WIDTH + width_ff
    d_normed_ff = None
    for c in range(width_ff // GROUP):
        up = 3 * INNER_WIDTH + c * GROUP
        down = out_start + INNER_WIDTH + c * GROUP
        d_act = nn(branch, w_ref[:, down : down + GROUP])
        d_hidden = (d_act * keep["slope"][rows, group_slice(c)].astype(F32)).astype(BF)
        work["d_hidden"][rows, group_slice(c)] = d_hidden
        part = nt(d_hidden, w_ref[:, up : up + GROUP])
        d_normed_ff = part if d_normed_ff is None else d_normed_ff + part
    middle = keep["middle"][rows, :]
    d_rows, d_gain_ff = norm_back(middle, gain_ff, d_normed_ff)
    d_middle = d_out + d_rows
    attn_back = d_middle.astype(BF)
    work["attn_back"][rows, :] = attn_back
    gate_rows = keep["gate"][item]
    lanes_of = head_lanes()
    gate = tn(split_rows(gate_rows), lanes_of)
    d_gated = nn(attn_back, w_ref[:, out_start : out_start + INNER_WIDTH])
    product = d_gated * keep["gated"][rows, :].astype(F32)
    high = product.astype(BF)
    rest = (product - high.astype(F32)).astype(BF)
    delta_rows = (nt(lanes_of, high) + nt(lanes_of, rest))[:HEAD_COUNT]
    d_logit = split_rows(delta_rows * (1.0 - gate_rows))
    d_attended = (d_gated * gate).astype(BF)
    half = GROUP // 2
    scale = HEAD_DIM**-0.5
    for g in range(2):
        lanes = group_slice(g)
        queries, keys = keep["q"][rows, lanes], keep["k"][rows, lanes]
        values, d_att = keep["v"][rows, lanes], d_attended[:, lanes]
        d_query = d_keys = d_values = None
        for h in range(4):
            halves, wholes = half_lanes(h), whole_lanes(h)
            key_h = picked(halves, keys)
            probs = keep["probs"][item, g * 4 + h]
            d_probs = nt(picked(wholes, values), d_att)
            delta = delta_rows[g * 4 + h : g * 4 + h + 1, :]
            d_scores = (probs.astype(F32) * (d_probs - delta)).astype(BF)
            part_v = nn(probs, picked(wholes, d_att))
            part_k = nn(d_scores, picked(halves, queries))
            part_q = tn(d_scores, key_h)
            if h == 0:
                d_query, d_keys, d_values = part_q, part_k, part_v
            else:
                d_query, d_keys, d_values = d_query + part_q, d_keys + part_k, d_values + part_v
        for start, t in ((0, d_query), (INNER_WIDTH, d_keys)):
            t = t * scale
            a, b = t[:, :half], t[:, half:]
            start = start + g * GROUP
            work["d_proj"][rows, start : start + half] = (a * cos + b * sin).astype(BF)
            work["d_proj"][rows, start + half : start + GROUP] = (b * cos - a * sin).astype(BF)
        start = 2 * INNER_WIDTH + g * GROUP
        work["d_proj"][rows, start : start + GROUP] = d_values.astype(BF)
    twice = jnp.concatenate([gate_weight, gate_weight], axis=0)
    d_normed = tn(d_logit, twice)
    for c in range(3 * INNER_WIDTH // INNER_WIDTH):
        part = slice(c * INNER_WIDTH, (c + 1) * INNER_WIDTH)
        d_normed = d_normed + nt(work["d_proj"][rows, part], w_ref[:, part])
    d_rows, d_gain_attn = norm_back(x, gain_attn, d_normed)
    d_gate = nn(d_logit, work["normed"][rows, :])
    sums[0:HEAD_COUNT, :] += d_gate[:HEAD_COUNT] + d_gate[HEAD_COUNT:]
    sums[HEAD_COUNT : HEAD_COUNT + 1, :] += d_gain_attn
    sums[HEAD_COUNT + 1 : HEAD_COUNT + 2, :] += d_gain_ff
    return d_middle + d_rows


def weight_sums(total, work, keep, width_ff):
    out_start = 3 * INNER_WIDTH + width_ff
    pairs = (
        (work["normed"], work["d_proj"], 0),
        (work["normed_ff"], work["d_hidden"], 3 * INNER_WIDTH),
        (work["attn_back"], keep["gated"], out_start),
        (work["branch"], keep["act"], out_start + INNER_WIDTH),
    )
    for left, right, start in pairs:
        turned = left[...].T
        for c in range(right.shape[-1] // INNER_WIDTH):
            part = slice(start + c * INNER_WIDTH, start + (c + 1) * INNER_WIDTH)
            total[:, part] += nn(turned, right[:, c * INNER_WIDTH : (c + 1) * INNER_WIDTH])


def turn_small(w_ref, small_ref):
    width = w_ref.shape[1] - SMALL_LANES
    rows = w_ref[:, width : width + LANES].astype(F32).T
    small_ref[...] = rows[: small_ref.shape[0]]


def small_parts(small_ref):
    gate_weight = small_ref[0:HEAD_COUNT, :].astype(BF)
    return (
        gate_weight,
        small_ref[HEAD_COUNT : HEAD_COUNT + 1, :],
        small_ref[HEAD_COUNT + 1 : HEAD_COUNT + 2, :],
    )


def finish_sums(total, sums, out_ref):
    width = total.shape[1] - SMALL_LANES
    model = total.shape[0]
    out_ref[:, :width] = total[:, :width].astype(out_ref.dtype)
    tall = jnp.concatenate([sums[...], jnp.zeros((SMALL_LANES - sums.shape[0], model), F32)], axis=0)
    out_ref[:, width:] = tall.T.astype(out_ref.dtype)


def start_sums(total, sums, before_ref, arrival):
    sums[...] = jnp.zeros_like(sums)
    if before_ref is None:
        total[...] = jnp.zeros_like(total)
    else:
        pltpu.make_async_copy(before_ref, total, arrival).start()


def await_sums(total, sums, before_ref, arrival):
    if before_ref is not None:
        width = total.shape[1] - SMALL_LANES
        pltpu.make_async_copy(before_ref, total, arrival).wait()
        sums[...] += total[:, width:].T[: sums.shape[0]]


SAVED = ("q", "k", "v", "gate", "probs", "gated", "middle", "act", "slope")


def time_forward_kernel(width_ff, len_ref, x_ref, w_ref, cos_ref, sin_ref, out_ref, *saved):
    small_ref = saved[-1]
    keep = dict(zip(SAVED, saved))

    @pl.when(pl.program_id(0) == 0)
    def _():
        turn_small(w_ref, small_ref)

    keys = iota((BLOCK, BLOCK), 0) < len_ref[0]
    x = x_ref[0].astype(F32)
    out = forward_block(
        x, w_ref, small_parts(small_ref), cos_ref[...], sin_ref[...], keys, keep, slice(None), 0, width_ff
    )
    parts, unused, frames, model = out_ref.shape
    out_ref[:, 0] = out.reshape(parts, frames, model).astype(BF)


def time_backward_kernel(width_ff, chained, per_step, *refs):
    x_ref, d_ref, w_ref, cos_ref, sin_ref = refs[:5]
    keep = dict(zip(SAVED, refs[5:14]))
    refs = refs[14:]
    before = refs[0] if chained else None
    dx_ref, grad_ref = refs[2:4] if chained else refs[:2]
    total, sums, normed, normed_ff, d_hidden, attn_back, branch, d_proj, arrival, small_ref = refs[-10:]
    work = dict(
        normed=normed, normed_ff=normed_ff, d_hidden=d_hidden, attn_back=attn_back, branch=branch, d_proj=d_proj
    )
    step = pl.program_id(0)

    @pl.when(step == 0)
    def _():
        start_sums(total, sums, before, arrival)
        turn_small(w_ref, small_ref)

    small = small_parts(small_ref)

    def one(i, carry):
        rows = pl.ds(pl.multiple_of(i * BLOCK, BLOCK), BLOCK)
        x = x_ref[i].astype(F32)
        work["normed"][rows, :] = (x * inverse_rms(x) * small[1]).astype(BF)
        middle = keep["middle"][rows, :]
        work["normed_ff"][rows, :] = (middle * inverse_rms(middle) * small[2]).astype(BF)
        d_out = d_ref[:, i].astype(F32).reshape(BLOCK, x.shape[1])
        dx_ref[i] = backward_block(
            d_out, x, w_ref, small, cos_ref[...], sin_ref[...], keep, work, sums, rows, i, width_ff
        )
        return carry

    lax.fori_loop(0, per_step, one, 0)
    if chained:

        @pl.when(step == 0)
        def _():
            await_sums(total, sums, before, arrival)

    weight_sums(total, work, keep, width_ff)

    @pl.when(step == pl.num_programs(0) - 1)
    def _():
        finish_sums(total, sums, grad_ref)


def gather_rows(ref, strides, factors):
    return jnp.concatenate(
        [
            jnp.concatenate([ref[p, s, :] * f for p in range(ref.shape[0])], axis=1)
            for s, f in zip(strides, factors)
        ],
        axis=0,
    )


def band_kernel(width_ff, chained, info_ref, *refs):
    x_ref, d_ref, w_ref, cos_ref, sin_ref = refs[:5]
    refs = refs[5:]
    before = refs[0] if chained else None
    out_ref, back_ref, grad_ref = refs[2:5] if chained else refs[:3]
    scratch = refs[-21:]
    keep = dict(zip(SAVED, scratch[:9]))
    total, sums, normed, normed_ff, d_hidden, attn_back, branch, d_proj, arrival, small_ref, rows_a, rows_b = scratch[9:]
    work = dict(
        normed=normed, normed_ff=normed_ff, d_hidden=d_hidden, attn_back=attn_back, branch=branch, d_proj=d_proj
    )
    keep.update(normed=normed, normed_ff=normed_ff)
    step = pl.program_id(0)
    bands, frames, model = x_ref.shape
    together = BLOCK // bands
    pieces = model // LANES

    @pl.when(step == 0)
    def _():
        start_sums(total, sums, before, arrival)
        turn_small(w_ref, small_ref)

    small = small_parts(small_ref)
    for p in range(pieces):
        lanes = slice(p * LANES, (p + 1) * LANES)
        rows_a[p] = x_ref[:, :, lanes].astype(F32).reshape(bands * frames, LANES)
        rows_b[p] = d_ref[:, :, lanes].astype(F32).reshape(bands * frames, LANES)
    same = iota((BLOCK, BLOCK), 0) // bands == iota((BLOCK, BLOCK), 1) // bands
    first = info_ref[1] + step * frames

    def one(j, carry):
        rows = pl.ds(pl.multiple_of(j * BLOCK, BLOCK), BLOCK)
        strides = [pl.ds(j * together + f, bands, stride=frames) for f in range(together)]
        valid = [
            (first + j * together + f < info_ref[0]).astype(F32) for f in range(together)
        ]
        x = gather_rows(rows_a, strides, [1.0] * together)
        d_out = gather_rows(rows_b, strides, valid)
        out = forward_block(
            x, w_ref, small, cos_ref[...], sin_ref[...], same, keep, rows, j, width_ff
        )
        for f in range(together):
            for p in range(pieces):
                part = out[f * bands : (f + 1) * bands, p * LANES : (p + 1) * LANES]
                rows_a[p, strides[f], :] = part * valid[f]
        back = backward_block(
            d_out, x, w_ref, small, cos_ref[...], sin_ref[...], keep, work, sums, rows, j, width_ff
        )
        for f in range(together):
            for p in range(pieces):
                part = back[f * bands : (f + 1) * bands, p * LANES : (p + 1) * LANES]
                rows_b[p, strides[f], :] = part
        return carry

    lax.fori_loop(0, frames // together, one, 0)
    for p in range(pieces):
        lanes = slice(p * LANES, (p + 1) * LANES)
        out_ref[:, :, lanes] = rows_a[p].reshape(bands, frames, LANES).astype(BF)
        back_ref[:, :, lanes] = rows_b[p].reshape(bands, frames, LANES).astype(BF)
    if chained:

        @pl.when(step == 0)
        def _():
            await_sums(total, sums, before, arrival)

    weight_sums(total, work, keep, width_ff)

    @pl.when(step == pl.num_programs(0) - 1)
    def _():
        finish_sums(total, sums, grad_ref)


def whole(shape):
    return pl.BlockSpec(shape, lambda *i: (0,) * len(shape), pipeline_mode=pl.Buffered(1))


def params(**more):
    return pltpu.CompilerParams(vmem_limit_bytes=VMEM_LIMIT, **more)


def rotary_tables(positions):
    half_width = HEAD_DIM // 2
    inverse = 10000.0 ** (-(jnp.arange(half_width, dtype=F32) * 2.0 / HEAD_DIM))
    angles = jnp.arange(positions, dtype=F32)[:, None] * inverse[None, :]
    angles = jnp.tile(angles, (BLOCK // positions, LANES // half_width))
    return (jnp.cos(angles), jnp.sin(angles))


def saved_shapes(tokens, items, model, width_ff):
    return (
        ((tokens, INNER_WIDTH), BF),
        ((tokens, INNER_WIDTH), BF),
        ((tokens, INNER_WIDTH), BF),
        ((items, HEAD_COUNT, BLOCK), F32),
        ((items, HEAD_COUNT, BLOCK, BLOCK), BF),
        ((tokens, INNER_WIDTH), BF),
        ((tokens, model), F32),
        ((tokens, width_ff), BF),
        ((tokens, width_ff), BF),
    )


def saved_specs(tokens, items, model, width_ff):
    return [
        pl.BlockSpec(shape, lambda i, *s, n=len(shape): (i,) + (0,) * (n - 1))
        for shape, kind in saved_shapes(tokens, items, model, width_ff)
    ]


def work_shapes(tokens, model, width_ff, columns):
    return [
        pltpu.VMEM((model, columns), F32),
        pltpu.VMEM((2 * HEAD_COUNT, model), F32),
        pltpu.VMEM((tokens, model), BF),
        pltpu.VMEM((tokens, model), BF),
        pltpu.VMEM((tokens, width_ff), BF),
        pltpu.VMEM((tokens, model), BF),
        pltpu.VMEM((tokens, model), BF),
        pltpu.VMEM((tokens, 3 * INNER_WIDTH), BF),
        pltpu.SemaphoreType.DMA,
        pltpu.VMEM((2 * HEAD_COUNT, model), F32),
    ]


def at_micro(m, shape, place):
    return pl.BlockSpec((None, None) + shape, lambda i, *s: (m, 0) + place(i))


def time_forward(m, x, length, weights, tables, parts, width_ff):
    seqs, frames, model = x.shape[2:]
    tokens = seqs * frames
    shapes = saved_shapes(tokens, seqs, model, width_ff)
    out = jax.ShapeDtypeStruct((parts, seqs, frames // parts, model), BF)
    return pl.pallas_call(
        partial(time_forward_kernel, width_ff),
        grid_spec=pltpu.PrefetchScalarGridSpec(
            num_scalar_prefetch=1,
            grid=(seqs,),
            in_specs=[
                at_micro(m, (1, frames, model), lambda i: (i, 0, 0)),
                whole(weights.shape),
                whole(tables[0].shape),
                whole(tables[1].shape),
            ],
            out_specs=[
                pl.BlockSpec((parts, 1, frames // parts, model), lambda i, s: (0, i, 0, 0)),
                *saved_specs(frames, 1, model, width_ff),
            ],
            scratch_shapes=[pltpu.VMEM((2 * HEAD_COUNT, model), F32)],
        ),
        out_shape=[out, *(jax.ShapeDtypeStruct(s, k) for s, k in shapes)],
        compiler_params=params(),
        cost_estimate=pl.CostEstimate(
            flops=int(tokens * 5e6), bytes_accessed=tokens * 15000, transcendentals=tokens * 5000
        ),
        name="time_forward",
    )(length, x, weights, *tables)


def time_backward(m, x, d_out, weights, tables, saved, before, kind, width_ff):
    seqs, frames, model = x.shape[2:]
    tokens = seqs * frames
    parts, unused, part_frames, unused_model = d_out.shape
    per_step = 2 if seqs % 2 == 0 else 1
    columns = weights.shape[1]
    ins = [x, d_out, weights, *tables, *saved, *before]
    rows = at_micro(m, (per_step, frames, model), lambda i: (i, 0, 0))
    any_space = pl.BlockSpec(memory_space=pl.ANY)
    return pl.pallas_call(
        partial(time_backward_kernel, width_ff, bool(before), per_step),
        grid=(seqs // per_step,),
        in_specs=[
            rows,
            pl.BlockSpec((parts, per_step, part_frames, model), lambda i: (0, i, 0, 0)),
            whole(weights.shape),
            whole(tables[0].shape),
            whole(tables[1].shape),
            *saved_specs(per_step * frames, per_step, model, width_ff),
        ]
        + [any_space] * len(before),
        out_specs=[rows, whole((model, columns))],
        out_shape=[
            jax.ShapeDtypeStruct(x.shape, F32),
            jax.ShapeDtypeStruct((model, columns), kind),
        ],
        input_output_aliases={len(ins) - 1: 0} if before else {},
        scratch_shapes=work_shapes(per_step * frames, model, width_ff, columns),
        compiler_params=params(),
        cost_estimate=pl.CostEstimate(
            flops=int(tokens * 9e6), bytes_accessed=tokens * 18000, transcendentals=0
        ),
        name="time_backward",
    )(*ins)


def band_both(m, x, d_out, info, weights, tables, before, kind, width_ff):
    bands, frames, model = x.shape
    tokens = bands * frames
    chunk = math.gcd(frames, 16)
    step_tokens = bands * chunk
    columns = weights.shape[1]
    ins = [info, x, d_out, weights, *tables, *before]
    rows = pl.BlockSpec((bands, chunk, model), lambda i, s: (0, i, 0))
    rows_m = at_micro(m, (bands, chunk, model), lambda i: (0, i, 0))
    saved = [
        pltpu.VMEM(s, k) for s, k in saved_shapes(step_tokens, step_tokens // BLOCK, model, width_ff)
    ]
    return pl.pallas_call(
        partial(band_kernel, width_ff, bool(before)),
        grid_spec=pltpu.PrefetchScalarGridSpec(
            num_scalar_prefetch=1,
            grid=(frames // chunk,),
            in_specs=[
                rows,
                rows_m,
                whole(weights.shape),
                whole(tables[0].shape),
                whole(tables[1].shape),
            ]
            + [pl.BlockSpec(memory_space=pl.ANY)] * len(before),
            out_specs=[rows_m, rows, whole((model, columns))],
            scratch_shapes=saved
            + work_shapes(step_tokens, model, width_ff, columns)
            + [pltpu.VMEM((model // LANES, step_tokens, LANES), F32)] * 2,
        ),
        out_shape=[
            jax.ShapeDtypeStruct(d_out.shape, BF),
            jax.ShapeDtypeStruct(x.shape, BF),
            jax.ShapeDtypeStruct((model, columns), kind),
        ],
        input_output_aliases={len(ins) - 1: 0} if before else {},
        compiler_params=params(),
        cost_estimate=pl.CostEstimate(
            flops=int(tokens * 14e6), bytes_accessed=tokens * 8000, transcendentals=tokens * 5000
        ),
        name="band_both",
    )(*ins)


MESH = pl.DeviceIdType.MESH


def seq_sides(parts):
    side = 1
    while 4 * side * side <= parts:
        side *= 2
    return parts // side, side


class Place:
    def __init__(self, parts):
        self.dp, self.seq = lax.axis_index("dp"), lax.axis_index("seq")
        self.core = self.dp % 2
        self.zs, self.ys = seq_sides(parts)
        self.z, self.y = self.seq // self.ys, self.seq % self.ys

    def sibling(self):
        return (self.dp + 1 - 2 * self.core, self.seq)

    def along_z(self, step):
        return (self.dp, self.seq + step * self.ys)

    def along_y(self, step):
        return (self.dp, self.seq + step)

    def has_z(self, step):
        return self.z + step < self.zs if step > 0 else self.z + step >= 0

    def has_y(self, step):
        return self.y + step < self.ys if step > 0 else self.y + step >= 0


def greet(place, others=()):
    barrier = pltpu.get_barrier_semaphore()
    pl.semaphore_signal(barrier, inc=1, device_id=place.sibling(), device_id_type=MESH)
    for other in others:
        pl.semaphore_signal(barrier, inc=1, device_id=other, device_id_type=MESH)
    for step in (1, -1):
        for has, to in ((place.has_z, place.along_z), (place.has_y, place.along_y)):

            @pl.when(has(step))
            def _(to=to, step=step):
                pl.semaphore_signal(barrier, inc=1, device_id=to(step), device_id_type=MESH)

    count = 1 + len(others)
    for has in (place.has_z, place.has_y):
        count = count + has(1).astype(jnp.int32) + has(-1).astype(jnp.int32)
    pl.semaphore_wait(barrier, count)


def gather_kernel(parts, shard_ref, out_ref, send_z, send_y, send_c, got, got_c, local):
    place = Place(parts)
    zs, ys = place.zs, place.ys
    wide = shard_ref.shape[1] // 2
    lanes = pl.ds(pl.multiple_of(place.core * wide, LANES), wide)
    other_lanes = pl.ds(pl.multiple_of((1 - place.core) * wide, LANES), wide)
    greet(place)
    own = pltpu.make_async_copy(shard_ref, out_ref.at[place.seq], local)
    own.start()

    def index(z, y):
        return z * ys + y

    def push(source, p, to, send, receive):
        return pltpu.make_async_remote_copy(
            src_ref=source, dst_ref=out_ref.at[p, :, lanes], send_sem=send, recv_sem=receive, device_id=to, device_id_type=MESH
        )

    def held(p):
        return out_ref.at[p, :, lanes]

    def when(condition, action):
        pl.when(condition)(action)

    def to_sibling(p):
        return push(held(p), p, place.sibling(), send_c.at[p], got_c.at[p])

    def from_sibling(p):
        there = out_ref.at[p, :, other_lanes]
        return pltpu.make_async_remote_copy(
            src_ref=there, dst_ref=there, send_sem=send_c.at[p], recv_sem=got_c.at[p], device_id=place.sibling(), device_id_type=MESH
        )

    def start_y(source, p, step, z_from):
        push(source, p, place.along_y(step), send_y.at[(step + 1) // 2, p], got.at[p]).start()

    def wait_here(p):
        push(held(p), p, place.sibling(), send_c.at[p], got.at[p]).wait_recv()

    mine = shard_ref.at[:, lanes]
    for step in (1, -1):
        when(place.has_z(step), lambda step=step: push(
            mine, place.seq, place.along_z(step), send_z.at[(step + 1) // 2, 0], got.at[place.seq]).start())
        when(place.has_y(step), lambda step=step: start_y(mine, place.seq, step, 0))

    for t in range(1, zs):
        for step in (1, -1):
            z = place.z - step * t
            here = (z >= 0) if step > 0 else (z < zs)

            @pl.when(here)
            def _(t=t, step=step, z=z):
                p = index(z, place.y)
                wait_here(p)
                if t < zs - 1:
                    when(place.has_z(step), lambda: push(
                        held(p), p, place.along_z(step), send_z.at[(step + 1) // 2, t], got.at[p]).start())
                for side in (1, -1):
                    when(place.has_y(side), lambda side=side: start_y(held(p), p, side, z))
                to_sibling(p).start()

    for t in range(1, ys):
        for step in (1, -1):
            y = place.y - step * t
            here = (y >= 0) if step > 0 else (y < ys)

            @pl.when(here)
            def _(t=t, step=step, y=y):
                for turn in range(zs):
                    p = index((place.z + turn) % zs, y)
                    wait_here(p)
                    if t < ys - 1:
                        when(place.has_y(step), lambda p=p: start_y(held(p), p, step, 0))
                    to_sibling(p).start()

    own.wait()
    for turn in range(1, parts):
        p = (place.seq + turn) % parts
        to_sibling(p).wait_send()
        from_sibling(p).wait_recv()
    for step in (1, -1):
        side = (step + 1) // 2
        for t in range(zs - 1):
            z = place.z - step * t
            sent = jnp.logical_and((z >= 0) if step > 0 else (z < zs), place.has_z(step))
            when(sent, lambda side=side, t=t: push(
                mine, place.seq, place.sibling(), send_z.at[side, t], got.at[place.seq]).wait_send())
        for t in range(ys - 1):
            y = place.y - step * t
            sent = jnp.logical_and((y >= 0) if step > 0 else (y < ys), place.has_y(step))

            @pl.when(sent)
            def _(side=side, y=y):
                for z in range(zs):
                    push(mine, place.seq, place.sibling(), send_y.at[side, index(z, y)], got.at[place.seq]).wait_send()


def gather_weights(shard, parts):
    rows, columns = shard.shape
    zs, ys = seq_sides(parts)
    dma = pltpu.SemaphoreType.DMA
    out = pl.pallas_call(
        partial(gather_kernel, parts),
        in_specs=[pl.BlockSpec(memory_space=pl.ANY)],
        out_specs=pl.BlockSpec(memory_space=pl.ANY),
        out_shape=jax.ShapeDtypeStruct((parts, rows, columns), shard.dtype),
        scratch_shapes=[dma((2, zs)), dma((2, parts)), dma((parts,)), dma((parts,)), dma((parts,)), dma],
        compiler_params=params(collective_id=1, has_side_effects=True),
        cost_estimate=pl.CostEstimate(flops=0, bytes_accessed=parts * rows * columns * 40, transcendentals=0),
        name="gather_weights",
    )(shard)
    return out.reshape(parts * rows, columns)


def add_into(acc, other):
    acc[...] = (acc[...].astype(F32) + other[...].astype(F32)).astype(acc.dtype)


class Line:
    def __init__(self, i, n, to, acc, slot, count, sends, receives):
        self.i, self.n, self.to, self.acc, self.slot, self.count = i, n, to, acc, slot, count
        self.sends, self.receives = sends, receives

    def copy(self, side, j, k):
        return pltpu.make_async_remote_copy(
            src_ref=self.acc(j, k),
            dst_ref=self.slot(side, j, k),
            send_sem=self.sends.at[side, j, k],
            recv_sem=self.receives.at[side, j, k],
            device_id=self.to(1 - 2 * side),
            device_id_type=MESH,
        )

    def take(self, side, j, k):
        self.copy(side, j, k).wait_recv()
        add_into(self.acc(j, k), self.slot(side, j, k))

    def send(self):
        for t in range(self.n - 1):
            for side, j in ((0, self.n - 1 - t), (1, t)):
                beyond = self.i < j if side == 0 else self.i > j
                inner = self.i > 0 if side == 0 else self.i < self.n - 1

                @pl.when(beyond)
                def _(side=side, j=j, inner=inner):
                    for k in range(self.count):
                        if self.n > 2:
                            pl.when(inner)(lambda k=k: self.take(side, j, k))
                        self.copy(side, j, k).start()

    def finish(self):
        for side, inner in ((0, self.i > 0), (1, self.i < self.n - 1)):

            @pl.when(inner)
            def _(side=side):
                for k in range(self.count):
                    self.take(side, self.i, k)

    def drain(self):
        for j in range(self.n):
            for side, beyond in ((0, self.i < j), (1, self.i > j)):

                @pl.when(beyond)
                def _(side=side, j=j):
                    for k in range(self.count):
                        self.copy(side, j, k).wait_send()


def reduce_kernel(parts, grad_ref, band_ref, out_ref, norm_ref, acc, in_c, in_ya, in_zb, in_za, in_yb, in_x, fin, squares, *sems):
    local, s_c, g_c, s_ya, g_ya, s_zb, g_zb, s_za, g_za, s_yb, g_yb, s_x, g_x, s_f, g_f, s_n, g_n = sems
    place = Place(parts)
    zs, ys = place.zs, place.ys
    xs = in_x.shape[0]
    x = place.dp // 2
    wide = acc.shape[-1]
    first = (wide // LANES + 1) // 2 * LANES
    a, b = pl.ds(0, first), pl.ds(first, wide - first)
    lanes = pl.ds(pl.multiple_of(place.core * wide, LANES), wide)
    other = pl.ds(pl.multiple_of((1 - place.core) * wide, LANES), wide)
    x_peers = [(lax.rem(x + t, xs) * 2 + place.core, place.seq) for t in range(1, xs)]
    seq_peers = [(place.dp, lax.rem(place.seq + t, parts)) for t in range(1, parts)]
    barrier = pltpu.get_barrier_semaphore()
    everyone = [place.sibling()] + x_peers + seq_peers
    for to in everyone:
        pl.semaphore_signal(barrier, inc=1, device_id=to, device_id_type=MESH)

    def mine(z):
        return pltpu.make_async_copy(grad_ref.at[z, :, :, lanes], acc.at[z], local.at[z])

    def swap(z):
        return pltpu.make_async_remote_copy(
            src_ref=grad_ref.at[z, :, :, other],
            dst_ref=in_c.at[z],
            send_sem=s_c.at[z],
            recv_sem=g_c.at[z],
            device_id=place.sibling(),
            device_id_type=MESH,
        )

    for z in range(zs):
        mine(z).start()
    pl.semaphore_wait(barrier, len(everyone))
    for z in range(zs):
        swap(z).start()
    line_ya = Line(
        place.y, ys, place.along_y, lambda j, k: acc.at[k, j, :, a], lambda s, j, k: in_ya.at[s, j, k], zs, s_ya, g_ya
    )
    line_zb = Line(
        place.z, zs, place.along_z, lambda j, k: acc.at[j, k, :, b], lambda s, j, k: in_zb.at[s, j, k], ys, s_zb, g_zb
    )
    line_za = Line(
        place.z, zs, place.along_z, lambda j, k: acc.at[j, place.y, :, a], lambda s, j, k: in_za.at[s, j, k], 1, s_za, g_za
    )
    line_yb = Line(
        place.y, ys, place.along_y, lambda j, k: acc.at[place.z, j, :, b], lambda s, j, k: in_yb.at[s, j, k], 1, s_yb, g_yb
    )
    for z in range(zs):
        mine(z).wait()
        swap(z).wait_recv()
        for y in range(ys):
            add_into(acc.at[z, y], in_c.at[z, y])
    line_ya.send()
    line_zb.send()
    line_zb.finish()
    line_yb.send()
    line_ya.finish()
    line_za.send()
    line_yb.finish()
    line_za.finish()
    own = acc.at[place.z, place.y]

    def spread(t):
        return pltpu.make_async_remote_copy(
            src_ref=own, dst_ref=in_x.at[x], send_sem=s_x.at[t], recv_sem=g_x.at[x], device_id=x_peers[t], device_id_type=MESH
        )

    def arrived(t):
        there = lax.rem(x + t + 1, xs)
        return pltpu.make_async_remote_copy(
            src_ref=own, dst_ref=in_x.at[there], send_sem=s_x.at[t], recv_sem=g_x.at[there], device_id=x_peers[t], device_id_type=MESH
        )

    for t in range(xs - 1):
        spread(t).start()
    in_x[x] = own[...]
    for t in range(xs - 1):
        arrived(t).wait_recv()
    total = in_x[0].astype(F32)
    for t in range(1, xs):
        total = total + in_x[t].astype(F32)
    fin[place.core] = total

    def half(c):
        return pltpu.make_async_remote_copy(
            src_ref=fin.at[c], dst_ref=fin.at[c], send_sem=s_f, recv_sem=g_f, device_id=place.sibling(), device_id_type=MESH
        )

    half(place.core).start()
    band = band_ref[...].astype(F32)
    partial_sum = jnp.sum(band * band, axis=(0, 1), keepdims=True)
    half(1 - place.core).wait_recv()
    for c in range(2):
        value = fin[c]
        out_ref[c] = value
        partial_sum = partial_sum + jnp.sum(value * value, axis=(0, 1), keepdims=True)
    squares[place.seq] = jnp.broadcast_to(partial_sum, squares.shape[1:])

    def tell(t):
        return pltpu.make_async_remote_copy(
            src_ref=squares.at[place.seq],
            dst_ref=squares.at[place.seq],
            send_sem=s_n.at[t],
            recv_sem=g_n.at[place.seq],
            device_id=seq_peers[t],
            device_id_type=MESH,
        )

    def told(t):
        there = lax.rem(place.seq + t + 1, parts)
        return pltpu.make_async_remote_copy(
            src_ref=squares.at[there],
            dst_ref=squares.at[there],
            send_sem=s_n.at[t],
            recv_sem=g_n.at[there],
            device_id=seq_peers[t],
            device_id_type=MESH,
        )

    for t in range(parts - 1):
        tell(t).start()
    for t in range(parts - 1):
        told(t).wait_recv()
    norm = squares[0]
    for p in range(1, parts):
        norm = norm + squares[p]
    norm_ref[...] = norm
    for line in (line_ya, line_zb, line_za, line_yb):
        line.drain()
    for z in range(zs):
        swap(z).wait_send()
    for t in range(xs - 1):
        spread(t).wait_send()
    half(place.core).wait_send()
    for t in range(parts - 1):
        tell(t).wait_send()


def reduce_gradient(grad, band, parts, replicas):
    zs, ys = seq_sides(parts)
    rows, columns = grad.shape[0] // parts, grad.shape[1]
    wide = columns // 2
    first = (wide // LANES + 1) // 2 * LANES
    rest = wide - first
    xs = replicas // 2
    dma = pltpu.SemaphoreType.DMA
    any_space = pl.BlockSpec(memory_space=pl.ANY)
    in_vmem = pl.BlockSpec(memory_space=pltpu.VMEM)
    total, norm = pl.pallas_call(
        partial(reduce_kernel, parts),
        in_specs=[any_space, in_vmem],
        out_specs=[in_vmem, in_vmem],
        out_shape=[
            jax.ShapeDtypeStruct((2, rows, wide), F32),
            jax.ShapeDtypeStruct((8, LANES), F32),
        ],
        scratch_shapes=[
            pltpu.VMEM((zs, ys, rows, wide), BF),
            pltpu.VMEM((zs, ys, rows, wide), BF),
            pltpu.VMEM((2, ys, zs, rows, first), BF),
            pltpu.VMEM((2, zs, ys, rows, rest), BF),
            pltpu.VMEM((2, zs, 1, rows, first), BF),
            pltpu.VMEM((2, ys, 1, rows, rest), BF),
            pltpu.VMEM((xs, rows, wide), BF),
            pltpu.VMEM((2, rows, wide), F32),
            pltpu.VMEM((parts, 8, LANES), F32),
            dma((zs,)),
            dma((zs,)),
            dma((zs,)),
            dma((2, ys, zs)),
            dma((2, ys, zs)),
            dma((2, zs, ys)),
            dma((2, zs, ys)),
            dma((2, zs, 1)),
            dma((2, zs, 1)),
            dma((2, ys, 1)),
            dma((2, ys, 1)),
            dma((max(xs - 1, 1),)),
            dma((xs,)),
            dma,
            dma,
            dma((parts - 1,)),
            dma((parts,)),
        ],
        compiler_params=params(collective_id=2, has_side_effects=True),
        cost_estimate=pl.CostEstimate(flops=0, bytes_accessed=columns * rows * parts * 60, transcendentals=0),
        name="reduce_gradient",
    )(grad.reshape(zs, ys, rows, columns), band)
    return jnp.concatenate([total[0], total[1]], axis=1), norm[0, 0]


def rotary_order(columns):
    lead = columns.shape[:-1]
    split = columns.reshape(lead + (-1, 4, 2, HEAD_DIM // 2))
    return jnp.swapaxes(split, -3, -2).reshape(columns.shape)


def head_order(columns):
    lead = columns.shape[:-1]
    split = columns.reshape(lead + (-1, 2, 4, HEAD_DIM // 2))
    return jnp.swapaxes(split, -3, -2).reshape(columns.shape)


def adam_step(master, gradient, first_old, second_old, learn_rate):
    first_new = BETA_ONE * first_old + (1.0 - BETA_ONE) * gradient
    second_new = BETA_TWO * second_old + (1.0 - BETA_TWO) * gradient * gradient
    first_hat = first_new / (1.0 - BETA_ONE**STEP)
    second_hat = second_new / (1.0 - BETA_TWO**STEP)
    updated = master - learn_rate * (first_hat / (jnp.sqrt(second_hat) + ADAM_EPS) + DECAY * master)
    return (updated, first_new, second_new)


def body(
    activations,
    cotangent,
    lengths,
    weight_in,
    weight_out,
    weight_small,
    first_in,
    first_out,
    first_small,
    second_in,
    second_out,
    second_small,
):
    parts = lax.axis_size("seq")
    micro, unused, band_dev, frames, model = activations.shape
    bands, frame_dev = cotangent.shape[2], cotangent.shape[3]
    turned = 2 * INNER_WIDTH
    width_in, width_out = weight_in.shape[2], weight_out.shape[2]
    width_ff = width_in - 3 * INNER_WIDTH
    small_width = weight_small.shape[2]
    full = []
    for layer in range(2):
        packed = jnp.concatenate(
            [
                rotary_order(weight_in[layer, :, :turned].astype(BF)),
                weight_in[layer, :, turned:].astype(BF),
                weight_out[layer].astype(BF),
                jnp.pad(weight_small[layer].astype(BF), ((0, 0), (0, SMALL_LANES - small_width))),
            ],
            axis=1,
        )
        full.append(gather_weights(packed, parts))
    time_tables, band_tables = rotary_tables(frames), rotary_tables(bands)
    frame_base = lax.axis_index("seq") * frame_dev

    def exchange(tensor):
        return lax.all_to_all(tensor, "seq", split_axis=0, concat_axis=0, tiled=True)

    streams, saves = [], []
    for m in range(micro):
        out, *saved = time_forward(m, activations, lengths[m], full[0], time_tables, parts, width_ff)
        saves.append(saved)
        streams.append(exchange(out).reshape(bands, frame_dev, model))
    backs, before = [], ()
    for m in range(micro):
        info = jnp.concatenate([lengths[m], frame_base[None].astype(jnp.int32)])
        kind = BF if m == micro - 1 else F32
        output, back, grad_band = band_both(
            m, streams[m], cotangent, info, full[1], band_tables, before, kind, width_ff
        )
        before = (grad_band, output)
        backs.append(exchange(back.reshape(parts, band_dev, frame_dev, model)))
    before = ()
    for m in range(micro):
        kind = BF if m == micro - 1 else F32
        d_input, grad_time = time_backward(
            m, activations, backs[m], full[0], time_tables, saves[m], before, kind, width_ff
        )
        before = (grad_time, d_input)
    replicas = lax.axis_size("dp")
    shard_band, unused = reduce_gradient(grad_band, jnp.zeros((weight_in.shape[1], grad_band.shape[1]), F32), parts, replicas)
    shard_time, squares = reduce_gradient(grad_time, shard_band, parts, replicas)
    shards = [
        (
            jnp.concatenate([head_order(shard[:, :turned]), shard[:, turned:width_in]], axis=1),
            shard[:, width_in : width_in + width_out],
            shard[:, width_in + width_out : width_in + width_out + small_width],
        )
        for shard in (shard_time, shard_band)
    ]
    shards = tuple(jnp.stack([shards[0][s], shards[1][s]]) for s in range(3))
    grad_norm = jnp.sqrt(squares)
    factor = jnp.minimum(1.0, CLIP_NORM / (grad_norm + 1e-06))
    small_rate = jnp.where(jnp.arange(small_width) < HEAD_COUNT, RATE_GATE, RATE_GAIN)
    new_in = adam_step(weight_in, shards[0] * factor, first_in, second_in, RATE_MATRIX)
    new_out = adam_step(weight_out, shards[1] * factor, first_out, second_out, RATE_MATRIX)
    new_small = adam_step(weight_small, shards[2] * factor, first_small, second_small, small_rate)
    return (
        output,
        d_input,
        grad_norm,
        new_in[0],
        new_out[0],
        new_small[0],
        new_in[1],
        new_out[1],
        new_small[1],
        new_in[2],
        new_out[2],
        new_small[2],
        new_in[0].astype(BF),
        new_out[0].astype(BF),
        new_small[0].astype(BF),
    )


def solution(mesh):
    by_seq = P(None, "seq", None)
    by_band = P(None, "dp", "seq", None, None)
    by_frame = P(None, "dp", None, "seq", None)
    return jax.shard_map(
        body,
        mesh=mesh,
        in_specs=(by_band, by_frame, P(None, "dp")) + (by_seq,) * 9,
        out_specs=(by_frame, by_band, P()) + (by_seq,) * 12,
        check_vma=False,
    )
```

```python
from functools import partial
import math

import jax
import jax.numpy as jnp
from jax import lax
from jax.experimental import pallas as pl
from jax.experimental.pallas import tpu as pltpu
from jax.sharding import PartitionSpec as P

HEAD_COUNT = 8
HEAD_DIM = 64
INNER_WIDTH = 512
STEP = 10
EPS_NORM = 1e-06
BETA_ONE = 0.9
BETA_TWO = 0.999
ADAM_EPS = 1e-08
DECAY = 0.1
RATE_MATRIX = 0.1
RATE_GATE = 0.1
RATE_GAIN = 0.5
CLIP_NORM = 1.0
MASKED = -1e30

BF = jnp.bfloat16
F32 = jnp.float32
GROUP = 256
BLOCK = 256
LANES = 128
SMALL_LANES = 2 * LANES
LOG2E = 1.4426950408889634
SCORE_EXP = LOG2E / math.sqrt(HEAD_DIM)
SQRT_HALF = math.sqrt(0.5)
GAUSS = 1.0 / math.sqrt(2.0 * math.pi)
VMEM_LIMIT = 60 * 2**20


def nn(a, b):
    return lax.dot_general(a, b, (((1,), (0,)), ((), ())), preferred_element_type=F32)


def nt(a, b):
    return lax.dot_general(a, b, (((1,), (1,)), ((), ())), preferred_element_type=F32)


def tn(a, b):
    return lax.dot_general(a, b, (((0,), (0,)), ((), ())), preferred_element_type=F32)


def iota(shape, dim):
    return lax.broadcasted_iota(jnp.int32, shape, dim)


def split_rows(rows):
    high = rows.astype(BF)
    rest = (rows - high.astype(F32)).astype(BF)
    return jnp.concatenate([high, rest], axis=0)


def head_lanes():
    shape = (2 * HEAD_COUNT, INNER_WIDTH)
    return (iota(shape, 1) // HEAD_DIM == iota(shape, 0) % HEAD_COUNT).astype(F32).astype(BF)


def inverse_rms(rows):
    return lax.rsqrt(jnp.mean(rows * rows, axis=-1, keepdims=True) + EPS_NORM)


def norm_back(rows, gain, grad):
    inverse = inverse_rms(rows)
    unit = rows * inverse
    scaled = grad * gain
    d_rows = inverse * (scaled - unit * jnp.mean(scaled * unit, axis=-1, keepdims=True))
    return d_rows, jnp.sum(grad * unit, axis=0, keepdims=True)


def half_lanes(h):
    return (iota((BLOCK, GROUP), 1) % LANES) // (HEAD_DIM // 2) == h


def whole_lanes(h):
    return iota((BLOCK, GROUP), 1) // HEAD_DIM == h


def picked(mask, tensor):
    return jnp.where(mask, tensor, jnp.zeros_like(tensor))


def group_slice(g):
    return slice(g * GROUP, (g + 1) * GROUP)


def forward_block(x, w_ref, small, cos, sin, bias_ref, keep, rows, item, width_ff):
    gate_weight, gain_attn, gain_ff = small
    normed = (x * inverse_rms(x) * gain_attn).astype(BF)
    if "normed" in keep:
        keep["normed"][rows, :] = normed
    gate_rows = jax.nn.sigmoid(nt(gate_weight, normed))
    keep["gate"][item] = gate_rows
    half = GROUP // 2
    for g in range(2):
        for part, name in ((0, "q"), (1, "k")):
            start = part * INNER_WIDTH + g * GROUP
            t = nn(normed, w_ref[:, start : start + GROUP])
            a, b = t[:, :half], t[:, half:]
            keep[name][rows, g * GROUP : g * GROUP + half] = (a * cos - b * sin).astype(BF)
            keep[name][rows, g * GROUP + half : (g + 1) * GROUP] = (b * cos + a * sin).astype(BF)
        start = 2 * INNER_WIDTH + g * GROUP
        keep["v"][rows, group_slice(g)] = nn(normed, w_ref[:, start : start + GROUP]).astype(BF)
    gate = tn(split_rows(gate_rows), head_lanes())
    for g in range(2):
        lanes = group_slice(g)
        queries, keys = keep["q"][rows, lanes], keep["k"][rows, lanes]
        values = keep["v"][rows, lanes]
        attended = None
        for h in range(4):
            scores = nt(picked(half_lanes(h), keys), queries) + bias_ref[...]
            peak = jnp.max(scores, axis=0, keepdims=True)
            terms = jnp.exp2((scores - peak) * SCORE_EXP)
            probs = (terms * (1.0 / jnp.sum(terms, axis=0, keepdims=True))).astype(BF)
            keep["probs"][item, g * 4 + h] = probs
            part = tn(probs, picked(whole_lanes(h), values))
            attended = part if attended is None else attended + part
        keep["gated"][rows, lanes] = (attended * gate[:, lanes]).astype(BF)
    out_start = 3 * INNER_WIDTH + width_ff
    middle = x + nt(keep["gated"][rows, :], w_ref[:, out_start : out_start + INNER_WIDTH])
    keep["middle"][rows, :] = middle
    normed_ff = (middle * inverse_rms(middle) * gain_ff).astype(BF)
    if "normed_ff" in keep:
        keep["normed_ff"][rows, :] = normed_ff
    result = middle
    for c in range(width_ff // GROUP):
        up = 3 * INNER_WIDTH + c * GROUP
        down = out_start + INNER_WIDTH + c * GROUP
        hidden = nn(normed_ff, w_ref[:, up : up + GROUP])
        cumulative = 0.5 + 0.5 * lax.erf(hidden * SQRT_HALF)
        activated = (hidden * cumulative).astype(BF)
        density = jnp.exp2(hidden * hidden * (-0.5 * LOG2E)) * GAUSS
        keep["act"][rows, group_slice(c)] = activated
        keep["slope"][rows, group_slice(c)] = (cumulative + hidden * density).astype(BF)
        result = result + nt(activated, w_ref[:, down : down + GROUP])
    return result


def backward_block(d_out, x, w_ref, small, cos, sin, keep, work, sums, rows, item, width_ff):
    gate_weight, gain_attn, gain_ff = small
    branch = d_out.astype(BF)
    work["branch"][rows, :] = branch
    out_start = 3 * INNER_WIDTH + width_ff
    d_normed_ff = None
    for c in range(width_ff // GROUP):
        up = 3 * INNER_WIDTH + c * GROUP
        down = out_start + INNER_WIDTH + c * GROUP
        d_act = nn(branch, w_ref[:, down : down + GROUP])
        d_hidden = (d_act * keep["slope"][rows, group_slice(c)].astype(F32)).astype(BF)
        work["d_hidden"][rows, group_slice(c)] = d_hidden
        part = nt(d_hidden, w_ref[:, up : up + GROUP])
        d_normed_ff = part if d_normed_ff is None else d_normed_ff + part
    middle = keep["middle"][rows, :]
    d_rows, d_gain_ff = norm_back(middle, gain_ff, d_normed_ff)
    d_middle = d_out + d_rows
    attn_back = d_middle.astype(BF)
    work["attn_back"][rows, :] = attn_back
    gate_rows = keep["gate"][item]
    lanes_of = head_lanes()
    gate = tn(split_rows(gate_rows), lanes_of)
    d_gated = nn(attn_back, w_ref[:, out_start : out_start + INNER_WIDTH])
    product = d_gated * keep["gated"][rows, :].astype(F32)
    high = product.astype(BF)
    rest = (product - high.astype(F32)).astype(BF)
    delta_rows = (nt(lanes_of, high) + nt(lanes_of, rest))[:HEAD_COUNT]
    d_logit = split_rows(delta_rows * (1.0 - gate_rows))
    d_attended = (d_gated * gate).astype(BF)
    half = GROUP // 2
    scale = HEAD_DIM**-0.5
    for g in range(2):
        lanes = group_slice(g)
        queries, keys = keep["q"][rows, lanes], keep["k"][rows, lanes]
        values, d_att = keep["v"][rows, lanes], d_attended[:, lanes]
        d_query = d_keys = d_values = None
        for h in range(4):
            halves, wholes = half_lanes(h), whole_lanes(h)
            key_h = picked(halves, keys)
            probs = keep["probs"][item, g * 4 + h]
            d_probs = nt(picked(wholes, values), d_att)
            delta = delta_rows[g * 4 + h : g * 4 + h + 1, :]
            d_scores = (probs.astype(F32) * (d_probs - delta)).astype(BF)
            part_v = nn(probs, picked(wholes, d_att))
            part_k = nn(d_scores, picked(halves, queries))
            part_q = tn(d_scores, key_h)
            if h == 0:
                d_query, d_keys, d_values = part_q, part_k, part_v
            else:
                d_query, d_keys, d_values = d_query + part_q, d_keys + part_k, d_values + part_v
        for start, t in ((0, d_query), (INNER_WIDTH, d_keys)):
            t = t * scale
            a, b = t[:, :half], t[:, half:]
            start = start + g * GROUP
            work["d_proj"][rows, start : start + half] = (a * cos + b * sin).astype(BF)
            work["d_proj"][rows, start + half : start + GROUP] = (b * cos - a * sin).astype(BF)
        start = 2 * INNER_WIDTH + g * GROUP
        work["d_proj"][rows, start : start + GROUP] = d_values.astype(BF)
    twice = jnp.concatenate([gate_weight, gate_weight], axis=0)
    d_normed = tn(d_logit, twice)
    for c in range(3 * INNER_WIDTH // INNER_WIDTH):
        part = slice(c * INNER_WIDTH, (c + 1) * INNER_WIDTH)
        d_normed = d_normed + nt(work["d_proj"][rows, part], w_ref[:, part])
    d_rows, d_gain_attn = norm_back(x, gain_attn, d_normed)
    d_gate = nn(d_logit, work["normed"][rows, :])
    sums[0:HEAD_COUNT, :] += d_gate[:HEAD_COUNT] + d_gate[HEAD_COUNT:]
    sums[HEAD_COUNT : HEAD_COUNT + 1, :] += d_gain_attn
    sums[HEAD_COUNT + 1 : HEAD_COUNT + 2, :] += d_gain_ff
    return d_middle + d_rows


def weight_sums(total, work, keep, width_ff):
    out_start = 3 * INNER_WIDTH + width_ff
    pairs = (
        (work["normed"], work["d_proj"], 0),
        (work["normed_ff"], work["d_hidden"], 3 * INNER_WIDTH),
        (work["attn_back"], keep["gated"], out_start),
        (work["branch"], keep["act"], out_start + INNER_WIDTH),
    )
    for left, right, start in pairs:
        turned = left[...].T
        for c in range(right.shape[-1] // INNER_WIDTH):
            part = slice(start + c * INNER_WIDTH, start + (c + 1) * INNER_WIDTH)
            total[:, part] += nn(turned, right[:, c * INNER_WIDTH : (c + 1) * INNER_WIDTH])


def turn_small(w_ref, small_ref):
    width = w_ref.shape[1] - SMALL_LANES
    rows = w_ref[:, width : width + LANES].astype(F32).T
    small_ref[...] = rows[: small_ref.shape[0]]


def small_parts(small_ref):
    gate_weight = small_ref[0:HEAD_COUNT, :].astype(BF)
    return (
        gate_weight,
        small_ref[HEAD_COUNT : HEAD_COUNT + 1, :],
        small_ref[HEAD_COUNT + 1 : HEAD_COUNT + 2, :],
    )


def finish_sums(total, sums, out_ref, arrival):
    width = total.shape[1] - SMALL_LANES
    model = total.shape[0]
    tall = jnp.concatenate([sums[...], jnp.zeros((SMALL_LANES - sums.shape[0], model), F32)], axis=0)
    if out_ref.dtype == F32:
        total[:, width:] = tall.T
        copy = pltpu.make_async_copy(total, out_ref, arrival)
        copy.start()
        copy.wait()
    else:
        out_ref[:, :width] = total[:, :width].astype(out_ref.dtype)
        out_ref[:, width:] = tall.T.astype(out_ref.dtype)


def start_sums(total, sums, before_ref, arrival):
    sums[...] = jnp.zeros_like(sums)
    if before_ref is None:
        total[...] = jnp.zeros_like(total)
    else:
        pltpu.make_async_copy(before_ref, total, arrival).start()


def await_sums(total, sums, before_ref, arrival):
    if before_ref is not None:
        width = total.shape[1] - SMALL_LANES
        pltpu.make_async_copy(before_ref, total, arrival).wait()
        sums[...] += total[:, width:].T[: sums.shape[0]]


SAVED = ("q", "k", "v", "gate", "probs", "gated", "middle", "act", "slope")


def time_forward_kernel(parts, width_ff, ride, x_ref, w_ref, cos_ref, sin_ref, bias_ref, *refs):
    step, steps = pl.program_id(0), pl.num_programs(0)
    if ride:
        shard_ref, out_ref, refs, full_ref = refs[0], refs[1], refs[2:], refs[11]
        gather = Gather(Place(parts), shard_ref, full_ref, *refs[-6:])
        small_ref = refs[-7]
        pl.when(step == 0)(gather.start)
        for hop in range(1, gather.hops + 1):
            pl.when(step == hop * steps // (gather.hops + 1))(partial(gather.hop, hop))
    else:
        out_ref, refs = refs[0], refs[1:]
        small_ref = refs[-1]
    keep = dict(zip(SAVED, refs))

    @pl.when(step == 0)
    def _():
        turn_small(w_ref, small_ref)

    x = x_ref[0].astype(F32)
    out = forward_block(
        x, w_ref, small_parts(small_ref), cos_ref[...], sin_ref[...], bias_ref, keep, slice(None), 0, width_ff
    )
    unused, alone, frames, model = out_ref.shape
    out_ref[:, 0] = out.reshape(parts, frames, model).astype(BF)
    if ride:
        pl.when(step == steps - 1)(gather.finish)


def time_backward_kernel(parts, width_ff, chained, ride, per_step, *refs):
    x_ref, d_ref, w_ref, cos_ref, sin_ref = refs[:5]
    keep = dict(zip(SAVED, refs[5:14]))
    refs = refs[14:]
    before = refs[0] if chained else None
    if chained:
        refs = refs[2:]
    step, steps = pl.program_id(0), pl.num_programs(0)
    if ride:
        other_ref, dx_ref, grad_ref, shard_ref = refs[:4]
        reduction = Reduction(Place(parts), other_ref, refs[-REDUCE_SCRATCH:])
        refs = refs[:-REDUCE_SCRATCH]
    else:
        dx_ref, grad_ref = refs[:2]
    total, sums, normed, normed_ff, d_hidden, attn_back, branch, d_proj, arrival, small_ref = refs[-10:]
    work = dict(
        normed=normed, normed_ff=normed_ff, d_hidden=d_hidden, attn_back=attn_back, branch=branch, d_proj=d_proj
    )

    @pl.when(step == 0)
    def _():
        start_sums(total, sums, before, arrival)
        turn_small(w_ref, small_ref)

    small = small_parts(small_ref)

    def one(i, carry):
        if ride:
            reduction.advance(step * per_step + i, steps * per_step - 1)
        rows = pl.ds(pl.multiple_of(i * BLOCK, BLOCK), BLOCK)
        x = x_ref[i].astype(F32)
        work["normed"][rows, :] = (x * inverse_rms(x) * small[1]).astype(BF)
        middle = keep["middle"][rows, :]
        work["normed_ff"][rows, :] = (middle * inverse_rms(middle) * small[2]).astype(BF)
        d_out = d_ref[:, i].astype(F32).reshape(BLOCK, x.shape[1])
        dx_ref[i] = backward_block(
            d_out, x, w_ref, small, cos_ref[...], sin_ref[...], keep, work, sums, rows, i, width_ff
        )
        return carry

    lax.fori_loop(0, per_step, one, 0)
    if chained:

        @pl.when(step == 0)
        def _():
            await_sums(total, sums, before, arrival)

    weight_sums(total, work, keep, width_ff)

    @pl.when(step == steps - 1)
    def _():
        finish_sums(total, sums, grad_ref, arrival)
        if ride:
            reduction.finish(shard_ref)


def gather_rows(ref, strides, factors):
    return jnp.concatenate(
        [
            jnp.concatenate([ref[p, s, :] * f for p in range(ref.shape[0])], axis=1)
            for s, f in zip(strides, factors)
        ],
        axis=0,
    )


def band_kernel(width_ff, chained, info_ref, *refs):
    x_ref, d_ref, w_ref, cos_ref, sin_ref, bias_ref = refs[:6]
    refs = refs[6:]
    before = refs[0] if chained else None
    out_ref, back_ref, grad_ref = refs[2:5] if chained else refs[:3]
    scratch = refs[-21:]
    keep = dict(zip(SAVED, scratch[:9]))
    total, sums, normed, normed_ff, d_hidden, attn_back, branch, d_proj, arrival, small_ref, rows_a, rows_b = scratch[9:]
    work = dict(
        normed=normed, normed_ff=normed_ff, d_hidden=d_hidden, attn_back=attn_back, branch=branch, d_proj=d_proj
    )
    keep.update(normed=normed, normed_ff=normed_ff)
    step = pl.program_id(0)
    bands, frames, model = x_ref.shape
    together = BLOCK // bands
    pieces = model // LANES

    @pl.when(step == 0)
    def _():
        start_sums(total, sums, before, arrival)
        turn_small(w_ref, small_ref)

    small = small_parts(small_ref)
    for p in range(pieces):
        lanes = slice(p * LANES, (p + 1) * LANES)
        rows_a[p] = x_ref[:, :, lanes].astype(F32).reshape(bands * frames, LANES)
        rows_b[p] = d_ref[:, :, lanes].astype(F32).reshape(bands * frames, LANES)
    first = info_ref[1] + step * frames

    def one(j, carry):
        rows = pl.ds(pl.multiple_of(j * BLOCK, BLOCK), BLOCK)
        strides = [pl.ds(j * together + f, bands, stride=frames) for f in range(together)]
        valid = [
            (first + j * together + f < info_ref[0]).astype(F32) for f in range(together)
        ]
        x = gather_rows(rows_a, strides, [1.0] * together)
        d_out = gather_rows(rows_b, strides, valid)
        out = forward_block(
            x, w_ref, small, cos_ref[...], sin_ref[...], bias_ref, keep, rows, j, width_ff
        )
        for f in range(together):
            for p in range(pieces):
                part = out[f * bands : (f + 1) * bands, p * LANES : (p + 1) * LANES]
                rows_a[p, strides[f], :] = part * valid[f]
        back = backward_block(
            d_out, x, w_ref, small, cos_ref[...], sin_ref[...], keep, work, sums, rows, j, width_ff
        )
        for f in range(together):
            for p in range(pieces):
                part = back[f * bands : (f + 1) * bands, p * LANES : (p + 1) * LANES]
                rows_b[p, strides[f], :] = part
        return carry

    lax.fori_loop(0, frames // together, one, 0)
    for p in range(pieces):
        lanes = slice(p * LANES, (p + 1) * LANES)
        out_ref[:, :, lanes] = rows_a[p].reshape(bands, frames, LANES).astype(BF)
        back_ref[:, :, lanes] = rows_b[p].reshape(bands, frames, LANES).astype(BF)
    if chained:

        @pl.when(step == 0)
        def _():
            await_sums(total, sums, before, arrival)

    weight_sums(total, work, keep, width_ff)

    @pl.when(step == pl.num_programs(0) - 1)
    def _():
        finish_sums(total, sums, grad_ref, arrival)


def whole(shape):
    return pl.BlockSpec(shape, lambda *i: (0,) * len(shape), pipeline_mode=pl.Buffered(1))


def params(**more):
    return pltpu.CompilerParams(vmem_limit_bytes=VMEM_LIMIT, **more)


def rotary_tables(positions):
    half_width = HEAD_DIM // 2
    inverse = 10000.0 ** (-(jnp.arange(half_width, dtype=F32) * 2.0 / HEAD_DIM))
    angles = jnp.arange(positions, dtype=F32)[:, None] * inverse[None, :]
    angles = jnp.tile(angles, (BLOCK // positions, LANES // half_width))
    return (jnp.cos(angles), jnp.sin(angles))


def saved_shapes(tokens, items, model, width_ff):
    return (
        ((tokens, INNER_WIDTH), BF),
        ((tokens, INNER_WIDTH), BF),
        ((tokens, INNER_WIDTH), BF),
        ((items, HEAD_COUNT, BLOCK), F32),
        ((items, HEAD_COUNT, BLOCK, BLOCK), BF),
        ((tokens, INNER_WIDTH), BF),
        ((tokens, model), F32),
        ((tokens, width_ff), BF),
        ((tokens, width_ff), BF),
    )


def saved_specs(tokens, items, model, width_ff):
    return [
        pl.BlockSpec(shape, lambda i, *s, n=len(shape): (i,) + (0,) * (n - 1))
        for shape, kind in saved_shapes(tokens, items, model, width_ff)
    ]


def work_shapes(tokens, model, width_ff, columns):
    return [
        pltpu.VMEM((model, columns), F32),
        pltpu.VMEM((2 * HEAD_COUNT, model), F32),
        pltpu.VMEM((tokens, model), BF),
        pltpu.VMEM((tokens, model), BF),
        pltpu.VMEM((tokens, width_ff), BF),
        pltpu.VMEM((tokens, model), BF),
        pltpu.VMEM((tokens, model), BF),
        pltpu.VMEM((tokens, 3 * INNER_WIDTH), BF),
        pltpu.SemaphoreType.DMA,
        pltpu.VMEM((2 * HEAD_COUNT, model), F32),
    ]


def at_micro(m, shape, place):
    return pl.BlockSpec((None, None) + shape, lambda i, *s: (m, 0) + place(i))


def time_forward(m, x, bias, weights, tables, shard, parts, width_ff):
    seqs, frames, model = x.shape[2:]
    tokens = seqs * frames
    shapes = saved_shapes(tokens, seqs, model, width_ff)
    out = jax.ShapeDtypeStruct((parts, seqs, frames // parts, model), BF)
    ride = shard is not None
    any_space = pl.BlockSpec(memory_space=pl.ANY)
    full = [jax.ShapeDtypeStruct((parts,) + shard.shape, BF)] if ride else []
    results = pl.pallas_call(
        partial(time_forward_kernel, parts, width_ff, ride),
        grid=(seqs,),
        in_specs=[
            at_micro(m, (1, frames, model), lambda i: (i, 0, 0)),
            whole(weights.shape),
            whole(tables[0].shape),
            whole(tables[1].shape),
            whole(bias.shape),
        ]
        + [any_space] * ride,
        out_specs=[
            pl.BlockSpec((parts, 1, frames // parts, model), lambda i: (0, i, 0, 0)),
            *saved_specs(frames, 1, model, width_ff),
        ]
        + [any_space] * ride,
        scratch_shapes=[pltpu.VMEM((2 * HEAD_COUNT, model), F32)] + (gather_scratch(parts) if ride else []),
        out_shape=[out, *(jax.ShapeDtypeStruct(s, k) for s, k in shapes)] + full,
        compiler_params=params(collective_id=3, has_side_effects=True) if ride else params(),
        cost_estimate=pl.CostEstimate(
            flops=int(tokens * 5e6), bytes_accessed=tokens * 15000, transcendentals=tokens * 5000
        ),
        name="time_forward_gather" if ride else "time_forward",
    )(x, weights, *tables, bias, *([shard] if ride else []))
    saved = results[1 : 1 + len(SAVED)]
    return results[0], saved, (results[-1].reshape(-1, shard.shape[1]) if ride else None)


def time_backward(m, x, d_out, weights, tables, saved, before, other, kind, width_ff):
    seqs, frames, model = x.shape[2:]
    tokens = seqs * frames
    parts, unused, part_frames, unused_model = d_out.shape
    per_step = 2 if seqs % 2 == 0 else 1
    columns = weights.shape[1]
    ride = other is not None
    ins = [x, d_out, weights, *tables, *saved, *before]
    aliases = {len(ins) - 1: 0} if before else {}
    more_specs, more_shapes, scratch = [], [], []
    any_space = pl.BlockSpec(memory_space=pl.ANY)
    if ride:
        zs, ys = seq_sides(parts)
        part = model // parts
        ins.append(other.reshape(zs, ys, part, columns))
        more_shapes = [jax.ShapeDtypeStruct((2, part, columns // 2), F32)]
        more_specs = [whole(more_shapes[0].shape)]
        scratch = reduce_scratch(parts, lax.axis_size("dp"), part, columns)
    rows = at_micro(m, (per_step, frames, model), lambda i: (i, 0, 0))
    return pl.pallas_call(
        partial(time_backward_kernel, parts, width_ff, bool(before), ride, per_step),
        grid=(seqs // per_step,),
        in_specs=[
            rows,
            pl.BlockSpec((parts, per_step, part_frames, model), lambda i: (0, i, 0, 0)),
            whole(weights.shape),
            whole(tables[0].shape),
            whole(tables[1].shape),
            *saved_specs(per_step * frames, per_step, model, width_ff),
        ]
        + [any_space] * (len(before) + ride),
        out_specs=[rows, any_space if kind == F32 else whole((model, columns))] + more_specs,
        out_shape=[
            jax.ShapeDtypeStruct(x.shape, F32),
            jax.ShapeDtypeStruct((model, columns), kind),
        ]
        + more_shapes,
        input_output_aliases=aliases,
        scratch_shapes=work_shapes(per_step * frames, model, width_ff, columns) + scratch,
        compiler_params=params(collective_id=4, has_side_effects=True) if ride else params(),
        cost_estimate=pl.CostEstimate(
            flops=int(tokens * 9e6), bytes_accessed=tokens * 18000, transcendentals=0
        ),
        name="time_backward_reduce" if ride else "time_backward",
    )(*ins)


def band_both(m, x, d_out, info, weights, tables, bias, before, kind, width_ff):
    bands, frames, model = x.shape
    tokens = bands * frames
    chunk = math.gcd(frames, 16)
    step_tokens = bands * chunk
    columns = weights.shape[1]
    ins = [info, x, d_out, weights, *tables, bias, *before]
    rows = pl.BlockSpec((bands, chunk, model), lambda i, s: (0, i, 0))
    rows_m = at_micro(m, (bands, chunk, model), lambda i: (0, i, 0))
    any_space = pl.BlockSpec(memory_space=pl.ANY)
    saved = [
        pltpu.VMEM(s, k) for s, k in saved_shapes(step_tokens, step_tokens // BLOCK, model, width_ff)
    ]
    return pl.pallas_call(
        partial(band_kernel, width_ff, bool(before)),
        grid_spec=pltpu.PrefetchScalarGridSpec(
            num_scalar_prefetch=1,
            grid=(frames // chunk,),
            in_specs=[
                rows,
                rows_m,
                whole(weights.shape),
                whole(tables[0].shape),
                whole(tables[1].shape),
                whole(bias.shape),
            ]
            + [any_space] * len(before),
            out_specs=[rows_m, rows, any_space if kind == F32 else whole((model, columns))],
            scratch_shapes=saved
            + work_shapes(step_tokens, model, width_ff, columns)
            + [pltpu.VMEM((model // LANES, step_tokens, LANES), F32)] * 2,
        ),
        out_shape=[
            jax.ShapeDtypeStruct(d_out.shape, BF),
            jax.ShapeDtypeStruct(x.shape, BF),
            jax.ShapeDtypeStruct((model, columns), kind),
        ],
        input_output_aliases={len(ins) - 1: 0} if before else {},
        compiler_params=params(),
        cost_estimate=pl.CostEstimate(
            flops=int(tokens * 14e6), bytes_accessed=tokens * 8000, transcendentals=tokens * 5000
        ),
        name="band_both",
    )(*ins)


MESH = pl.DeviceIdType.MESH


def seq_sides(parts):
    side = 1
    while 4 * side * side <= parts:
        side *= 2
    return parts // side, side


class Place:
    def __init__(self, parts):
        self.dp, self.seq = lax.axis_index("dp"), lax.axis_index("seq")
        self.core = self.dp % 2
        self.zs, self.ys = seq_sides(parts)
        self.z, self.y = self.seq // self.ys, self.seq % self.ys

    def sibling(self):
        return (self.dp + 1 - 2 * self.core, self.seq)

    def along_z(self, step):
        return (self.dp, self.seq + step * self.ys)

    def along_y(self, step):
        return (self.dp, self.seq + step)

    def has_z(self, step):
        return self.z + step < self.zs if step > 0 else self.z + step >= 0

    def has_y(self, step):
        return self.y + step < self.ys if step > 0 else self.y + step >= 0


def greet(place, others=()):
    barrier = pltpu.get_barrier_semaphore()
    pl.semaphore_signal(barrier, inc=1, device_id=place.sibling(), device_id_type=MESH)
    for other in others:
        pl.semaphore_signal(barrier, inc=1, device_id=other, device_id_type=MESH)
    for step in (1, -1):
        for has, to in ((place.has_z, place.along_z), (place.has_y, place.along_y)):

            @pl.when(has(step))
            def _(to=to, step=step):
                pl.semaphore_signal(barrier, inc=1, device_id=to(step), device_id_type=MESH)

    count = 1 + len(others)
    for has in (place.has_z, place.has_y):
        count = count + has(1).astype(jnp.int32) + has(-1).astype(jnp.int32)
    pl.semaphore_wait(barrier, count)


class Gather:
    def __init__(self, place, shard_ref, out_ref, send_z, send_y, send_c, got, got_c, local):
        self.place, self.shard, self.out = place, shard_ref, out_ref
        self.send_z, self.send_y, self.send_c, self.got, self.got_c, self.local = send_z, send_y, send_c, got, got_c, local
        wide = shard_ref.shape[1] // 2
        self.lanes = pl.ds(pl.multiple_of(place.core * wide, LANES), wide)
        self.other_lanes = pl.ds(pl.multiple_of((1 - place.core) * wide, LANES), wide)
        self.mine = shard_ref.at[:, self.lanes]
        self.hops = place.zs

    def index(self, z, y):
        return z * self.place.ys + y

    def held(self, p):
        return self.out.at[p, :, self.lanes]

    def push(self, source, p, to, send, receive):
        return pltpu.make_async_remote_copy(
            src_ref=source, dst_ref=self.held(p), send_sem=send, recv_sem=receive, device_id=to, device_id_type=MESH
        )

    def to_sibling(self, p):
        return self.push(self.held(p), p, self.place.sibling(), self.send_c.at[p], self.got_c.at[p])

    def from_sibling(self, p):
        there = self.out.at[p, :, self.other_lanes]
        return pltpu.make_async_remote_copy(
            src_ref=there,
            dst_ref=there,
            send_sem=self.send_c.at[p],
            recv_sem=self.got_c.at[p],
            device_id=self.place.sibling(),
            device_id_type=MESH,
        )

    def along_z(self, source, p, step, t):
        return self.push(source, p, self.place.along_z(step), self.send_z.at[(step + 1) // 2, t], self.got.at[p])

    def along_y(self, source, p, step):
        return self.push(source, p, self.place.along_y(step), self.send_y.at[(step + 1) // 2, p], self.got.at[p])

    def await_block(self, p):
        self.push(self.held(p), p, self.place.sibling(), self.send_c.at[p], self.got.at[p]).wait_recv()

    def own(self):
        return pltpu.make_async_copy(self.shard, self.out.at[self.place.seq], self.local)

    def start(self):
        place = self.place
        greet(place)
        self.own().start()
        for step in (1, -1):
            pl.when(place.has_z(step))(lambda step=step: self.along_z(self.mine, place.seq, step, 0).start())
            pl.when(place.has_y(step))(lambda step=step: self.along_y(self.mine, place.seq, step).start())

    def hop(self, t):
        if t == self.place.zs:
            return self.other_lines()
        place = self.place
        for step in (1, -1):
            z = place.z - step * t
            here = (z >= 0) if step > 0 else (z < place.zs)

            @pl.when(here)
            def _(step=step, z=z):
                p = self.index(z, place.y)
                self.await_block(p)
                if t < place.zs - 1:
                    pl.when(place.has_z(step))(lambda: self.along_z(self.held(p), p, step, t).start())
                for side in (1, -1):
                    pl.when(place.has_y(side))(lambda side=side: self.along_y(self.held(p), p, side).start())
                self.to_sibling(p).start()

    def other_lines(self):
        place = self.place
        for t in range(1, place.ys):
            for step in (1, -1):
                y = place.y - step * t
                here = (y >= 0) if step > 0 else (y < place.ys)

                @pl.when(here)
                def _(t=t, step=step, y=y):
                    for turn in range(place.zs):
                        p = self.index(lax.rem(place.z + turn, place.zs), y)
                        self.await_block(p)
                        if t < place.ys - 1:
                            pl.when(place.has_y(step))(lambda p=p: self.along_y(self.held(p), p, step).start())
                        self.to_sibling(p).start()

    def finish(self):
        place = self.place
        self.own().wait()
        for turn in range(1, place.zs * place.ys):
            p = lax.rem(place.seq + turn, place.zs * place.ys)
            self.to_sibling(p).wait_send()
            self.from_sibling(p).wait_recv()
        for step in (1, -1):
            for t in range(place.zs - 1):
                z = place.z - step * t
                sent = jnp.logical_and((z >= 0) if step > 0 else (z < place.zs), place.has_z(step))
                pl.when(sent)(lambda step=step, t=t: self.along_z(self.mine, place.seq, step, t).wait_send())
            for t in range(place.ys - 1):
                y = place.y - step * t
                sent = jnp.logical_and((y >= 0) if step > 0 else (y < place.ys), place.has_y(step))

                @pl.when(sent)
                def _(step=step, y=y):
                    for z in range(place.zs):
                        self.along_y(self.mine, self.index(z, y), step).wait_send()


def gather_kernel(parts, shard_ref, out_ref, *sems):
    gather = Gather(Place(parts), shard_ref, out_ref, *sems)
    gather.start()
    for hop in range(1, gather.hops + 1):
        gather.hop(hop)
    gather.finish()


def gather_scratch(parts):
    zs, ys = seq_sides(parts)
    dma = pltpu.SemaphoreType.DMA
    return [dma((2, zs)), dma((2, parts)), dma((parts,)), dma((parts,)), dma((parts,)), dma]


def gather_weights(shard, parts):
    rows, columns = shard.shape
    out = pl.pallas_call(
        partial(gather_kernel, parts),
        in_specs=[pl.BlockSpec(memory_space=pl.ANY)],
        out_specs=pl.BlockSpec(memory_space=pl.ANY),
        out_shape=jax.ShapeDtypeStruct((parts, rows, columns), shard.dtype),
        scratch_shapes=gather_scratch(parts),
        compiler_params=params(collective_id=1, has_side_effects=True),
        cost_estimate=pl.CostEstimate(flops=0, bytes_accessed=parts * rows * columns * 40, transcendentals=0),
        name="gather_weights",
    )(shard)
    return out.reshape(parts * rows, columns)


def add_into(acc, other):
    acc[...] = (acc[...].astype(F32) + other[...].astype(F32)).astype(acc.dtype)


class Line:
    def __init__(self, i, n, to, acc, slot, count, sends, receives):
        self.i, self.n, self.to, self.acc, self.slot, self.count = i, n, to, acc, slot, count
        self.sends, self.receives = sends, receives

    def copy(self, side, j, k):
        return pltpu.make_async_remote_copy(
            src_ref=self.acc(j, k),
            dst_ref=self.slot(side, j, k),
            send_sem=self.sends.at[side, j, k],
            recv_sem=self.receives.at[side, j, k],
            device_id=self.to(1 - 2 * side),
            device_id_type=MESH,
        )

    def take(self, side, j, k):
        self.copy(side, j, k).wait_recv()
        add_into(self.acc(j, k), self.slot(side, j, k))

    def send(self, now, base):
        for t in range(self.n - 1):
            for side, j, passed in ((0, self.n - 1 - t, self.i), (1, t, self.n - 1 - self.i)):
                beyond = self.i < j if side == 0 else self.i > j
                inner = self.i > 0 if side == 0 else self.i < self.n - 1

                @pl.when(jnp.logical_and(beyond, now(base + passed + t)))
                def _(side=side, j=j, inner=inner):
                    for k in range(self.count):
                        if self.n > 2:
                            pl.when(inner)(lambda k=k: self.take(side, j, k))
                        self.copy(side, j, k).start()

    def finish(self):
        for side, inner in ((0, self.i > 0), (1, self.i < self.n - 1)):

            @pl.when(inner)
            def _(side=side):
                for k in range(self.count):
                    self.take(side, self.i, k)

    def drain(self):
        for j in range(self.n):
            for side, beyond in ((0, self.i < j), (1, self.i > j)):

                @pl.when(beyond)
                def _(side=side, j=j):
                    for k in range(self.count):
                        self.copy(side, j, k).wait_send()


REDUCE_SCRATCH = 23


def reduce_scratch(parts, replicas, rows, columns):
    zs, ys = seq_sides(parts)
    wide = columns // 2
    first = (wide // LANES + 1) // 2 * LANES
    rest = wide - first
    xs = replicas // 2
    dma = pltpu.SemaphoreType.DMA
    return [
        pltpu.VMEM((zs, ys, rows, wide), BF),
        pltpu.VMEM((zs, ys, rows, wide), BF),
        pltpu.VMEM((2, ys, zs, rows, first), BF),
        pltpu.VMEM((2, zs, ys, rows, rest), BF),
        pltpu.VMEM((2, zs, 1, rows, first), BF),
        pltpu.VMEM((2, ys, 1, rows, rest), BF),
        pltpu.VMEM((xs, rows, wide), BF),
        pltpu.VMEM((2, rows, wide), F32),
        dma((zs,)),
        dma((zs,)),
        dma((zs,)),
        dma((2, ys, zs)),
        dma((2, ys, zs)),
        dma((2, zs, ys)),
        dma((2, zs, ys)),
        dma((2, zs, 1)),
        dma((2, zs, 1)),
        dma((2, ys, 1)),
        dma((2, ys, 1)),
        dma((max(xs - 1, 1),)),
        dma((xs,)),
        dma,
        dma,
    ]


class Reduction:
    def __init__(self, place, grad_ref, scratch, others=()):
        self.place, self.grad, self.others = place, grad_ref, list(others)
        self.acc, self.in_c, in_ya, in_zb, in_za, in_yb, self.in_x, self.fin = scratch[:8]
        self.local, self.s_c, self.g_c, s_ya, g_ya, s_zb, g_zb, s_za, g_za, s_yb, g_yb = scratch[8:19]
        self.s_x, self.g_x, self.s_f, self.g_f = scratch[19:]
        acc = self.acc
        zs, ys = place.zs, place.ys
        self.xs = self.in_x.shape[0]
        self.x = place.dp // 2
        wide = acc.shape[-1]
        first = (wide // LANES + 1) // 2 * LANES
        a, b = pl.ds(0, first), pl.ds(first, wide - first)
        self.lanes = pl.ds(pl.multiple_of(place.core * wide, LANES), wide)
        self.other = pl.ds(pl.multiple_of((1 - place.core) * wide, LANES), wide)
        self.x_peers = [(lax.rem(self.x + t, self.xs) * 2 + place.core, place.seq) for t in range(1, self.xs)]
        self.line_ya = Line(
            place.y, ys, place.along_y, lambda j, k: acc.at[k, j, :, a], lambda s, j, k: in_ya.at[s, j, k], zs, s_ya, g_ya
        )
        self.line_zb = Line(
            place.z, zs, place.along_z, lambda j, k: acc.at[j, k, :, b], lambda s, j, k: in_zb.at[s, j, k], ys, s_zb, g_zb
        )
        self.line_za = Line(
            place.z, zs, place.along_z, lambda j, k: acc.at[j, place.y, :, a], lambda s, j, k: in_za.at[s, j, k], 1, s_za, g_za
        )
        self.line_yb = Line(
            place.y, ys, place.along_y, lambda j, k: acc.at[place.z, j, :, b], lambda s, j, k: in_yb.at[s, j, k], 1, s_yb, g_yb
        )
        self.own = acc.at[place.z, place.y]

    def mine(self, z):
        return pltpu.make_async_copy(self.grad.at[z, :, :, self.lanes], self.acc.at[z], self.local.at[z])

    def swap(self, z):
        return pltpu.make_async_remote_copy(
            src_ref=self.grad.at[z, :, :, self.other],
            dst_ref=self.in_c.at[z],
            send_sem=self.s_c.at[z],
            recv_sem=self.g_c.at[z],
            device_id=self.place.sibling(),
            device_id_type=MESH,
        )

    def spread(self, t):
        return pltpu.make_async_remote_copy(
            src_ref=self.own,
            dst_ref=self.in_x.at[self.x],
            send_sem=self.s_x.at[t],
            recv_sem=self.g_x.at[self.x],
            device_id=self.x_peers[t],
            device_id_type=MESH,
        )

    def arrived(self, t):
        there = lax.rem(self.x + t + 1, self.xs)
        return pltpu.make_async_remote_copy(
            src_ref=self.own,
            dst_ref=self.in_x.at[there],
            send_sem=self.s_x.at[t],
            recv_sem=self.g_x.at[there],
            device_id=self.x_peers[t],
            device_id_type=MESH,
        )

    def half(self, c):
        return pltpu.make_async_remote_copy(
            src_ref=self.fin.at[c],
            dst_ref=self.fin.at[c],
            send_sem=self.s_f,
            recv_sem=self.g_f,
            device_id=self.place.sibling(),
            device_id_type=MESH,
        )

    def greet(self):
        place = self.place
        barrier = pltpu.get_barrier_semaphore()
        lines = [] if self.others else [(place.has_z, place.along_z), (place.has_y, place.along_y)]
        count = 0
        for to in [place.sibling()] + self.x_peers + self.others:
            pl.semaphore_signal(barrier, inc=1, device_id=to, device_id_type=MESH)
            count = count + 1
        for has, to in lines:
            for step in (1, -1):
                pl.when(has(step))(
                    lambda to=to, step=step: pl.semaphore_signal(
                        barrier, inc=1, device_id=to(step), device_id_type=MESH
                    )
                )
                count = count + has(step).astype(jnp.int32)
        pl.semaphore_wait(barrier, count)

    def open(self):
        for z in range(self.place.zs):
            self.mine(z).start()
        self.greet()
        for z in range(self.place.zs):
            self.swap(z).start()

    def fold_cores(self):
        for z in range(self.place.zs):
            self.mine(z).wait()
            self.swap(z).wait_recv()
            for y in range(self.place.ys):
                add_into(self.acc.at[z, y], self.in_c.at[z, y])

    def spread_all(self):
        for t in range(self.xs - 1):
            self.spread(t).start()

    def fold_x(self):
        self.in_x[self.x] = self.own[...]
        for t in range(self.xs - 1):
            self.arrived(t).wait_recv()
        total = self.in_x[0].astype(F32)
        for t in range(1, self.xs):
            total = total + self.in_x[t].astype(F32)
        self.fin[self.place.core] = total
        self.half(self.place.core).start()

    def advance(self, slot, last):
        def now(time):
            return slot == jnp.minimum(time, last)

        zs, ys = self.place.zs, self.place.ys
        pl.when(now(0))(self.open)
        pl.when(now(1))(self.fold_cores)
        self.line_ya.send(now, 1)
        self.line_zb.send(now, 1)
        pl.when(now(zs))(self.line_zb.finish)
        self.line_yb.send(now, zs)
        ready = max(zs - 1, ys)
        pl.when(now(ready))(self.line_ya.finish)
        self.line_za.send(now, ready)
        done = max(ready + zs - 1, zs + ys - 1)
        pl.when(now(done))(self.line_yb.finish)
        pl.when(now(done))(self.line_za.finish)
        pl.when(now(done))(self.spread_all)
        pl.when(now(done + 1))(self.fold_x)

    def finish(self, out_ref):
        self.half(1 - self.place.core).wait_recv()
        for c in range(2):
            out_ref[c] = self.fin[c]
        for line in (self.line_ya, self.line_zb, self.line_za, self.line_yb):
            line.drain()
        for z in range(self.place.zs):
            self.swap(z).wait_send()
        for t in range(self.xs - 1):
            self.spread(t).wait_send()
        self.half(self.place.core).wait_send()


def reduce_kernel(parts, grad_ref, band_ref, out_ref, norm_ref, squares, s_n, g_n, *scratch):
    place = Place(parts)
    peers = [(place.dp, lax.rem(place.seq + t, parts)) for t in range(1, parts)]
    reduction = Reduction(place, grad_ref, scratch, peers)

    def always(time):
        return True

    reduction.open()
    reduction.fold_cores()
    reduction.line_ya.send(always, 0)
    reduction.line_zb.send(always, 0)
    reduction.line_zb.finish()
    reduction.line_yb.send(always, 0)
    reduction.line_ya.finish()
    reduction.line_za.send(always, 0)
    reduction.line_yb.finish()
    reduction.line_za.finish()
    reduction.spread_all()
    reduction.fold_x()
    band = band_ref[...]
    partial_sum = jnp.sum(band * band, axis=(0, 1, 2), keepdims=True)[0]
    reduction.finish(out_ref)
    value = out_ref[...]
    partial_sum = partial_sum + jnp.sum(value * value, axis=(0, 1, 2), keepdims=True)[0]
    squares[place.seq] = jnp.broadcast_to(partial_sum, squares.shape[1:])

    def tell(t, there):
        return pltpu.make_async_remote_copy(
            src_ref=squares.at[there],
            dst_ref=squares.at[there],
            send_sem=s_n.at[t],
            recv_sem=g_n.at[there],
            device_id=peers[t],
            device_id_type=MESH,
        )

    for t in range(parts - 1):
        tell(t, place.seq).start()
    for t in range(parts - 1):
        tell(t, lax.rem(place.seq + t + 1, parts)).wait_recv()
    norm = squares[0]
    for p in range(1, parts):
        norm = norm + squares[p]
    norm_ref[...] = norm
    for t in range(parts - 1):
        tell(t, place.seq).wait_send()


def reduce_gradient(grad, band, parts, replicas):
    zs, ys = seq_sides(parts)
    rows, columns = grad.shape[0] // parts, grad.shape[1]
    dma = pltpu.SemaphoreType.DMA
    in_vmem = pl.BlockSpec(memory_space=pltpu.VMEM)
    total, norm = pl.pallas_call(
        partial(reduce_kernel, parts),
        in_specs=[pl.BlockSpec(memory_space=pl.ANY), in_vmem],
        out_specs=[in_vmem, in_vmem],
        out_shape=[
            jax.ShapeDtypeStruct((2, rows, columns // 2), F32),
            jax.ShapeDtypeStruct((8, LANES), F32),
        ],
        scratch_shapes=[pltpu.VMEM((parts, 8, LANES), F32), dma((parts - 1,)), dma((parts,))]
        + reduce_scratch(parts, replicas, rows, columns),
        compiler_params=params(collective_id=2, has_side_effects=True),
        cost_estimate=pl.CostEstimate(flops=0, bytes_accessed=columns * rows * parts * 60, transcendentals=0),
        name="reduce_gradient",
    )(grad.reshape(zs, ys, rows, columns), band)
    return total, norm[0, 0]


def rotary_order(columns):
    lead = columns.shape[:-1]
    split = columns.reshape(lead + (-1, 4, 2, HEAD_DIM // 2))
    return jnp.swapaxes(split, -3, -2).reshape(columns.shape)


def head_order(columns):
    lead = columns.shape[:-1]
    split = columns.reshape(lead + (-1, 2, 4, HEAD_DIM // 2))
    return jnp.swapaxes(split, -3, -2).reshape(columns.shape)


def adam_step(master, gradient, first_old, second_old, learn_rate):
    first_new = BETA_ONE * first_old + (1.0 - BETA_ONE) * gradient
    second_new = BETA_TWO * second_old + (1.0 - BETA_TWO) * gradient * gradient
    first_hat = first_new / (1.0 - BETA_ONE**STEP)
    second_hat = second_new / (1.0 - BETA_TWO**STEP)
    updated = master - learn_rate * (first_hat / (jnp.sqrt(second_hat) + ADAM_EPS) + DECAY * master)
    return (updated, first_new, second_new)


def body(
    activations,
    cotangent,
    lengths,
    weight_in,
    weight_out,
    weight_small,
    first_in,
    first_out,
    first_small,
    second_in,
    second_out,
    second_small,
):
    parts = lax.axis_size("seq")
    micro, unused, band_dev, frames, model = activations.shape
    bands, frame_dev = cotangent.shape[2], cotangent.shape[3]
    turned = 2 * INNER_WIDTH
    width_in, width_out = weight_in.shape[2], weight_out.shape[2]
    width_ff = width_in - 3 * INNER_WIDTH
    small_width = weight_small.shape[2]
    packed = [
        jnp.concatenate(
            [
                rotary_order(weight_in[layer, :, :turned].astype(BF)),
                weight_in[layer, :, turned:].astype(BF),
                weight_out[layer].astype(BF),
                jnp.pad(weight_small[layer].astype(BF), ((0, 0), (0, SMALL_LANES - small_width))),
            ],
            axis=1,
        )
        for layer in range(2)
    ]
    time_weights = gather_weights(packed[0], parts)
    time_tables, band_tables = rotary_tables(frames), rotary_tables(bands)
    frame_base = lax.axis_index("seq") * frame_dev

    def exchange(tensor):
        return lax.all_to_all(tensor, "seq", split_axis=0, concat_axis=0, tiled=True)

    streams, saves, band_weights = [], [], None
    for m in range(micro):
        bias = jnp.where(jnp.arange(frames) < lengths[m], 0.0, MASKED).astype(F32)
        bias = jnp.broadcast_to(bias[:, None], (frames, frames))
        out, saved, gathered = time_forward(
            m, activations, bias, time_weights, time_tables, packed[1] if m == 0 else None, parts, width_ff
        )
        band_weights = gathered if m == 0 else band_weights
        saves.append(saved)
        streams.append(exchange(out).reshape(bands, frame_dev, model))
    backs, before = [], ()
    frame_of = jnp.arange(BLOCK) // bands
    bias = jnp.where(frame_of[:, None] == frame_of[None, :], 0.0, MASKED).astype(F32)
    for m in range(micro):
        info = jnp.concatenate([lengths[m], frame_base[None].astype(jnp.int32)])
        kind = BF if m == micro - 1 else F32
        output, back, grad_band = band_both(
            m, streams[m], cotangent, info, band_weights, band_tables, bias, before, kind, width_ff
        )
        before = (grad_band, output)
        backs.append(exchange(back.reshape(parts, band_dev, frame_dev, model)))
    before = ()
    for m in range(micro):
        kind = BF if m == micro - 1 else F32
        d_input, grad_time, *shard = time_backward(
            m,
            activations,
            backs[m],
            time_weights,
            time_tables,
            saves[m],
            before,
            grad_band if m == 0 else None,
            kind,
            width_ff,
        )
        shard_band = shard[0] if m == 0 else shard_band
        before = (grad_time, d_input)
    shard_time, squares = reduce_gradient(grad_time, shard_band, parts, lax.axis_size("dp"))
    shards = []
    for halves in (shard_time, shard_band):
        shard = jnp.concatenate([halves[0], halves[1]], axis=1)
        shards.append(
            (
                jnp.concatenate([head_order(shard[:, :turned]), shard[:, turned:width_in]], axis=1),
                shard[:, width_in : width_in + width_out],
                shard[:, width_in + width_out : width_in + width_out + small_width],
            )
        )
    shards = tuple(jnp.stack([shards[0][s], shards[1][s]]) for s in range(3))
    grad_norm = jnp.sqrt(squares)
    factor = jnp.minimum(1.0, CLIP_NORM / (grad_norm + 1e-06))
    small_rate = jnp.where(jnp.arange(small_width) < HEAD_COUNT, RATE_GATE, RATE_GAIN)
    new_in = adam_step(weight_in, shards[0] * factor, first_in, second_in, RATE_MATRIX)
    new_out = adam_step(weight_out, shards[1] * factor, first_out, second_out, RATE_MATRIX)
    new_small = adam_step(weight_small, shards[2] * factor, first_small, second_small, small_rate)
    return (
        output,
        d_input,
        grad_norm,
        new_in[0],
        new_out[0],
        new_small[0],
        new_in[1],
        new_out[1],
        new_small[1],
        new_in[2],
        new_out[2],
        new_small[2],
        new_in[0].astype(BF),
        new_out[0].astype(BF),
        new_small[0].astype(BF),
    )


def solution(mesh):
    by_seq = P(None, "seq", None)
    by_band = P(None, "dp", "seq", None, None)
    by_frame = P(None, "dp", None, "seq", None)
    return jax.shard_map(
        body,
        mesh=mesh,
        in_specs=(by_band, by_frame, P(None, "dp")) + (by_seq,) * 9,
        out_specs=(by_frame, by_band, P()) + (by_seq,) * 12,
        check_vma=False,
    )
```

```python
from functools import partial
import math

import jax
import jax.numpy as jnp
from jax import lax
from jax.experimental import pallas as pl
from jax.experimental.pallas import tpu as pltpu
from jax.sharding import PartitionSpec as P

HEAD_COUNT = 8
HEAD_DIM = 64
INNER_WIDTH = 512
STEP = 10
EPS_NORM = 1e-06
BETA_ONE = 0.9
BETA_TWO = 0.999
ADAM_EPS = 1e-08
DECAY = 0.1
RATE_MATRIX = 0.1
RATE_GATE = 0.1
RATE_GAIN = 0.5
CLIP_NORM = 1.0
MASKED = -1e30

BF = jnp.bfloat16
F32 = jnp.float32
GROUP = 256
BLOCK = 256
LANES = 128
SMALL_LANES = 2 * LANES
LOG2E = 1.4426950408889634
SCORE_EXP = LOG2E / math.sqrt(HEAD_DIM)
SQRT_HALF = math.sqrt(0.5)
GAUSS = 1.0 / math.sqrt(2.0 * math.pi)
VMEM_LIMIT = 60 * 2**20


def nn(a, b):
    return lax.dot_general(a, b, (((1,), (0,)), ((), ())), preferred_element_type=F32)


def nt(a, b):
    return lax.dot_general(a, b, (((1,), (1,)), ((), ())), preferred_element_type=F32)


def tn(a, b):
    return lax.dot_general(a, b, (((0,), (0,)), ((), ())), preferred_element_type=F32)


def iota(shape, dim):
    return lax.broadcasted_iota(jnp.int32, shape, dim)


def split_rows(rows):
    high = rows.astype(BF)
    rest = (rows - high.astype(F32)).astype(BF)
    return jnp.concatenate([high, rest], axis=0)


def head_lanes():
    shape = (2 * HEAD_COUNT, INNER_WIDTH)
    return (iota(shape, 1) // HEAD_DIM == iota(shape, 0) % HEAD_COUNT).astype(F32).astype(BF)


def inverse_rms(rows):
    return lax.rsqrt(jnp.mean(rows * rows, axis=-1, keepdims=True) + EPS_NORM)


def norm_back(rows, gain, grad):
    inverse = inverse_rms(rows)
    unit = rows * inverse
    scaled = grad * gain
    d_rows = inverse * (scaled - unit * jnp.mean(scaled * unit, axis=-1, keepdims=True))
    return d_rows, jnp.sum(grad * unit, axis=0, keepdims=True)


def half_lanes(h):
    return (iota((BLOCK, GROUP), 1) % LANES) // (HEAD_DIM // 2) == h


def whole_lanes(h):
    return iota((BLOCK, GROUP), 1) // HEAD_DIM == h


def picked(mask, tensor):
    return jnp.where(mask, tensor, jnp.zeros_like(tensor))


def group_slice(g):
    return slice(g * GROUP, (g + 1) * GROUP)


def forward_block(x, w_ref, small, cos, sin, bias_ref, keep, start, item, width_ff, tick=None):
    gate_weight, gain_attn, gain_ff = small
    size = x.shape[0]
    rows = pl.ds(start, size)
    normed = (x * inverse_rms(x) * gain_attn).astype(BF)
    if "normed" in keep:
        keep["normed"][rows, :] = normed
    gate_rows = jax.nn.sigmoid(nt(gate_weight, normed))
    keep["gate"][:, rows] = gate_rows
    half = GROUP // 2
    for g in range(2):
        for part, name in ((0, "q"), (1, "k")):
            column = part * INNER_WIDTH + g * GROUP
            t = nn(normed, w_ref[:, column : column + GROUP])
            a, b = t[:, :half], t[:, half:]
            keep[name][rows, g * GROUP : g * GROUP + half] = (a * cos - b * sin).astype(BF)
            keep[name][rows, g * GROUP + half : (g + 1) * GROUP] = (b * cos + a * sin).astype(BF)
        column = 2 * INNER_WIDTH + g * GROUP
        keep["v"][rows, group_slice(g)] = nn(normed, w_ref[:, column : column + GROUP]).astype(BF)
    gate = tn(split_rows(gate_rows), head_lanes())
    for n in range(size // BLOCK):
        if tick and n == size // BLOCK - 1:
            tick()
        block = pl.ds(start + n * BLOCK, BLOCK)
        for g in range(2):
            lanes = group_slice(g)
            queries, keys = keep["q"][block, lanes], keep["k"][block, lanes]
            values = keep["v"][block, lanes]
            parts, heads = [], []
            for h in range(4):
                scores = nt(picked(half_lanes(h), keys), queries) + bias_ref[...]
                peak = jnp.max(scores, axis=0, keepdims=True)
                terms = jnp.exp2((scores - peak) * SCORE_EXP)
                probs = (terms * (1.0 / jnp.sum(terms, axis=0, keepdims=True))).astype(BF)
                keep["probs"][item + n, g * 4 + h] = probs
                parts.append(probs)
                heads.append(picked(whole_lanes(h), values))
            attended = tn(jnp.concatenate(parts, axis=0), jnp.concatenate(heads, axis=0))
            keep["gated"][block, lanes] = (attended * gate[n * BLOCK : (n + 1) * BLOCK, lanes]).astype(BF)
    out_start = 3 * INNER_WIDTH + width_ff
    middle = x + nt(keep["gated"][rows, :], w_ref[:, out_start : out_start + INNER_WIDTH])
    keep["middle"][rows, :] = middle
    normed_ff = (middle * inverse_rms(middle) * gain_ff).astype(BF)
    if "normed_ff" in keep:
        keep["normed_ff"][rows, :] = normed_ff
    result = middle
    for c in range(width_ff // GROUP):
        up = 3 * INNER_WIDTH + c * GROUP
        down = out_start + INNER_WIDTH + c * GROUP
        hidden = nn(normed_ff, w_ref[:, up : up + GROUP])
        cumulative = 0.5 + 0.5 * lax.erf(hidden * SQRT_HALF)
        activated = (hidden * cumulative).astype(BF)
        density = jnp.exp2(hidden * hidden * (-0.5 * LOG2E)) * GAUSS
        keep["act"][rows, group_slice(c)] = activated
        keep["slope"][rows, group_slice(c)] = (cumulative + hidden * density).astype(BF)
        result = result + nt(activated, w_ref[:, down : down + GROUP])
    return result


def backward_block(d_out, x, w_ref, small, cos, sin, keep, work, sums, start, item, width_ff, tick=None):
    gate_weight, gain_attn, gain_ff = small
    size = x.shape[0]
    rows = pl.ds(start, size)
    branch = d_out.astype(BF)
    work["branch"][rows, :] = branch
    out_start = 3 * INNER_WIDTH + width_ff
    d_normed_ff = None
    for c in range(width_ff // GROUP):
        up = 3 * INNER_WIDTH + c * GROUP
        down = out_start + INNER_WIDTH + c * GROUP
        d_act = nn(branch, w_ref[:, down : down + GROUP])
        d_hidden = (d_act * keep["slope"][rows, group_slice(c)].astype(F32)).astype(BF)
        work["d_hidden"][rows, group_slice(c)] = d_hidden
    up = 3 * INNER_WIDTH
    d_normed_ff = nt(work["d_hidden"][rows, :], w_ref[:, up : up + width_ff])
    middle = keep["middle"][rows, :]
    d_rows, d_gain_ff = norm_back(middle, gain_ff, d_normed_ff)
    d_middle = d_out + d_rows
    attn_back = d_middle.astype(BF)
    work["attn_back"][rows, :] = attn_back
    gate_rows = keep["gate"][:, rows]
    lanes_of = head_lanes()
    gate = tn(split_rows(gate_rows), lanes_of)
    d_gated = nn(attn_back, w_ref[:, out_start : out_start + INNER_WIDTH])
    product = d_gated * keep["gated"][rows, :].astype(F32)
    high = product.astype(BF)
    rest = (product - high.astype(F32)).astype(BF)
    delta_rows = (nt(lanes_of, high) + nt(lanes_of, rest))[:HEAD_COUNT]
    d_logit = split_rows(delta_rows * (1.0 - gate_rows))
    d_attended = (d_gated * gate).astype(BF)
    half = GROUP // 2
    scale = HEAD_DIM**-0.5
    for n in range(size // BLOCK):
        if tick and n == size // BLOCK - 1:
            tick()
        block = pl.ds(start + n * BLOCK, BLOCK)
        inner = slice(n * BLOCK, (n + 1) * BLOCK)
        for g in range(2):
            lanes = group_slice(g)
            queries, keys = keep["q"][block, lanes], keep["k"][block, lanes]
            values, d_att = keep["v"][block, lanes], d_attended[inner, lanes]
            p_list, s_list, q_list, a_list, k_list = [], [], [], [], []
            for h in range(4):
                halves, wholes = half_lanes(h), whole_lanes(h)
                probs = keep["probs"][item + n, g * 4 + h]
                d_probs = nt(picked(wholes, values), d_att)
                delta = delta_rows[g * 4 + h : g * 4 + h + 1, inner]
                d_scores = (probs.astype(F32) * (d_probs - delta)).astype(BF)
                p_list.append(probs)
                s_list.append(d_scores)
                a_list.append(picked(wholes, d_att))
                q_list.append(picked(halves, queries))
                k_list.append(picked(halves, keys))
            d_values = nn(jnp.concatenate(p_list, axis=1), jnp.concatenate(a_list, axis=0))
            d_keys = nn(jnp.concatenate(s_list, axis=1), jnp.concatenate(q_list, axis=0))
            d_query = tn(jnp.concatenate(s_list, axis=0), jnp.concatenate(k_list, axis=0))
            for column, t in ((0, d_query), (INNER_WIDTH, d_keys)):
                t = t * scale
                a, b = t[:, :half], t[:, half:]
                c, s = cos[inner], sin[inner]
                column = column + g * GROUP
                work["d_proj"][block, column : column + half] = (a * c + b * s).astype(BF)
                work["d_proj"][block, column + half : column + GROUP] = (b * c - a * s).astype(BF)
            column = 2 * INNER_WIDTH + g * GROUP
            work["d_proj"][block, column : column + GROUP] = d_values.astype(BF)
    twice = jnp.concatenate([gate_weight, gate_weight], axis=0)
    d_normed = tn(d_logit, twice)
    for c in range(3 * INNER_WIDTH // INNER_WIDTH):
        part = slice(c * INNER_WIDTH, (c + 1) * INNER_WIDTH)
        d_normed = d_normed + nt(work["d_proj"][rows, part], w_ref[:, part])
    d_rows, d_gain_attn = norm_back(x, gain_attn, d_normed)
    d_gate = nn(d_logit, work["normed"][rows, :])
    sums[0:HEAD_COUNT, :] += d_gate[:HEAD_COUNT] + d_gate[HEAD_COUNT:]
    sums[HEAD_COUNT : HEAD_COUNT + 1, :] += d_gain_attn
    sums[HEAD_COUNT + 1 : HEAD_COUNT + 2, :] += d_gain_ff
    return d_middle + d_rows


def weight_sums(total, work, keep, width_ff):
    out_start = 3 * INNER_WIDTH + width_ff
    pairs = (
        (work["normed"], work["d_proj"], 0),
        (work["normed_ff"], work["d_hidden"], 3 * INNER_WIDTH),
        (work["attn_back"], keep["gated"], out_start),
        (work["branch"], keep["act"], out_start + INNER_WIDTH),
    )
    for left, right, start in pairs:
        turned = left[...].T
        for c in range(right.shape[-1] // INNER_WIDTH):
            part = slice(start + c * INNER_WIDTH, start + (c + 1) * INNER_WIDTH)
            total[:, part] += nn(turned, right[:, c * INNER_WIDTH : (c + 1) * INNER_WIDTH])


def turn_small(w_ref, small_ref):
    width = w_ref.shape[1] - SMALL_LANES
    rows = w_ref[:, width : width + LANES].astype(F32).T
    small_ref[...] = rows[: small_ref.shape[0]]


def small_parts(small_ref):
    gate_weight = small_ref[0:HEAD_COUNT, :].astype(BF)
    return (
        gate_weight,
        small_ref[HEAD_COUNT : HEAD_COUNT + 1, :],
        small_ref[HEAD_COUNT + 1 : HEAD_COUNT + 2, :],
    )


def finish_sums(total, sums, out_ref, arrival):
    width = total.shape[1] - SMALL_LANES
    model = total.shape[0]
    tall = jnp.concatenate([sums[...], jnp.zeros((SMALL_LANES - sums.shape[0], model), F32)], axis=0)
    if out_ref.dtype == F32:
        total[:, width:] = tall.T
        copy = pltpu.make_async_copy(total, out_ref, arrival)
        copy.start()
        copy.wait()
    else:
        out_ref[:, :width] = total[:, :width].astype(out_ref.dtype)
        out_ref[:, width:] = tall.T.astype(out_ref.dtype)


def start_sums(total, sums, before_ref, arrival):
    sums[...] = jnp.zeros_like(sums)
    if before_ref is None:
        total[...] = jnp.zeros_like(total)
    else:
        pltpu.make_async_copy(before_ref, total, arrival).start()


def await_sums(total, sums, before_ref, arrival):
    if before_ref is not None:
        width = total.shape[1] - SMALL_LANES
        pltpu.make_async_copy(before_ref, total, arrival).wait()
        sums[...] += total[:, width:].T[: sums.shape[0]]


SAVED = ("q", "k", "v", "gate", "probs", "gated", "middle", "act", "slope")


def time_forward_kernel(parts, width_ff, ride, x_ref, w_ref, cos_ref, sin_ref, bias_ref, *refs):
    step, steps = pl.program_id(0), pl.num_programs(0)
    if ride:
        shard_ref, out_ref, refs, full_ref = refs[0], refs[1], refs[2:], refs[11]
        gather = Gather(Place(parts), shard_ref, full_ref, *refs[-6:])
        small_ref = refs[-7]
        pl.when(step == 0)(gather.start)
        gather.advance(2 * step, 2 * steps)
    else:
        out_ref, refs = refs[0], refs[1:]
        small_ref = refs[-1]
    keep = dict(zip(SAVED, refs))

    @pl.when(step == 0)
    def _():
        turn_small(w_ref, small_ref)

    per_step, whole_frames, model = x_ref.shape
    x = x_ref[...].astype(F32).reshape(per_step * whole_frames, model)
    out = forward_block(
        x, w_ref, small_parts(small_ref), cos_ref[...], sin_ref[...], bias_ref, keep, 0, 0, width_ff,
        partial(gather.advance, 2 * step + 1, 2 * steps) if ride else None,
    )
    frames = out_ref.shape[2]
    for n in range(per_step):
        out_ref[:, n] = out[n * whole_frames : (n + 1) * whole_frames].reshape(parts, frames, model).astype(BF)
    if ride:
        pl.when(step == steps - 1)(gather.finish)


def time_backward_kernel(parts, width_ff, chained, ride, per_step, *refs):
    x_ref, d_ref, w_ref, cos_ref, sin_ref = refs[:5]
    keep = dict(zip(SAVED, refs[5:14]))
    refs = refs[14:]
    before = refs[0] if chained else None
    refs = refs[2 - ride :] if chained else refs
    step, steps = pl.program_id(0), pl.num_programs(0)
    if ride:
        other_ref, dx_ref, grad_ref, shard_ref = refs[:4]
        reduction = Reduction(Place(parts), other_ref, refs[-REDUCE_SCRATCH:])
        refs = refs[:-REDUCE_SCRATCH]
    else:
        dx_ref, grad_ref = refs[:2]
    total, sums, normed, normed_ff, d_hidden, attn_back, branch, d_proj, arrival, small_ref = refs[-10:]
    work = dict(
        normed=normed, normed_ff=normed_ff, d_hidden=d_hidden, attn_back=attn_back, branch=branch, d_proj=d_proj
    )

    @pl.when(step == 0)
    def _():
        start_sums(total, sums, before, arrival)
        turn_small(w_ref, small_ref)

    small = small_parts(small_ref)
    if ride:
        reduction.advance(2 * step, 2 * steps - 1)
    model = x_ref.shape[2]
    x = x_ref[...].astype(F32).reshape(per_step * BLOCK, model)
    work["normed"][...] = (x * inverse_rms(x) * small[1]).astype(BF)
    middle = keep["middle"][...]
    work["normed_ff"][...] = (middle * inverse_rms(middle) * small[2]).astype(BF)
    d_out = jnp.concatenate([d_ref[:, i].astype(F32).reshape(BLOCK, model) for i in range(per_step)], axis=0)
    d_x = backward_block(
        d_out, x, w_ref, small, cos_ref[...], sin_ref[...], keep, work, sums, 0, 0, width_ff,
        partial(reduction.advance, 2 * step + 1, 2 * steps - 1) if ride else None,
    )
    dx_ref[...] = d_x.reshape(dx_ref.shape)
    if chained:

        @pl.when(step == 0)
        def _():
            await_sums(total, sums, before, arrival)

    weight_sums(total, work, keep, width_ff)

    @pl.when(step == steps - 1)
    def _():
        finish_sums(total, sums, grad_ref, arrival)
        if ride:
            reduction.finish(shard_ref)


def gather_rows(ref, strides, factors):
    return jnp.concatenate(
        [
            jnp.concatenate([ref[p, s, :] * f for p in range(ref.shape[0])], axis=1)
            for s, f in zip(strides, factors)
        ],
        axis=0,
    )


def band_kernel(width_ff, chained, info_ref, *refs):
    x_ref, d_ref, w_ref, cos_ref, sin_ref, bias_ref = refs[:6]
    refs = refs[6:]
    before = refs[0] if chained else None
    out_ref, back_ref, grad_ref = refs[2:5] if chained else refs[:3]
    scratch = refs[-21:]
    keep = dict(zip(SAVED, scratch[:9]))
    total, sums, normed, normed_ff, d_hidden, attn_back, branch, d_proj, arrival, small_ref, rows_a, rows_b = scratch[9:]
    work = dict(
        normed=normed, normed_ff=normed_ff, d_hidden=d_hidden, attn_back=attn_back, branch=branch, d_proj=d_proj
    )
    keep.update(normed=normed, normed_ff=normed_ff)
    step = pl.program_id(0)
    bands, frames, model = x_ref.shape
    pieces = model // LANES

    @pl.when(step == 0)
    def _():
        start_sums(total, sums, before, arrival)
        turn_small(w_ref, small_ref)

    small = small_parts(small_ref)
    for p in range(pieces):
        lanes = slice(p * LANES, (p + 1) * LANES)
        rows_a[p] = x_ref[:, :, lanes].astype(F32).reshape(bands * frames, LANES)
        rows_b[p] = d_ref[:, :, lanes].astype(F32).reshape(bands * frames, LANES)
    first = info_ref[1] + step * frames

    size = cos_ref.shape[0]
    spread = size // bands

    def one(j, carry):
        start = pl.multiple_of(j * size, size)
        item = j * (size // BLOCK)
        strides = [pl.ds(j * spread + f, bands, stride=frames) for f in range(spread)]
        valid = [(first + j * spread + f < info_ref[0]).astype(F32) for f in range(spread)]
        x = gather_rows(rows_a, strides, [1.0] * spread)
        d_out = gather_rows(rows_b, strides, valid)
        out = forward_block(
            x, w_ref, small, cos_ref[...], sin_ref[...], bias_ref, keep, start, item, width_ff
        )
        for f in range(spread):
            for p in range(pieces):
                part = out[f * bands : (f + 1) * bands, p * LANES : (p + 1) * LANES]
                rows_a[p, strides[f], :] = part * valid[f]
        back = backward_block(
            d_out, x, w_ref, small, cos_ref[...], sin_ref[...], keep, work, sums, start, item, width_ff
        )
        for f in range(spread):
            for p in range(pieces):
                part = back[f * bands : (f + 1) * bands, p * LANES : (p + 1) * LANES]
                rows_b[p, strides[f], :] = part
        return carry

    lax.fori_loop(0, bands * frames // size, one, 0)
    for p in range(pieces):
        lanes = slice(p * LANES, (p + 1) * LANES)
        out_ref[:, :, lanes] = rows_a[p].reshape(bands, frames, LANES).astype(BF)
        back_ref[:, :, lanes] = rows_b[p].reshape(bands, frames, LANES).astype(BF)
    if chained:

        @pl.when(step == 0)
        def _():
            await_sums(total, sums, before, arrival)

    weight_sums(total, work, keep, width_ff)

    @pl.when(step == pl.num_programs(0) - 1)
    def _():
        finish_sums(total, sums, grad_ref, arrival)


def whole(shape):
    return pl.BlockSpec(shape, lambda *i: (0,) * len(shape), pipeline_mode=pl.Buffered(1))


def params(**more):
    return pltpu.CompilerParams(vmem_limit_bytes=VMEM_LIMIT, **more)


def rotary_tables(positions, rows):
    half_width = HEAD_DIM // 2
    inverse = 10000.0 ** (-(jnp.arange(half_width, dtype=F32) * 2.0 / HEAD_DIM))
    angles = jnp.arange(positions, dtype=F32)[:, None] * inverse[None, :]
    angles = jnp.tile(angles, (rows // positions, LANES // half_width))
    return (jnp.cos(angles), jnp.sin(angles))


def saved_shapes(tokens, items, model, width_ff):
    return (
        ((tokens, INNER_WIDTH), BF),
        ((tokens, INNER_WIDTH), BF),
        ((tokens, INNER_WIDTH), BF),
        ((HEAD_COUNT, tokens), F32),
        ((items, HEAD_COUNT, BLOCK, BLOCK), BF),
        ((tokens, INNER_WIDTH), BF),
        ((tokens, model), F32),
        ((tokens, width_ff), BF),
        ((tokens, width_ff), BF),
    )


def saved_specs(tokens, items, model, width_ff):
    def place(shape):
        if shape[0] == HEAD_COUNT:
            return pl.BlockSpec(shape, lambda i, *s: (0, i))
        return pl.BlockSpec(shape, lambda i, *s: (i,) + (0,) * (len(shape) - 1))

    return [place(shape) for shape, kind in saved_shapes(tokens, items, model, width_ff)]


def work_shapes(tokens, model, width_ff, columns):
    return [
        pltpu.VMEM((model, columns), F32),
        pltpu.VMEM((2 * HEAD_COUNT, model), F32),
        pltpu.VMEM((tokens, model), BF),
        pltpu.VMEM((tokens, model), BF),
        pltpu.VMEM((tokens, width_ff), BF),
        pltpu.VMEM((tokens, model), BF),
        pltpu.VMEM((tokens, model), BF),
        pltpu.VMEM((tokens, 3 * INNER_WIDTH), BF),
        pltpu.SemaphoreType.DMA,
        pltpu.VMEM((2 * HEAD_COUNT, model), F32),
    ]


def at_micro(m, shape, place):
    return pl.BlockSpec((None, None) + shape, lambda i, *s: (m, 0) + place(i))


def sequences(seqs):
    return 2 if seqs % 2 == 0 else 1


def time_forward(m, x, bias, weights, tables, shard, parts, width_ff):
    seqs, frames, model = x.shape[2:]
    tokens = seqs * frames
    shapes = saved_shapes(tokens, seqs, model, width_ff)
    out = jax.ShapeDtypeStruct((parts, seqs, frames // parts, model), BF)
    ride = shard is not None
    per_step = sequences(seqs)
    any_space = pl.BlockSpec(memory_space=pl.ANY)
    full = [jax.ShapeDtypeStruct((parts,) + shard.shape, BF)] if ride else []
    results = pl.pallas_call(
        partial(time_forward_kernel, parts, width_ff, ride),
        grid=(seqs // per_step,),
        in_specs=[
            at_micro(m, (per_step, frames, model), lambda i: (i, 0, 0)),
            whole(weights.shape),
            whole(tables[0].shape),
            whole(tables[1].shape),
            whole(bias.shape),
        ]
        + [any_space] * ride,
        out_specs=[
            pl.BlockSpec((parts, per_step, frames // parts, model), lambda i: (0, i, 0, 0)),
            *saved_specs(per_step * frames, per_step, model, width_ff),
        ]
        + [any_space] * ride,
        scratch_shapes=[pltpu.VMEM((2 * HEAD_COUNT, model), F32)] + (gather_scratch(parts) if ride else []),
        out_shape=[out, *(jax.ShapeDtypeStruct(s, k) for s, k in shapes)] + full,
        compiler_params=params(collective_id=3, has_side_effects=True) if ride else params(),
        cost_estimate=pl.CostEstimate(
            flops=int(tokens * 5e6), bytes_accessed=tokens * 15000, transcendentals=tokens * 5000
        ),
        name="time_forward_gather" if ride else "time_forward",
    )(x, weights, *tables, bias, *([shard] if ride else []))
    saved = results[1 : 1 + len(SAVED)]
    return results[0], saved, (results[-1].reshape(-1, shard.shape[1]) if ride else None)


def time_backward(m, x, d_out, weights, tables, saved, before, other, kind, width_ff):
    seqs, frames, model = x.shape[2:]
    tokens = seqs * frames
    parts, unused, part_frames, unused_model = d_out.shape
    per_step = sequences(seqs)
    columns = weights.shape[1]
    ride = other is not None
    if ride:
        before = before[:1]
    ins = [x, d_out, weights, *tables, *saved, *before]
    aliases = {len(ins) - 1: 0} if len(before) == 2 else {}
    target = (1, 1) + x.shape[2:] if ride else x.shape
    more_specs, more_shapes, scratch = [], [], []
    any_space = pl.BlockSpec(memory_space=pl.ANY)
    if ride:
        zs, ys = seq_sides(parts)
        part = model // parts
        ins.append(other.reshape(zs, ys, part, columns))
        more_shapes = [jax.ShapeDtypeStruct((2, part, columns // 2), F32)]
        more_specs = [whole(more_shapes[0].shape)]
        scratch = reduce_scratch(parts, lax.axis_size("dp"), part, columns)
    rows = at_micro(m, (per_step, frames, model), lambda i: (i, 0, 0))
    return pl.pallas_call(
        partial(time_backward_kernel, parts, width_ff, bool(before), ride, per_step),
        grid=(seqs // per_step,),
        in_specs=[
            rows,
            pl.BlockSpec((parts, per_step, part_frames, model), lambda i: (0, i, 0, 0)),
            whole(weights.shape),
            whole(tables[0].shape),
            whole(tables[1].shape),
            *saved_specs(per_step * frames, per_step, model, width_ff),
        ]
        + [any_space] * (len(before) + ride),
        out_specs=[
            at_micro(0 if ride else m, (per_step, frames, model), lambda i: (i, 0, 0)),
            any_space if kind == F32 else whole((model, columns)),
        ]
        + more_specs,
        out_shape=[
            jax.ShapeDtypeStruct(target, F32),
            jax.ShapeDtypeStruct((model, columns), kind),
        ]
        + more_shapes,
        input_output_aliases=aliases,
        scratch_shapes=work_shapes(per_step * frames, model, width_ff, columns) + scratch,
        compiler_params=params(collective_id=4, has_side_effects=True) if ride else params(),
        cost_estimate=pl.CostEstimate(
            flops=int(tokens * 9e6), bytes_accessed=tokens * 18000, transcendentals=0
        ),
        name="time_backward_reduce" if ride else "time_backward",
    )(*ins)


def band_both(m, x, d_out, info, weights, tables, bias, before, kind, width_ff):
    bands, frames, model = x.shape
    tokens = bands * frames
    chunk = math.gcd(frames, 16)
    step_tokens = bands * chunk
    columns = weights.shape[1]
    ins = [info, x, d_out, weights, *tables, bias, *before]
    rows = pl.BlockSpec((bands, chunk, model), lambda i, s: (0, i, 0))
    rows_m = at_micro(m, (bands, chunk, model), lambda i: (0, i, 0))
    any_space = pl.BlockSpec(memory_space=pl.ANY)
    saved = [
        pltpu.VMEM(s, k) for s, k in saved_shapes(step_tokens, step_tokens // BLOCK, model, width_ff)
    ]
    return pl.pallas_call(
        partial(band_kernel, width_ff, bool(before)),
        grid_spec=pltpu.PrefetchScalarGridSpec(
            num_scalar_prefetch=1,
            grid=(frames // chunk,),
            in_specs=[
                rows,
                rows_m,
                whole(weights.shape),
                whole(tables[0].shape),
                whole(tables[1].shape),
                whole(bias.shape),
            ]
            + [any_space] * len(before),
            out_specs=[rows_m, rows, any_space if kind == F32 else whole((model, columns))],
            scratch_shapes=saved
            + work_shapes(step_tokens, model, width_ff, columns)
            + [pltpu.VMEM((model // LANES, step_tokens, LANES), F32)] * 2,
        ),
        out_shape=[
            jax.ShapeDtypeStruct(d_out.shape, BF),
            jax.ShapeDtypeStruct(x.shape, BF),
            jax.ShapeDtypeStruct((model, columns), kind),
        ],
        input_output_aliases={len(ins) - 1: 0} if before else {},
        compiler_params=params(),
        cost_estimate=pl.CostEstimate(
            flops=int(tokens * 14e6), bytes_accessed=tokens * 8000, transcendentals=tokens * 5000
        ),
        name="band_both",
    )(*ins)


MESH = pl.DeviceIdType.MESH


def seq_sides(parts):
    side = 1
    while 4 * side * side <= parts:
        side *= 2
    return parts // side, side


class Place:
    def __init__(self, parts):
        self.dp, self.seq = lax.axis_index("dp"), lax.axis_index("seq")
        self.core = self.dp % 2
        self.zs, self.ys = seq_sides(parts)
        self.z, self.y = self.seq // self.ys, self.seq % self.ys

    def sibling(self):
        return (self.dp + 1 - 2 * self.core, self.seq)

    def along_z(self, step):
        return (self.dp, self.seq + step * self.ys)

    def along_y(self, step):
        return (self.dp, self.seq + step)

    def has_z(self, step):
        return self.z + step < self.zs if step > 0 else self.z + step >= 0

    def has_y(self, step):
        return self.y + step < self.ys if step > 0 else self.y + step >= 0


def greet(place, others=()):
    barrier = pltpu.get_barrier_semaphore()
    pl.semaphore_signal(barrier, inc=1, device_id=place.sibling(), device_id_type=MESH)
    for other in others:
        pl.semaphore_signal(barrier, inc=1, device_id=other, device_id_type=MESH)
    for step in (1, -1):
        for has, to in ((place.has_z, place.along_z), (place.has_y, place.along_y)):

            @pl.when(has(step))
            def _(to=to, step=step):
                pl.semaphore_signal(barrier, inc=1, device_id=to(step), device_id_type=MESH)

    count = 1 + len(others)
    for has in (place.has_z, place.has_y):
        count = count + has(1).astype(jnp.int32) + has(-1).astype(jnp.int32)
    pl.semaphore_wait(barrier, count)


class Gather:
    def __init__(self, place, shard_ref, out_ref, send_z, send_y, send_c, got, got_c, local):
        self.place, self.shard, self.out = place, shard_ref, out_ref
        self.send_z, self.send_y, self.send_c, self.got, self.got_c, self.local = send_z, send_y, send_c, got, got_c, local
        wide = shard_ref.shape[1] // 2
        self.lanes = pl.ds(pl.multiple_of(place.core * wide, LANES), wide)
        self.other_lanes = pl.ds(pl.multiple_of((1 - place.core) * wide, LANES), wide)
        self.mine = shard_ref.at[:, self.lanes]
        self.hops = place.zs

    def index(self, z, y):
        return z * self.place.ys + y

    def held(self, p):
        return self.out.at[p, :, self.lanes]

    def push(self, source, p, to, send, receive):
        return pltpu.make_async_remote_copy(
            src_ref=source, dst_ref=self.held(p), send_sem=send, recv_sem=receive, device_id=to, device_id_type=MESH
        )

    def to_sibling(self, p):
        return self.push(self.held(p), p, self.place.sibling(), self.send_c.at[p], self.got_c.at[p])

    def from_sibling(self, p):
        there = self.out.at[p, :, self.other_lanes]
        return pltpu.make_async_remote_copy(
            src_ref=there,
            dst_ref=there,
            send_sem=self.send_c.at[p],
            recv_sem=self.got_c.at[p],
            device_id=self.place.sibling(),
            device_id_type=MESH,
        )

    def along_z(self, source, p, step, t):
        return self.push(source, p, self.place.along_z(step), self.send_z.at[(step + 1) // 2, t], self.got.at[p])

    def along_y(self, source, p, step):
        return self.push(source, p, self.place.along_y(step), self.send_y.at[(step + 1) // 2, p], self.got.at[p])

    def await_block(self, p):
        self.push(self.held(p), p, self.place.sibling(), self.send_c.at[p], self.got.at[p]).wait_recv()

    def own(self):
        return pltpu.make_async_copy(self.shard, self.out.at[self.place.seq], self.local)

    def start(self):
        place = self.place
        greet(place)
        self.own().start()
        for step in (1, -1):
            pl.when(place.has_z(step))(lambda step=step: self.along_z(self.mine, place.seq, step, 0).start())
            pl.when(place.has_y(step))(lambda step=step: self.along_y(self.mine, place.seq, step).start())

    def advance(self, slot, slots):
        for hop in range(1, self.hops + 1):
            due = (hop * (slots - 1) + self.hops - 1) // self.hops
            pl.when(slot == due)(partial(self.hop, hop))

    def hop(self, t):
        if t == self.place.zs:
            return self.other_lines()
        place = self.place
        for step in (1, -1):
            z = place.z - step * t
            here = (z >= 0) if step > 0 else (z < place.zs)

            @pl.when(here)
            def _(step=step, z=z):
                p = self.index(z, place.y)
                self.await_block(p)
                if t < place.zs - 1:
                    pl.when(place.has_z(step))(lambda: self.along_z(self.held(p), p, step, t).start())
                for side in (1, -1):
                    pl.when(place.has_y(side))(lambda side=side: self.along_y(self.held(p), p, side).start())
                self.to_sibling(p).start()

    def other_lines(self):
        place = self.place
        for t in range(1, place.ys):
            for step in (1, -1):
                y = place.y - step * t
                here = (y >= 0) if step > 0 else (y < place.ys)

                @pl.when(here)
                def _(t=t, step=step, y=y):
                    for turn in range(place.zs):
                        p = self.index(lax.rem(place.z + turn, place.zs), y)
                        self.await_block(p)
                        if t < place.ys - 1:
                            pl.when(place.has_y(step))(lambda p=p: self.along_y(self.held(p), p, step).start())
                        self.to_sibling(p).start()

    def finish(self):
        place = self.place
        self.own().wait()
        for turn in range(1, place.zs * place.ys):
            p = lax.rem(place.seq + turn, place.zs * place.ys)
            self.to_sibling(p).wait_send()
            self.from_sibling(p).wait_recv()
        for step in (1, -1):
            for t in range(place.zs - 1):
                z = place.z - step * t
                sent = jnp.logical_and((z >= 0) if step > 0 else (z < place.zs), place.has_z(step))
                pl.when(sent)(lambda step=step, t=t: self.along_z(self.mine, place.seq, step, t).wait_send())
            for t in range(place.ys - 1):
                y = place.y - step * t
                sent = jnp.logical_and((y >= 0) if step > 0 else (y < place.ys), place.has_y(step))

                @pl.when(sent)
                def _(step=step, y=y):
                    for z in range(place.zs):
                        self.along_y(self.mine, self.index(z, y), step).wait_send()


def gather_kernel(parts, shard_ref, out_ref, *sems):
    gather = Gather(Place(parts), shard_ref, out_ref, *sems)
    gather.start()
    for hop in range(1, gather.hops + 1):
        gather.hop(hop)
    gather.finish()


def gather_scratch(parts):
    zs, ys = seq_sides(parts)
    dma = pltpu.SemaphoreType.DMA
    return [dma((2, zs)), dma((2, parts)), dma((parts,)), dma((parts,)), dma((parts,)), dma]


def gather_weights(shard, parts):
    rows, columns = shard.shape
    out = pl.pallas_call(
        partial(gather_kernel, parts),
        in_specs=[pl.BlockSpec(memory_space=pl.ANY)],
        out_specs=pl.BlockSpec(memory_space=pl.ANY),
        out_shape=jax.ShapeDtypeStruct((parts, rows, columns), shard.dtype),
        scratch_shapes=gather_scratch(parts),
        compiler_params=params(collective_id=1, has_side_effects=True),
        cost_estimate=pl.CostEstimate(flops=0, bytes_accessed=parts * rows * columns * 40, transcendentals=0),
        name="gather_weights",
    )(shard)
    return out.reshape(parts * rows, columns)


def add_into(acc, other):
    acc[...] = (acc[...].astype(F32) + other[...].astype(F32)).astype(acc.dtype)


class Line:
    def __init__(self, i, n, to, acc, slot, count, sends, receives):
        self.i, self.n, self.to, self.acc, self.slot, self.count = i, n, to, acc, slot, count
        self.sends, self.receives = sends, receives

    def copy(self, side, j, k):
        return pltpu.make_async_remote_copy(
            src_ref=self.acc(j, k),
            dst_ref=self.slot(side, j, k),
            send_sem=self.sends.at[side, j, k],
            recv_sem=self.receives.at[side, j, k],
            device_id=self.to(1 - 2 * side),
            device_id_type=MESH,
        )

    def take(self, side, j, k):
        self.copy(side, j, k).wait_recv()
        add_into(self.acc(j, k), self.slot(side, j, k))

    def send(self, now, base):
        for t in range(self.n - 1):
            for side, j, passed in ((0, self.n - 1 - t, self.i), (1, t, self.n - 1 - self.i)):
                beyond = self.i < j if side == 0 else self.i > j
                inner = self.i > 0 if side == 0 else self.i < self.n - 1

                @pl.when(jnp.logical_and(beyond, now(base + passed + t)))
                def _(side=side, j=j, inner=inner):
                    for k in range(self.count):
                        if self.n > 2:
                            pl.when(inner)(lambda k=k: self.take(side, j, k))
                        self.copy(side, j, k).start()

    def finish(self):
        for side, inner in ((0, self.i > 0), (1, self.i < self.n - 1)):

            @pl.when(inner)
            def _(side=side):
                for k in range(self.count):
                    self.take(side, self.i, k)

    def drain(self):
        for j in range(self.n):
            for side, beyond in ((0, self.i < j), (1, self.i > j)):

                @pl.when(beyond)
                def _(side=side, j=j):
                    for k in range(self.count):
                        self.copy(side, j, k).wait_send()


REDUCE_SCRATCH = 23


def reduce_scratch(parts, replicas, rows, columns):
    zs, ys = seq_sides(parts)
    wide = columns // 2
    first = (wide // LANES + 1) // 2 * LANES
    rest = wide - first
    xs = replicas // 2
    dma = pltpu.SemaphoreType.DMA
    return [
        pltpu.VMEM((zs, ys, rows, wide), BF),
        pltpu.VMEM((zs, ys, rows, wide), BF),
        pltpu.VMEM((2, ys, zs, rows, first), BF),
        pltpu.VMEM((2, zs, ys, rows, rest), BF),
        pltpu.VMEM((2, zs, 1, rows, first), BF),
        pltpu.VMEM((2, ys, 1, rows, rest), BF),
        pltpu.VMEM((xs, rows, wide), BF),
        pltpu.VMEM((2, rows, wide), F32),
        dma((zs,)),
        dma((zs,)),
        dma((zs,)),
        dma((2, ys, zs)),
        dma((2, ys, zs)),
        dma((2, zs, ys)),
        dma((2, zs, ys)),
        dma((2, zs, 1)),
        dma((2, zs, 1)),
        dma((2, ys, 1)),
        dma((2, ys, 1)),
        dma((max(xs - 1, 1),)),
        dma((xs,)),
        dma,
        dma,
    ]


class Reduction:
    def __init__(self, place, grad_ref, scratch, others=()):
        self.place, self.grad, self.others = place, grad_ref, list(others)
        self.acc, self.in_c, in_ya, in_zb, in_za, in_yb, self.in_x, self.fin = scratch[:8]
        self.local, self.s_c, self.g_c, s_ya, g_ya, s_zb, g_zb, s_za, g_za, s_yb, g_yb = scratch[8:19]
        self.s_x, self.g_x, self.s_f, self.g_f = scratch[19:]
        acc = self.acc
        zs, ys = place.zs, place.ys
        self.xs = self.in_x.shape[0]
        self.x = place.dp // 2
        wide = acc.shape[-1]
        first = (wide // LANES + 1) // 2 * LANES
        a, b = pl.ds(0, first), pl.ds(first, wide - first)
        self.lanes = pl.ds(pl.multiple_of(place.core * wide, LANES), wide)
        self.other = pl.ds(pl.multiple_of((1 - place.core) * wide, LANES), wide)
        self.x_peers = [(lax.rem(self.x + t, self.xs) * 2 + place.core, place.seq) for t in range(1, self.xs)]
        self.line_ya = Line(
            place.y, ys, place.along_y, lambda j, k: acc.at[k, j, :, a], lambda s, j, k: in_ya.at[s, j, k], zs, s_ya, g_ya
        )
        self.line_zb = Line(
            place.z, zs, place.along_z, lambda j, k: acc.at[j, k, :, b], lambda s, j, k: in_zb.at[s, j, k], ys, s_zb, g_zb
        )
        self.line_za = Line(
            place.z, zs, place.along_z, lambda j, k: acc.at[j, place.y, :, a], lambda s, j, k: in_za.at[s, j, k], 1, s_za, g_za
        )
        self.line_yb = Line(
            place.y, ys, place.along_y, lambda j, k: acc.at[place.z, j, :, b], lambda s, j, k: in_yb.at[s, j, k], 1, s_yb, g_yb
        )
        self.own = acc.at[place.z, place.y]

    def mine(self, z):
        return pltpu.make_async_copy(self.grad.at[z, :, :, self.lanes], self.acc.at[z], self.local.at[z])

    def swap(self, z):
        return pltpu.make_async_remote_copy(
            src_ref=self.grad.at[z, :, :, self.other],
            dst_ref=self.in_c.at[z],
            send_sem=self.s_c.at[z],
            recv_sem=self.g_c.at[z],
            device_id=self.place.sibling(),
            device_id_type=MESH,
        )

    def spread(self, t):
        return pltpu.make_async_remote_copy(
            src_ref=self.own,
            dst_ref=self.in_x.at[self.x],
            send_sem=self.s_x.at[t],
            recv_sem=self.g_x.at[self.x],
            device_id=self.x_peers[t],
            device_id_type=MESH,
        )

    def arrived(self, t):
        there = lax.rem(self.x + t + 1, self.xs)
        return pltpu.make_async_remote_copy(
            src_ref=self.own,
            dst_ref=self.in_x.at[there],
            send_sem=self.s_x.at[t],
            recv_sem=self.g_x.at[there],
            device_id=self.x_peers[t],
            device_id_type=MESH,
        )

    def half(self, c):
        return pltpu.make_async_remote_copy(
            src_ref=self.fin.at[c],
            dst_ref=self.fin.at[c],
            send_sem=self.s_f,
            recv_sem=self.g_f,
            device_id=self.place.sibling(),
            device_id_type=MESH,
        )

    def greet(self):
        place = self.place
        barrier = pltpu.get_barrier_semaphore()
        lines = [] if self.others else [(place.has_z, place.along_z), (place.has_y, place.along_y)]
        count = 0
        for to in [place.sibling()] + self.x_peers + self.others:
            pl.semaphore_signal(barrier, inc=1, device_id=to, device_id_type=MESH)
            count = count + 1
        for has, to in lines:
            for step in (1, -1):
                pl.when(has(step))(
                    lambda to=to, step=step: pl.semaphore_signal(
                        barrier, inc=1, device_id=to(step), device_id_type=MESH
                    )
                )
                count = count + has(step).astype(jnp.int32)
        pl.semaphore_wait(barrier, count)

    def open(self):
        for z in range(self.place.zs):
            self.mine(z).start()
        self.greet()
        for z in range(self.place.zs):
            self.swap(z).start()

    def fold_cores(self):
        for z in range(self.place.zs):
            self.mine(z).wait()
            self.swap(z).wait_recv()
            for y in range(self.place.ys):
                add_into(self.acc.at[z, y], self.in_c.at[z, y])

    def spread_all(self):
        for t in range(self.xs - 1):
            self.spread(t).start()

    def fold_x(self):
        self.in_x[self.x] = self.own[...]
        for t in range(self.xs - 1):
            self.arrived(t).wait_recv()
        total = self.in_x[0].astype(F32)
        for t in range(1, self.xs):
            total = total + self.in_x[t].astype(F32)
        self.fin[self.place.core] = total
        self.half(self.place.core).start()

    def advance(self, slot, last):
        def now(time):
            return slot == jnp.minimum(time, last)

        zs, ys = self.place.zs, self.place.ys
        pl.when(now(0))(self.open)
        pl.when(now(1))(self.fold_cores)
        self.line_ya.send(now, 1)
        self.line_zb.send(now, 1)
        pl.when(now(zs))(self.line_zb.finish)
        self.line_yb.send(now, zs)
        ready = max(zs - 1, ys)
        pl.when(now(ready))(self.line_ya.finish)
        self.line_za.send(now, ready)
        done = max(ready + zs - 1, zs + ys - 1)
        pl.when(now(done))(self.line_yb.finish)
        pl.when(now(done))(self.line_za.finish)
        pl.when(now(done))(self.spread_all)
        pl.when(now(done + 1))(self.fold_x)

    def finish(self, out_ref):
        self.half(1 - self.place.core).wait_recv()
        for c in range(2):
            out_ref[c] = self.fin[c]
        for line in (self.line_ya, self.line_zb, self.line_za, self.line_yb):
            line.drain()
        for z in range(self.place.zs):
            self.swap(z).wait_send()
        for t in range(self.xs - 1):
            self.spread(t).wait_send()
        self.half(self.place.core).wait_send()


def reduce_kernel(parts, grad_ref, band_ref, out_ref, norm_ref, squares, s_n, g_n, *scratch):
    place = Place(parts)
    peers = [(place.dp, lax.rem(place.seq + t, parts)) for t in range(1, parts)]
    reduction = Reduction(place, grad_ref, scratch, peers)

    def always(time):
        return True

    reduction.open()
    reduction.fold_cores()
    reduction.line_ya.send(always, 0)
    reduction.line_zb.send(always, 0)
    reduction.line_zb.finish()
    reduction.line_yb.send(always, 0)
    reduction.line_ya.finish()
    reduction.line_za.send(always, 0)
    reduction.line_yb.finish()
    reduction.line_za.finish()
    reduction.spread_all()
    reduction.fold_x()
    band = band_ref[...]
    partial_sum = jnp.sum(band * band, axis=(0, 1, 2), keepdims=True)[0]
    reduction.finish(out_ref.at[0])
    out_ref[1] = band_ref[...]
    value = out_ref[0]
    partial_sum = partial_sum + jnp.sum(value * value, axis=(0, 1, 2), keepdims=True)[0]
    squares[place.seq] = jnp.broadcast_to(partial_sum, squares.shape[1:])

    def tell(t, there):
        return pltpu.make_async_remote_copy(
            src_ref=squares.at[there],
            dst_ref=squares.at[there],
            send_sem=s_n.at[t],
            recv_sem=g_n.at[there],
            device_id=peers[t],
            device_id_type=MESH,
        )

    for t in range(parts - 1):
        tell(t, place.seq).start()
    for t in range(parts - 1):
        tell(t, lax.rem(place.seq + t + 1, parts)).wait_recv()
    norm = squares[0]
    for p in range(1, parts):
        norm = norm + squares[p]
    norm_ref[...] = norm
    for t in range(parts - 1):
        tell(t, place.seq).wait_send()


def reduce_gradient(grad, band, parts, replicas):
    zs, ys = seq_sides(parts)
    rows, columns = grad.shape[0] // parts, grad.shape[1]
    dma = pltpu.SemaphoreType.DMA
    in_vmem = pl.BlockSpec(memory_space=pltpu.VMEM)
    total, norm = pl.pallas_call(
        partial(reduce_kernel, parts),
        in_specs=[pl.BlockSpec(memory_space=pl.ANY), in_vmem],
        out_specs=[in_vmem, in_vmem],
        out_shape=[
            jax.ShapeDtypeStruct((2, 2, rows, columns // 2), F32),
            jax.ShapeDtypeStruct((8, LANES), F32),
        ],
        scratch_shapes=[pltpu.VMEM((parts, 8, LANES), F32), dma((parts - 1,)), dma((parts,))]
        + reduce_scratch(parts, replicas, rows, columns),
        compiler_params=params(collective_id=2, has_side_effects=True),
        cost_estimate=pl.CostEstimate(flops=0, bytes_accessed=columns * rows * parts * 60, transcendentals=0),
        name="reduce_gradient",
    )(grad.reshape(zs, ys, rows, columns), band)
    return total, norm


def rotary_order(columns):
    lead = columns.shape[:-1]
    split = columns.reshape(lead + (-1, 4, 2, HEAD_DIM // 2))
    return jnp.swapaxes(split, -3, -2).reshape(columns.shape)


def adam_step(master, gradient, first_old, second_old, learn_rate):
    first_new = BETA_ONE * first_old + (1.0 - BETA_ONE) * gradient
    second_new = BETA_TWO * second_old + (1.0 - BETA_TWO) * gradient * gradient
    first_hat = first_new / (1.0 - BETA_ONE**STEP)
    second_hat = second_new / (1.0 - BETA_TWO**STEP)
    updated = master - learn_rate * (first_hat / (jnp.sqrt(second_hat) + ADAM_EPS) + DECAY * master)
    return (updated, first_new, second_new)


def heads_in_order(first, second):
    half = HEAD_DIM // 2
    lane = iota(first.shape, 1) // half

    def turn(t, places):
        return pltpu.roll(t, places % LANES, 1) if places % LANES else t

    results = []
    for low in (0, 2):
        pieces = [turn(first, -low * half), turn(second, half - low * half)]
        pieces += [turn(first, half - low * half), turn(second, 2 * half - low * half)]
        out = pieces[0]
        for place in range(1, 4):
            out = jnp.where(lane == place, pieces[place], out)
        results.append(out)
    return results


def update_kernel(grads_ref, squares_ref, *refs):
    masters, firsts, seconds = refs[0:2], refs[2:4], refs[4:6]
    outs = refs[6:]
    norm = jnp.sqrt(squares_ref[0:1, 0:1])
    factor = jnp.minimum(1.0, CLIP_NORM / (norm + 1e-06))
    half = grads_ref.shape[2]
    width_in, width_out = (ref.shape[1] for ref in masters)

    def gradient(start, size):
        return grads_ref[start // half, :, start % half : start % half + size] * factor

    def update(which, column, size, grad, rate):
        part = slice(column, column + size)
        new = adam_step(
            masters[which][:, part], grad, firsts[which][:, part], seconds[which][:, part], rate
        )
        for k in range(3):
            outs[2 * k + which][:, part] = new[k]
        outs[6 + which][:, part] = new[0].astype(BF)

    for start in range(0, 2 * INNER_WIDTH, GROUP):
        pair = heads_in_order(gradient(start, LANES), gradient(start + LANES, LANES))
        for n in range(2):
            update(0, start + n * LANES, LANES, pair[n], RATE_MATRIX)
    for which, width, base, begin in ((0, width_in, 0, 2 * INNER_WIDTH), (1, width_out, width_in, 0)):
        for column in range(begin, width, LANES):
            update(which, column, LANES, gradient(base + column, LANES), RATE_MATRIX)


def update_weights(grads, squares, masters, firsts, seconds):
    states = [*masters, *firsts, *seconds]

    def by_layer(t):
        return pl.BlockSpec((None,) + t.shape[1:], lambda i: (i, 0, 0))

    return pl.pallas_call(
        update_kernel,
        grid=(2,),
        in_specs=[pl.BlockSpec((None,) + grads.shape[1:], lambda i: (i, 0, 0, 0)), whole(squares.shape)]
        + [by_layer(t) for t in states],
        out_specs=[by_layer(t) for t in states + list(masters)],
        out_shape=[jax.ShapeDtypeStruct(t.shape, F32) for t in states]
        + [jax.ShapeDtypeStruct(t.shape, BF) for t in masters],
        compiler_params=params(),
        name="update_weights",
    )(grads, squares, *states)


def body(
    activations,
    cotangent,
    lengths,
    weight_in,
    weight_out,
    weight_small,
    first_in,
    first_out,
    first_small,
    second_in,
    second_out,
    second_small,
):
    parts = lax.axis_size("seq")
    micro, unused, band_dev, frames, model = activations.shape
    bands, frame_dev = cotangent.shape[2], cotangent.shape[3]
    turned = 2 * INNER_WIDTH
    width_in, width_out = weight_in.shape[2], weight_out.shape[2]
    width_ff = width_in - 3 * INNER_WIDTH
    small_width = weight_small.shape[2]
    packed = [
        jnp.concatenate(
            [
                rotary_order(weight_in[layer, :, :turned].astype(BF)),
                weight_in[layer, :, turned:].astype(BF),
                weight_out[layer].astype(BF),
                jnp.pad(weight_small[layer].astype(BF), ((0, 0), (0, SMALL_LANES - small_width))),
            ],
            axis=1,
        )
        for layer in range(2)
    ]
    time_weights = gather_weights(packed[0], parts)
    time_tables = rotary_tables(frames, sequences(band_dev) * frames)
    band_tables = rotary_tables(bands, min(2 * BLOCK, frame_dev * bands))
    frame_base = lax.axis_index("seq") * frame_dev

    def exchange(tensor):
        return lax.all_to_all(tensor, "seq", split_axis=0, concat_axis=0, tiled=True)

    streams, saves, band_weights = [], [], None
    for m in range(micro):
        bias = jnp.where(jnp.arange(frames) < lengths[m], 0.0, MASKED).astype(F32)
        bias = jnp.broadcast_to(bias[:, None], (frames, frames))
        out, saved, gathered = time_forward(
            m, activations, bias, time_weights, time_tables, packed[1] if m == 0 else None, parts, width_ff
        )
        band_weights = gathered if m == 0 else band_weights
        saves.append(saved)
        streams.append(exchange(out).reshape(bands, frame_dev, model))
    backs, before = [], ()
    frame_of = jnp.arange(BLOCK) // bands
    bias = jnp.where(frame_of[:, None] == frame_of[None, :], 0.0, MASKED).astype(F32)
    for m in range(micro):
        info = jnp.concatenate([lengths[m], frame_base[None].astype(jnp.int32)])
        kind = BF if m == micro - 1 else F32
        output, back, grad_band = band_both(
            m, streams[m], cotangent, info, band_weights, band_tables, bias, before, kind, width_ff
        )
        before = (grad_band, output)
        backs.append(exchange(back.reshape(parts, band_dev, frame_dev, model)))
    before = ()
    for m in range(micro):
        kind = BF if m == micro - 1 else F32
        part, grad_time, *shard = time_backward(
            m,
            activations,
            backs[m],
            time_weights,
            time_tables,
            saves[m],
            before,
            grad_band if m == micro - 1 else None,
            kind,
            width_ff,
        )
        if m < micro - 1:
            d_input = part
            before = (grad_time, d_input)
        else:
            d_input = lax.dynamic_update_slice(d_input, part, (m, 0, 0, 0, 0))
    grads, squares = reduce_gradient(grad_time, shard[0], parts, lax.axis_size("dp"))
    new = update_weights(grads, squares, (weight_in, weight_out), (first_in, first_out), (second_in, second_out))
    norm = jnp.sqrt(squares[0, 0])
    factor = jnp.minimum(1.0, CLIP_NORM / (norm + 1e-06))
    start = width_in + width_out - grads.shape[3]
    rate = jnp.where(jnp.arange(small_width) < HEAD_COUNT, RATE_GATE, RATE_GAIN)
    small = adam_step(
        weight_small, grads[:, 1, :, start : start + small_width] * factor, first_small, second_small, rate
    )
    return (
        output,
        d_input,
        norm,
        new[0],
        new[1],
        small[0],
        new[2],
        new[3],
        small[1],
        new[4],
        new[5],
        small[2],
        new[6],
        new[7],
        small[0].astype(BF),
    )


def solution(mesh):
    by_seq = P(None, "seq", None)
    by_band = P(None, "dp", "seq", None, None)
    by_frame = P(None, "dp", None, "seq", None)
    return jax.shard_map(
        body,
        mesh=mesh,
        in_specs=(by_band, by_frame, P(None, "dp")) + (by_seq,) * 9,
        out_specs=(by_frame, by_band, P()) + (by_seq,) * 12,
        check_vma=False,
    )
```

```python
from functools import partial
import math

import jax
import jax.numpy as jnp
import numpy as np
from jax import lax
from jax.experimental import pallas as pl
from jax.experimental.pallas import tpu as pltpu
from jax.sharding import PartitionSpec as P

HEAD_COUNT = 8
HEAD_DIM = 64
INNER_WIDTH = 512
STEP = 10
EPS_NORM = 1e-06
BETA_ONE = 0.9
BETA_TWO = 0.999
ADAM_EPS = 1e-08
DECAY = 0.1
RATE_MATRIX = 0.1
RATE_GATE = 0.1
RATE_GAIN = 0.5
CLIP_NORM = 1.0
MASKED = -1e30

BF = jnp.bfloat16
F32 = jnp.float32
GROUP = 256
BLOCK = 256
LANES = 128
SMALL_LANES = 2 * LANES
LOG2E = 1.4426950408889634
SCORE_EXP = LOG2E / math.sqrt(HEAD_DIM)
SQRT_HALF = math.sqrt(0.5)
GAUSS = 1.0 / math.sqrt(2.0 * math.pi)
VMEM_LIMIT = 60 * 2**20


def nn(a, b):
    return lax.dot_general(a, b, (((1,), (0,)), ((), ())), preferred_element_type=F32)


def nt(a, b):
    return lax.dot_general(a, b, (((1,), (1,)), ((), ())), preferred_element_type=F32)


def tn(a, b):
    return lax.dot_general(a, b, (((0,), (0,)), ((), ())), preferred_element_type=F32)


def iota(shape, dim):
    return lax.broadcasted_iota(jnp.int32, shape, dim)


def split_rows(rows):
    high = rows.astype(BF)
    rest = (rows - high.astype(F32)).astype(BF)
    return jnp.concatenate([high, rest], axis=0)


def head_lanes():
    shape = (2 * HEAD_COUNT, INNER_WIDTH)
    return (iota(shape, 1) // HEAD_DIM == iota(shape, 0) % HEAD_COUNT).astype(F32).astype(BF)


def inverse_rms(rows):
    return lax.rsqrt(jnp.mean(rows * rows, axis=-1, keepdims=True) + EPS_NORM)


def norm_back(rows, gain, grad):
    inverse = inverse_rms(rows)
    unit = rows * inverse
    scaled = grad * gain
    d_rows = inverse * (scaled - unit * jnp.mean(scaled * unit, axis=-1, keepdims=True))
    return d_rows, jnp.sum(grad * unit, axis=0, keepdims=True)


def half_lanes(h):
    return (iota((BLOCK, GROUP), 1) % LANES) // (HEAD_DIM // 2) == h


def whole_lanes(h):
    return iota((BLOCK, GROUP), 1) // HEAD_DIM == h


def picked(mask, tensor):
    return jnp.where(mask, tensor, jnp.zeros_like(tensor))


def group_slice(g):
    return slice(g * GROUP, (g + 1) * GROUP)


def forward_block(x, w_ref, small, cos, sin, bias_ref, keep, start, item, width_ff, tick=None):
    gate_weight, gain_attn, gain_ff = small
    size = x.shape[0]
    rows = pl.ds(start, size)
    normed = (x * inverse_rms(x) * gain_attn).astype(BF)
    if "normed" in keep:
        keep["normed"][rows, :] = normed
    gate_rows = jax.nn.sigmoid(nt(gate_weight, normed))
    keep["gate"][:, rows] = gate_rows
    half = GROUP // 2
    for g in range(2):
        for part, name in ((0, "q"), (1, "k")):
            column = part * INNER_WIDTH + g * GROUP
            t = nn(normed, w_ref[:, column : column + GROUP])
            a, b = t[:, :half], t[:, half:]
            keep[name][rows, g * GROUP : g * GROUP + half] = (a * cos - b * sin).astype(BF)
            keep[name][rows, g * GROUP + half : (g + 1) * GROUP] = (b * cos + a * sin).astype(BF)
        column = 2 * INNER_WIDTH + g * GROUP
        keep["v"][rows, group_slice(g)] = nn(normed, w_ref[:, column : column + GROUP]).astype(BF)
    gate = tn(split_rows(gate_rows), head_lanes())
    for n in range(size // BLOCK):
        if tick and n == size // BLOCK - 1:
            tick()
        block = pl.ds(start + n * BLOCK, BLOCK)
        for g in range(2):
            lanes = group_slice(g)
            queries, keys = keep["q"][block, lanes], keep["k"][block, lanes]
            values = keep["v"][block, lanes]
            parts, heads = [], []
            for h in range(4):
                scores = nt(picked(half_lanes(h), keys), queries) + bias_ref[...]
                peak = jnp.max(scores, axis=0, keepdims=True)
                terms = jnp.exp2((scores - peak) * SCORE_EXP)
                probs = (terms * (1.0 / jnp.sum(terms, axis=0, keepdims=True))).astype(BF)
                keep["probs"][item + n, g * 4 + h] = probs
                parts.append(probs)
                heads.append(picked(whole_lanes(h), values))
            attended = tn(jnp.concatenate(parts, axis=0), jnp.concatenate(heads, axis=0))
            keep["gated"][block, lanes] = (attended * gate[n * BLOCK : (n + 1) * BLOCK, lanes]).astype(BF)
    out_start = 3 * INNER_WIDTH + width_ff
    middle = x + nt(keep["gated"][rows, :], w_ref[:, out_start : out_start + INNER_WIDTH])
    keep["middle"][rows, :] = middle
    normed_ff = (middle * inverse_rms(middle) * gain_ff).astype(BF)
    if "normed_ff" in keep:
        keep["normed_ff"][rows, :] = normed_ff
    result = middle
    for c in range(width_ff // GROUP):
        up = 3 * INNER_WIDTH + c * GROUP
        down = out_start + INNER_WIDTH + c * GROUP
        hidden = nn(normed_ff, w_ref[:, up : up + GROUP])
        cumulative = 0.5 + 0.5 * lax.erf(hidden * SQRT_HALF)
        activated = (hidden * cumulative).astype(BF)
        density = jnp.exp2(hidden * hidden * (-0.5 * LOG2E)) * GAUSS
        keep["act"][rows, group_slice(c)] = activated
        keep["slope"][rows, group_slice(c)] = (cumulative + hidden * density).astype(BF)
        result = result + nt(activated, w_ref[:, down : down + GROUP])
    return result


def backward_block(d_out, x, w_ref, small, cos, sin, keep, work, sums, start, item, width_ff, tick=None):
    gate_weight, gain_attn, gain_ff = small
    size = x.shape[0]
    rows = pl.ds(start, size)
    branch = d_out.astype(BF)
    work["branch"][rows, :] = branch
    out_start = 3 * INNER_WIDTH + width_ff
    d_normed_ff = None
    for c in range(width_ff // GROUP):
        up = 3 * INNER_WIDTH + c * GROUP
        down = out_start + INNER_WIDTH + c * GROUP
        d_act = nn(branch, w_ref[:, down : down + GROUP])
        d_hidden = (d_act * keep["slope"][rows, group_slice(c)].astype(F32)).astype(BF)
        work["d_hidden"][rows, group_slice(c)] = d_hidden
    up = 3 * INNER_WIDTH
    d_normed_ff = nt(work["d_hidden"][rows, :], w_ref[:, up : up + width_ff])
    middle = keep["middle"][rows, :]
    d_rows, d_gain_ff = norm_back(middle, gain_ff, d_normed_ff)
    d_middle = d_out + d_rows
    attn_back = d_middle.astype(BF)
    work["attn_back"][rows, :] = attn_back
    gate_rows = keep["gate"][:, rows]
    lanes_of = head_lanes()
    gate = tn(split_rows(gate_rows), lanes_of)
    d_gated = nn(attn_back, w_ref[:, out_start : out_start + INNER_WIDTH])
    product = d_gated * keep["gated"][rows, :].astype(F32)
    high = product.astype(BF)
    rest = (product - high.astype(F32)).astype(BF)
    delta_rows = (nt(lanes_of, high) + nt(lanes_of, rest))[:HEAD_COUNT]
    d_logit = split_rows(delta_rows * (1.0 - gate_rows))
    d_attended = (d_gated * gate).astype(BF)
    half = GROUP // 2
    scale = HEAD_DIM**-0.5
    for n in range(size // BLOCK):
        if tick and n == size // BLOCK - 1:
            tick()
        block = pl.ds(start + n * BLOCK, BLOCK)
        inner = slice(n * BLOCK, (n + 1) * BLOCK)
        for g in range(2):
            lanes = group_slice(g)
            queries, keys = keep["q"][block, lanes], keep["k"][block, lanes]
            values, d_att = keep["v"][block, lanes], d_attended[inner, lanes]
            p_list, s_list, q_list, a_list, k_list = [], [], [], [], []
            for h in range(4):
                halves, wholes = half_lanes(h), whole_lanes(h)
                probs = keep["probs"][item + n, g * 4 + h]
                d_probs = nt(picked(wholes, values), d_att)
                delta = delta_rows[g * 4 + h : g * 4 + h + 1, inner]
                d_scores = (probs.astype(F32) * (d_probs - delta)).astype(BF)
                p_list.append(probs)
                s_list.append(d_scores)
                a_list.append(picked(wholes, d_att))
                q_list.append(picked(halves, queries))
                k_list.append(picked(halves, keys))
            d_values = nn(jnp.concatenate(p_list, axis=1), jnp.concatenate(a_list, axis=0))
            d_keys = nn(jnp.concatenate(s_list, axis=1), jnp.concatenate(q_list, axis=0))
            d_query = tn(jnp.concatenate(s_list, axis=0), jnp.concatenate(k_list, axis=0))
            for column, t in ((0, d_query), (INNER_WIDTH, d_keys)):
                t = t * scale
                a, b = t[:, :half], t[:, half:]
                c, s = cos[inner], sin[inner]
                column = column + g * GROUP
                work["d_proj"][block, column : column + half] = (a * c + b * s).astype(BF)
                work["d_proj"][block, column + half : column + GROUP] = (b * c - a * s).astype(BF)
            column = 2 * INNER_WIDTH + g * GROUP
            work["d_proj"][block, column : column + GROUP] = d_values.astype(BF)
    twice = jnp.concatenate([gate_weight, gate_weight], axis=0)
    d_normed = tn(d_logit, twice)
    for c in range(3 * INNER_WIDTH // INNER_WIDTH):
        part = slice(c * INNER_WIDTH, (c + 1) * INNER_WIDTH)
        d_normed = d_normed + nt(work["d_proj"][rows, part], w_ref[:, part])
    d_rows, d_gain_attn = norm_back(x, gain_attn, d_normed)
    d_gate = nn(d_logit, work["normed"][rows, :])
    sums[0:HEAD_COUNT, :] += d_gate[:HEAD_COUNT] + d_gate[HEAD_COUNT:]
    sums[HEAD_COUNT : HEAD_COUNT + 1, :] += d_gain_attn
    sums[HEAD_COUNT + 1 : HEAD_COUNT + 2, :] += d_gain_ff
    return d_middle + d_rows


def weight_sums(total, work, keep, width_ff):
    out_start = 3 * INNER_WIDTH + width_ff
    pairs = (
        (work["normed"], work["d_proj"], 0),
        (work["normed_ff"], work["d_hidden"], 3 * INNER_WIDTH),
        (work["attn_back"], keep["gated"], out_start),
        (work["branch"], keep["act"], out_start + INNER_WIDTH),
    )
    for left, right, start in pairs:
        turned = left[...].T
        for c in range(right.shape[-1] // INNER_WIDTH):
            part = slice(start + c * INNER_WIDTH, start + (c + 1) * INNER_WIDTH)
            total[:, part] += nn(turned, right[:, c * INNER_WIDTH : (c + 1) * INNER_WIDTH])


def masked_keys(valid):
    return jnp.where(valid, 0.0, MASKED).astype(F32)


def turn_small(w_ref, small_ref):
    width = w_ref.shape[1] - SMALL_LANES
    rows = w_ref[:, width : width + LANES].astype(F32).T
    small_ref[...] = rows[: small_ref.shape[0]]


def small_parts(small_ref):
    gate_weight = small_ref[0:HEAD_COUNT, :].astype(BF)
    return (
        gate_weight,
        small_ref[HEAD_COUNT : HEAD_COUNT + 1, :],
        small_ref[HEAD_COUNT + 1 : HEAD_COUNT + 2, :],
    )


def finish_sums(total, sums, out_ref, arrival):
    width = total.shape[1] - SMALL_LANES
    model = total.shape[0]
    tall = jnp.concatenate([sums[...], jnp.zeros((SMALL_LANES - sums.shape[0], model), F32)], axis=0)
    if out_ref.dtype == F32:
        total[:, width:] = tall.T
        copy = pltpu.make_async_copy(total, out_ref, arrival)
        copy.start()
        copy.wait()
    else:
        out_ref[:, :width] = total[:, :width].astype(out_ref.dtype)
        out_ref[:, width:] = tall.T.astype(out_ref.dtype)


def start_sums(total, sums, before_ref, arrival):
    sums[...] = jnp.zeros_like(sums)
    if before_ref is None:
        total[...] = jnp.zeros_like(total)
    else:
        pltpu.make_async_copy(before_ref, total, arrival).start()


def await_sums(total, sums, before_ref, arrival):
    if before_ref is not None:
        width = total.shape[1] - SMALL_LANES
        pltpu.make_async_copy(before_ref, total, arrival).wait()
        sums[...] += total[:, width:].T[: sums.shape[0]]


SAVED = ("q", "k", "v", "gate", "probs", "gated", "middle", "act", "slope")


def time_forward_kernel(parts, width_ff, ride, m, x_ref, w_ref, cos_ref, sin_ref, len_ref, *refs):
    step, steps = pl.program_id(0), pl.num_programs(0)
    tick, gather = None, None
    if ride:
        shard_ref, out_ref, refs, full_ref = refs[0], refs[1], refs[2:], refs[11]
        sems = refs[-GATHER_SCRATCH:]
        small_ref, bias_ref = refs[-GATHER_SCRATCH - 2 : -GATHER_SCRATCH]
        if ride == "lines":
            gather = Gather(Place(parts), shard_ref, full_ref, *sems, at_once=False)
            pl.when(step == 0)(gather.start)
            gather.advance(2 * step, 2 * steps)
            tick = partial(gather.advance, 2 * step + 1, 2 * steps)
        else:
            gather = Gather(Place(parts), None, full_ref, *sems)
            pl.when(step == 0)(gather.open_passing)
            pl.when(step == steps - 1)(gather.pass_taken)
    else:
        out_ref, refs = refs[0], refs[1:]
        small_ref, bias_ref = refs[-2:]
    keep = dict(zip(SAVED, refs))

    @pl.when(step == 0)
    def _():
        turn_small(w_ref, small_ref)
        bias_ref[...] = masked_keys(iota((BLOCK, BLOCK), 0) < len_ref[m : m + 1, :])

    per_step, whole_frames, model = x_ref.shape
    x = x_ref[...].astype(F32).reshape(per_step * whole_frames, model)
    out = forward_block(
        x, w_ref, small_parts(small_ref), cos_ref[...], sin_ref[...], bias_ref, keep, 0, 0, width_ff, tick
    )
    frames = out_ref.shape[2]
    for n in range(per_step):
        out_ref[:, n] = out[n * whole_frames : (n + 1) * whole_frames].reshape(parts, frames, model).astype(BF)

    @pl.when(step == steps - 1)
    def _():
        if ride == "lines":
            gather.other_lines()
            gather.finish_lines()
        elif ride:
            gather.finish_passing()


def time_backward_kernel(parts, width_ff, chained, ride, per_step, *refs):
    x_ref, d_ref, w_ref, cos_ref, sin_ref = refs[:5]
    keep = dict(zip(SAVED, refs[5:14]))
    refs = refs[14:]
    before = refs[0] if chained else None
    refs = refs[2 - ride :] if chained else refs
    step, steps = pl.program_id(0), pl.num_programs(0)
    if ride:
        other_ref, dx_ref, grad_ref, shard_ref = refs[:4]
        reduction = Reduction(Place(parts), other_ref, refs[-REDUCE_SCRATCH:])
        refs = refs[:-REDUCE_SCRATCH]
    else:
        dx_ref, grad_ref = refs[:2]
    total, sums, normed, normed_ff, d_hidden, attn_back, branch, d_proj, arrival, small_ref = refs[-10:]
    work = dict(
        normed=normed, normed_ff=normed_ff, d_hidden=d_hidden, attn_back=attn_back, branch=branch, d_proj=d_proj
    )

    @pl.when(step == 0)
    def _():
        start_sums(total, sums, before, arrival)
        turn_small(w_ref, small_ref)

    small = small_parts(small_ref)
    if ride:
        reduction.advance(2 * step, 2 * steps - 1)
    model = x_ref.shape[2]
    x = x_ref[...].astype(F32).reshape(per_step * BLOCK, model)
    work["normed"][...] = (x * inverse_rms(x) * small[1]).astype(BF)
    middle = keep["middle"][...]
    work["normed_ff"][...] = (middle * inverse_rms(middle) * small[2]).astype(BF)
    d_out = jnp.concatenate([d_ref[:, i].astype(F32).reshape(BLOCK, model) for i in range(per_step)], axis=0)
    d_x = backward_block(
        d_out, x, w_ref, small, cos_ref[...], sin_ref[...], keep, work, sums, 0, 0, width_ff,
        partial(reduction.advance, 2 * step + 1, 2 * steps - 1) if ride else None,
    )
    dx_ref[...] = d_x.reshape(dx_ref.shape)
    if chained:

        @pl.when(step == 0)
        def _():
            await_sums(total, sums, before, arrival)

    weight_sums(total, work, keep, width_ff)

    @pl.when(step == steps - 1)
    def _():
        finish_sums(total, sums, grad_ref, arrival)
        if ride:
            reduction.finish()
            shard_ref[...] = reduction.own[...]
            reduction.drain()


def gather_rows(ref, strides, factors):
    return jnp.concatenate(
        [
            jnp.concatenate([ref[p, s, :] * f for p in range(ref.shape[0])], axis=1)
            for s, f in zip(strides, factors)
        ],
        axis=0,
    )


def band_kernel(width_ff, chained, m, len_ref, *refs):
    x_ref, d_ref, w_ref, cos_ref, sin_ref = refs[:5]
    refs = refs[5:]
    before = refs[0] if chained else None
    out_ref, back_ref, grad_ref = refs[2:5] if chained else refs[:3]
    scratch = refs[-22:]
    keep = dict(zip(SAVED, scratch[:9]))
    total, sums, normed, normed_ff, d_hidden, attn_back, branch, d_proj, arrival, small_ref, rows_a, rows_b, bias_ref = scratch[9:]
    work = dict(
        normed=normed, normed_ff=normed_ff, d_hidden=d_hidden, attn_back=attn_back, branch=branch, d_proj=d_proj
    )
    keep.update(normed=normed, normed_ff=normed_ff)
    step = pl.program_id(0)
    bands, frames, model = x_ref.shape
    pieces = model // LANES

    @pl.when(step == 0)
    def _():
        start_sums(total, sums, before, arrival)
        turn_small(w_ref, small_ref)
        same = iota((BLOCK, BLOCK), 0) // bands == iota((BLOCK, BLOCK), 1) // bands
        bias_ref[...] = masked_keys(same)

    small = small_parts(small_ref)
    for p in range(pieces):
        lanes = slice(p * LANES, (p + 1) * LANES)
        rows_a[p] = x_ref[:, :, lanes].astype(F32).reshape(bands * frames, LANES)
        rows_b[p] = d_ref[:, :, lanes].astype(F32).reshape(bands * frames, LANES)
    first = (lax.axis_index("seq") * pl.num_programs(0) + step) * frames

    size = cos_ref.shape[0]
    spread = size // bands

    def one(j, carry):
        start = pl.multiple_of(j * size, size)
        item = j * (size // BLOCK)
        strides = [pl.ds(j * spread + f, bands, stride=frames) for f in range(spread)]
        valid = [(first + j * spread + f < len_ref[m, 0]).astype(F32) for f in range(spread)]
        x = gather_rows(rows_a, strides, [1.0] * spread)
        d_out = gather_rows(rows_b, strides, valid)
        out = forward_block(
            x, w_ref, small, cos_ref[...], sin_ref[...], bias_ref, keep, start, item, width_ff
        )
        for f in range(spread):
            for p in range(pieces):
                part = out[f * bands : (f + 1) * bands, p * LANES : (p + 1) * LANES]
                rows_a[p, strides[f], :] = part * valid[f]
        back = backward_block(
            d_out, x, w_ref, small, cos_ref[...], sin_ref[...], keep, work, sums, start, item, width_ff
        )
        for f in range(spread):
            for p in range(pieces):
                part = back[f * bands : (f + 1) * bands, p * LANES : (p + 1) * LANES]
                rows_b[p, strides[f], :] = part
        return carry

    lax.fori_loop(0, bands * frames // size, one, 0)
    for p in range(pieces):
        lanes = slice(p * LANES, (p + 1) * LANES)
        out_ref[:, :, lanes] = rows_a[p].reshape(bands, frames, LANES).astype(BF)
        back_ref[:, :, lanes] = rows_b[p].reshape(bands, frames, LANES).astype(BF)
    if chained:

        @pl.when(step == 0)
        def _():
            await_sums(total, sums, before, arrival)

    weight_sums(total, work, keep, width_ff)

    @pl.when(step == pl.num_programs(0) - 1)
    def _():
        finish_sums(total, sums, grad_ref, arrival)


def whole(shape):
    return pl.BlockSpec(shape, lambda *i: (0,) * len(shape), pipeline_mode=pl.Buffered(1))


def params(**more):
    return pltpu.CompilerParams(vmem_limit_bytes=VMEM_LIMIT, **more)


def rotary_tables(positions, rows):
    half_width = HEAD_DIM // 2
    inverse = np.float32(10000.0) ** (-(np.arange(half_width, dtype=np.float32) * np.float32(2.0 / HEAD_DIM)))
    angles = np.arange(positions, dtype=np.float32)[:, None] * inverse[None, :].astype(np.float32)
    angles = np.tile(angles, (rows // positions, LANES // half_width))
    return (jnp.asarray(np.cos(angles), F32), jnp.asarray(np.sin(angles), F32))


def saved_shapes(tokens, items, model, width_ff):
    return (
        ((tokens, INNER_WIDTH), BF),
        ((tokens, INNER_WIDTH), BF),
        ((tokens, INNER_WIDTH), BF),
        ((HEAD_COUNT, tokens), F32),
        ((items, HEAD_COUNT, BLOCK, BLOCK), BF),
        ((tokens, INNER_WIDTH), BF),
        ((tokens, model), F32),
        ((tokens, width_ff), BF),
        ((tokens, width_ff), BF),
    )


def saved_specs(tokens, items, model, width_ff):
    def place(shape):
        if shape[0] == HEAD_COUNT:
            return pl.BlockSpec(shape, lambda i, *s: (0, i))
        return pl.BlockSpec(shape, lambda i, *s: (i,) + (0,) * (len(shape) - 1))

    return [place(shape) for shape, kind in saved_shapes(tokens, items, model, width_ff)]


def work_shapes(tokens, model, width_ff, columns):
    return [
        pltpu.VMEM((model, columns), F32),
        pltpu.VMEM((2 * HEAD_COUNT, model), F32),
        pltpu.VMEM((tokens, model), BF),
        pltpu.VMEM((tokens, model), BF),
        pltpu.VMEM((tokens, width_ff), BF),
        pltpu.VMEM((tokens, model), BF),
        pltpu.VMEM((tokens, model), BF),
        pltpu.VMEM((tokens, 3 * INNER_WIDTH), BF),
        pltpu.SemaphoreType.DMA,
        pltpu.VMEM((2 * HEAD_COUNT, model), F32),
    ]


def at_micro(m, shape, place):
    return pl.BlockSpec((None, None) + shape, lambda i, *s: (m, 0) + place(i))


def sequences(seqs):
    return 2 if seqs % 2 == 0 else 1


def time_forward(m, x, lengths, weights, tables, ride, other, parts, width_ff):
    seqs, frames, model = x.shape[2:]
    tokens = seqs * frames
    shapes = saved_shapes(tokens, seqs, model, width_ff)
    out = jax.ShapeDtypeStruct((parts, seqs, frames // parts, model), BF)
    per_step = sequences(seqs)
    any_space = pl.BlockSpec(memory_space=pl.ANY)
    riding = 1 if ride else 0
    full = [jax.ShapeDtypeStruct((parts,) + other.shape[-2:], BF)] * riding
    aliases = {5: 1 + len(SAVED)} if ride == "pass" else {}
    results = pl.pallas_call(
        partial(time_forward_kernel, parts, width_ff, ride, m),
        grid=(seqs // per_step,),
        in_specs=[
            at_micro(m, (per_step, frames, model), lambda i: (i, 0, 0)),
            whole(weights.shape),
            whole(tables[0].shape),
            whole(tables[1].shape),
            whole(lengths.shape),
        ]
        + [any_space] * riding,
        out_specs=[
            pl.BlockSpec((parts, per_step, frames // parts, model), lambda i: (0, i, 0, 0)),
            *saved_specs(per_step * frames, per_step, model, width_ff),
        ]
        + [any_space] * riding,
        scratch_shapes=[pltpu.VMEM((2 * HEAD_COUNT, model), F32), pltpu.VMEM((BLOCK, BLOCK), F32)]
        + (gather_scratch(parts) if ride else []),
        out_shape=[out, *(jax.ShapeDtypeStruct(s, k) for s, k in shapes)] + full,
        input_output_aliases=aliases,
        compiler_params=params(collective_id=3 if ride == "lines" else 5, has_side_effects=True) if ride else params(),
        cost_estimate=pl.CostEstimate(
            flops=int(tokens * 5e6), bytes_accessed=tokens * 15000, transcendentals=tokens * 5000
        ),
        name="time_forward_" + ride if ride else "time_forward",
    )(x, weights, *tables, lengths, *([other] if ride else []))
    saved = results[1 : 1 + len(SAVED)]
    return results[0], saved, (results[-1] if ride else other)


def time_backward(m, x, d_out, weights, tables, saved, before, other, kind, width_ff):
    seqs, frames, model = x.shape[2:]
    tokens = seqs * frames
    parts, unused, part_frames, unused_model = d_out.shape
    per_step = sequences(seqs)
    columns = weights.shape[1]
    ride = other is not None
    if ride:
        before = before[:1]
    ins = [x, d_out, weights, *tables, *saved, *before]
    aliases = {len(ins) - 1: 0} if len(before) == 2 else {}
    target = (1, 1) + x.shape[2:] if ride else x.shape
    more_specs, more_shapes, scratch = [], [], []
    any_space = pl.BlockSpec(memory_space=pl.ANY)
    if ride:
        zs, ys = seq_sides(parts)
        part = model // parts
        ins.append(other.reshape(zs, ys, part, columns))
        more_shapes = [jax.ShapeDtypeStruct((part, columns // 2), BF)]
        more_specs = [whole(more_shapes[0].shape)]
        scratch = reduce_scratch(parts, part, columns)
    rows = at_micro(m, (per_step, frames, model), lambda i: (i, 0, 0))
    return pl.pallas_call(
        partial(time_backward_kernel, parts, width_ff, bool(before), ride, per_step),
        grid=(seqs // per_step,),
        in_specs=[
            rows,
            pl.BlockSpec((parts, per_step, part_frames, model), lambda i: (0, i, 0, 0)),
            whole(weights.shape),
            whole(tables[0].shape),
            whole(tables[1].shape),
            *saved_specs(per_step * frames, per_step, model, width_ff),
        ]
        + [any_space] * (len(before) + ride),
        out_specs=[
            at_micro(0 if ride else m, (per_step, frames, model), lambda i: (i, 0, 0)),
            any_space if kind == F32 else whole((model, columns)),
        ]
        + more_specs,
        out_shape=[
            jax.ShapeDtypeStruct(target, F32),
            jax.ShapeDtypeStruct((model, columns), kind),
        ]
        + more_shapes,
        input_output_aliases=aliases,
        scratch_shapes=work_shapes(per_step * frames, model, width_ff, columns) + scratch,
        compiler_params=params(collective_id=4, has_side_effects=True) if ride else params(),
        cost_estimate=pl.CostEstimate(
            flops=int(tokens * 9e6), bytes_accessed=tokens * 18000, transcendentals=0
        ),
        name="time_backward_reduce" if ride else "time_backward",
    )(*ins)


def band_both(m, x, d_out, lengths, weights, tables, before, kind, width_ff):
    bands, frames, model = x.shape
    tokens = bands * frames
    chunk = math.gcd(frames, 16)
    step_tokens = bands * chunk
    columns = weights.shape[1]
    ins = [lengths, x, d_out, weights, *tables, *before]
    rows = pl.BlockSpec((bands, chunk, model), lambda i, s: (0, i, 0))
    rows_m = at_micro(m, (bands, chunk, model), lambda i: (0, i, 0))
    any_space = pl.BlockSpec(memory_space=pl.ANY)
    saved = [
        pltpu.VMEM(s, k) for s, k in saved_shapes(step_tokens, step_tokens // BLOCK, model, width_ff)
    ]
    return pl.pallas_call(
        partial(band_kernel, width_ff, bool(before), m),
        grid_spec=pltpu.PrefetchScalarGridSpec(
            num_scalar_prefetch=1,
            grid=(frames // chunk,),
            in_specs=[
                rows,
                rows_m,
                whole(weights.shape),
                whole(tables[0].shape),
                whole(tables[1].shape),
            ]
            + [any_space] * len(before),
            out_specs=[rows_m, rows, any_space if kind == F32 else whole((model, columns))],
            scratch_shapes=saved
            + work_shapes(step_tokens, model, width_ff, columns)
            + [pltpu.VMEM((model // LANES, step_tokens, LANES), F32)] * 2
            + [pltpu.VMEM((BLOCK, BLOCK), F32)],
        ),
        out_shape=[
            jax.ShapeDtypeStruct(d_out.shape, BF),
            jax.ShapeDtypeStruct(x.shape, BF),
            jax.ShapeDtypeStruct((model, columns), kind),
        ],
        input_output_aliases={len(ins) - 1: 0} if before else {},
        compiler_params=params(),
        cost_estimate=pl.CostEstimate(
            flops=int(tokens * 14e6), bytes_accessed=tokens * 8000, transcendentals=tokens * 5000
        ),
        name="band_both",
    )(*ins)


MESH = pl.DeviceIdType.MESH


def seq_sides(parts):
    side = 1
    while 4 * side * side <= parts:
        side *= 2
    return parts // side, side


class Place:
    def __init__(self, parts):
        self.dp, self.seq = lax.axis_index("dp"), lax.axis_index("seq")
        self.core = self.dp % 2
        self.zs, self.ys = seq_sides(parts)
        self.z, self.y = self.seq // self.ys, self.seq % self.ys

    def sibling(self):
        return (self.dp + 1 - 2 * self.core, self.seq)

    def along_z(self, step):
        return (self.dp, self.seq + step * self.ys)

    def along_y(self, step):
        return (self.dp, self.seq + step)

    def has_z(self, step):
        return self.z + step < self.zs if step > 0 else self.z + step >= 0

    def has_y(self, step):
        return self.y + step < self.ys if step > 0 else self.y + step >= 0


def greet(place, others=()):
    barrier = pltpu.get_barrier_semaphore()
    pl.semaphore_signal(barrier, inc=1, device_id=place.sibling(), device_id_type=MESH)
    for other in others:
        pl.semaphore_signal(barrier, inc=1, device_id=other, device_id_type=MESH)
    for step in (1, -1):
        for has, to in ((place.has_z, place.along_z), (place.has_y, place.along_y)):

            @pl.when(has(step))
            def _(to=to, step=step):
                pl.semaphore_signal(barrier, inc=1, device_id=to(step), device_id_type=MESH)

    count = 1 + len(others)
    for has in (place.has_z, place.has_y):
        count = count + has(1).astype(jnp.int32) + has(-1).astype(jnp.int32)
    pl.semaphore_wait(barrier, count)


GATHER_SCRATCH = 9


class Gather:
    def __init__(
        self, place, shard_ref, out_ref, send_z, send_y, send_c, got, got_c, local, send_x, got_x, send_cx, at_once=True
    ):
        self.place, self.shard, self.out, self.at_once = place, shard_ref, out_ref, at_once
        self.send_z, self.send_y, self.send_c, self.got, self.got_c, self.local = send_z, send_y, send_c, got, got_c, local
        self.send_x, self.got_x, self.send_cx = send_x, got_x, send_cx
        wide = out_ref.shape[2] // 2
        self.blocks = place.zs * place.ys
        self.crossing = lax.axis_size("dp") == 4 and wide % (3 * LANES) == 0
        third = wide // 3
        x = place.dp // 2

        def columns(core, start, size):
            return pl.ds(pl.multiple_of(core * wide + start, LANES), size)

        if self.crossing:
            self.lanes = columns(place.core, x * third, 2 * third)
            self.other_lanes = columns(1 - place.core, x * third, 2 * third)
            self.given = columns(place.core, x * 2 * third, third)
            self.taken = columns(place.core, (1 - x) * 2 * third, third)
            self.other_taken = columns(1 - place.core, (1 - x) * 2 * third, third)
            self.across = (lax.rem(place.dp + 2, 4), place.seq)
        else:
            self.lanes = columns(place.core, 0, wide)
            self.other_lanes = columns(1 - place.core, 0, wide)
        self.mine = None if shard_ref is None else shard_ref.at[:, self.lanes]
        self.hops = place.zs
        self.others = [lax.rem(place.seq + turn, self.blocks) for turn in range(1, self.blocks)]

    def index(self, z, y):
        return z * self.place.ys + y

    def held(self, p):
        return self.out.at[p, :, self.lanes]

    def push(self, source, p, to, send, receive):
        return pltpu.make_async_remote_copy(
            src_ref=source, dst_ref=self.held(p), send_sem=send, recv_sem=receive, device_id=to, device_id_type=MESH
        )

    def same(self, p, lanes, to, send, receive):
        there = self.out.at[p, :, lanes]
        return pltpu.make_async_remote_copy(
            src_ref=there, dst_ref=there, send_sem=send, recv_sem=receive, device_id=to, device_id_type=MESH
        )

    def to_sibling(self, p):
        return self.same(p, self.lanes, self.place.sibling(), self.send_c.at[p], self.got_c.at[0, p])

    def from_sibling(self, p):
        return self.same(p, self.other_lanes, self.place.sibling(), self.send_c.at[p], self.got_c.at[0, p])

    def give(self, p):
        return self.same(p, self.given, self.across, self.send_x.at[p], self.got_x.at[p])

    def take(self, p):
        return self.same(p, self.taken, self.across, self.send_x.at[p], self.got_x.at[p])

    def taken_to_sibling(self, p):
        return self.same(p, self.taken, self.place.sibling(), self.send_cx.at[p], self.got_c.at[1, p])

    def taken_from_sibling(self, p):
        return self.same(p, self.other_taken, self.place.sibling(), self.send_cx.at[p], self.got_c.at[1, p])

    def along_z(self, source, p, step, t):
        return self.push(source, p, self.place.along_z(step), self.send_z.at[(step + 1) // 2, t], self.got.at[p])

    def along_y(self, source, p, step):
        return self.push(source, p, self.place.along_y(step), self.send_y.at[(step + 1) // 2, p], self.got.at[p])

    def await_block(self, p):
        self.push(self.held(p), p, self.place.sibling(), self.send_c.at[p], self.got.at[p]).wait_recv()

    def hand_on(self, p):
        if self.at_once:
            self.pass_on(p)

    def pass_on(self, p):
        if self.crossing:
            self.give(p).start()
        self.to_sibling(p).start()

    def open_passing(self):
        barrier = pltpu.get_barrier_semaphore()
        peers = [self.place.sibling()] + ([self.across] if self.crossing else [])
        for to in peers:
            pl.semaphore_signal(barrier, inc=1, device_id=to, device_id_type=MESH)
        pl.semaphore_wait(barrier, len(peers))
        for p in self.others:
            self.pass_on(p)

    def own(self):
        return pltpu.make_async_copy(self.shard, self.out.at[self.place.seq], self.local)

    def start(self):
        place = self.place
        greet(place, [self.across] if self.crossing else [])
        self.own().start()
        for step in (1, -1):
            pl.when(place.has_z(step))(lambda step=step: self.along_z(self.mine, place.seq, step, 0).start())
            pl.when(place.has_y(step))(lambda step=step: self.along_y(self.mine, place.seq, step).start())

    def advance(self, slot, slots):
        for hop in range(1, self.hops):
            due = (hop * (slots - 2) + self.hops - 2) // (self.hops - 1) if self.hops > 1 else 0
            pl.when(slot == due)(partial(self.hop, hop))

    def hop(self, t):
        if t == self.place.zs:
            return self.other_lines()
        place = self.place
        for step in (1, -1):
            z = place.z - step * t
            here = (z >= 0) if step > 0 else (z < place.zs)

            @pl.when(here)
            def _(step=step, z=z):
                p = self.index(z, place.y)
                self.await_block(p)
                if t < place.zs - 1:
                    pl.when(place.has_z(step))(lambda: self.along_z(self.held(p), p, step, t).start())
                for side in (1, -1):
                    pl.when(place.has_y(side))(lambda side=side: self.along_y(self.held(p), p, side).start())
                self.hand_on(p)

    def other_lines(self):
        place = self.place
        for t in range(1, place.ys):
            for step in (1, -1):
                y = place.y - step * t
                here = (y >= 0) if step > 0 else (y < place.ys)

                @pl.when(here)
                def _(t=t, step=step, y=y):
                    for turn in range(place.zs):
                        p = self.index(lax.rem(place.z + turn, place.zs), y)
                        self.await_block(p)
                        if t < place.ys - 1:
                            pl.when(place.has_y(step))(lambda p=p: self.along_y(self.held(p), p, step).start())
                        self.hand_on(p)

    def pass_taken(self):
        if self.crossing:
            for p in self.others:
                self.take(p).wait_recv()
                self.taken_to_sibling(p).start()

    def finish_passing(self):
        for p in self.others:
            self.to_sibling(p).wait_send()
            self.from_sibling(p).wait_recv()
        if self.crossing:
            for p in self.others:
                self.give(p).wait_send()
                self.taken_to_sibling(p).wait_send()
                self.taken_from_sibling(p).wait_recv()

    def finish_lines(self):
        place = self.place
        self.own().wait()
        for step in (1, -1):
            for t in range(place.zs - 1):
                z = place.z - step * t
                sent = jnp.logical_and((z >= 0) if step > 0 else (z < place.zs), place.has_z(step))
                pl.when(sent)(lambda step=step, t=t: self.along_z(self.mine, place.seq, step, t).wait_send())
            for t in range(place.ys - 1):
                y = place.y - step * t
                sent = jnp.logical_and((y >= 0) if step > 0 else (y < place.ys), place.has_y(step))

                @pl.when(sent)
                def _(step=step, y=y):
                    for z in range(place.zs):
                        self.along_y(self.mine, self.index(z, y), step).wait_send()


def gather_kernel(parts, shard_ref, out_ref, *sems):
    gather = Gather(Place(parts), shard_ref, out_ref, *sems)
    gather.start()
    for hop in range(1, gather.hops + 1):
        gather.hop(hop)
    gather.pass_taken()
    gather.finish_passing()
    gather.finish_lines()


def gather_scratch(parts):
    zs, ys = seq_sides(parts)
    dma = pltpu.SemaphoreType.DMA
    each = dma((parts,))
    return [dma((2, zs)), dma((2, parts)), each, each, dma((2, parts)), dma, each, each, each]


def gather_weights(shard, parts):
    rows, columns = shard.shape
    out = pl.pallas_call(
        partial(gather_kernel, parts),
        in_specs=[pl.BlockSpec(memory_space=pl.ANY)],
        out_specs=pl.BlockSpec(memory_space=pl.ANY),
        out_shape=jax.ShapeDtypeStruct((parts, rows, columns), shard.dtype),
        scratch_shapes=gather_scratch(parts),
        compiler_params=params(collective_id=1, has_side_effects=True),
        cost_estimate=pl.CostEstimate(flops=0, bytes_accessed=parts * rows * columns * 40, transcendentals=0),
        name="gather_weights",
    )(shard)
    return out.reshape(parts * rows, columns)


def add_into(acc, other):
    acc[...] = (acc[...].astype(F32) + other[...].astype(F32)).astype(acc.dtype)


class Line:
    def __init__(self, i, n, to, acc, slot, count, sends, receives):
        self.i, self.n, self.to, self.acc, self.slot, self.count = i, n, to, acc, slot, count
        self.sends, self.receives = sends, receives

    def copy(self, side, j, k):
        return pltpu.make_async_remote_copy(
            src_ref=self.acc(j, k),
            dst_ref=self.slot(side, j, k),
            send_sem=self.sends.at[side, j, k],
            recv_sem=self.receives.at[side, j, k],
            device_id=self.to(1 - 2 * side),
            device_id_type=MESH,
        )

    def take(self, side, j, k):
        self.copy(side, j, k).wait_recv()
        add_into(self.acc(j, k), self.slot(side, j, k))

    def send_pair(self, k):
        pl.when(self.i == 0)(lambda: self.copy(0, 1, k).start())
        pl.when(self.i == 1)(lambda: self.copy(1, 0, k).start())

    def send(self, now, base):
        for t in range(self.n - 1):
            for side, j, passed in ((0, self.n - 1 - t, self.i), (1, t, self.n - 1 - self.i)):
                beyond = self.i < j if side == 0 else self.i > j
                inner = self.i > 0 if side == 0 else self.i < self.n - 1

                @pl.when(jnp.logical_and(beyond, now(base + passed + t)))
                def _(side=side, j=j, inner=inner):
                    for k in range(self.count):
                        if self.n > 2:
                            pl.when(inner)(lambda k=k: self.take(side, j, k))
                        self.copy(side, j, k).start()

    def finish(self):
        for side, inner in ((0, self.i > 0), (1, self.i < self.n - 1)):

            @pl.when(inner)
            def _(side=side):
                for k in range(self.count):
                    self.take(side, self.i, k)

    def drain(self):
        for j in range(self.n):
            for side, beyond in ((0, self.i < j), (1, self.i > j)):

                @pl.when(beyond)
                def _(side=side, j=j):
                    for k in range(self.count):
                        self.copy(side, j, k).wait_send()


def first_columns(wide):
    return wide // LANES // 3 * 2 * LANES


REDUCE_SCRATCH = 17
ACROSS_SCRATCH = 6


def reduce_scratch(parts, rows, columns):
    zs, ys = seq_sides(parts)
    wide = columns // 2
    first = first_columns(wide)
    rest = wide - first
    dma = pltpu.SemaphoreType.DMA
    return [
        pltpu.VMEM((zs, ys, rows, wide), BF),
        pltpu.VMEM((zs, ys, rows, wide), BF),
        pltpu.VMEM((2, ys, zs, rows, first), BF),
        pltpu.VMEM((2, zs, ys, rows, rest), BF),
        pltpu.VMEM((2, zs, 2, rows, first // 2), BF),
        pltpu.VMEM((2, ys, 1, rows, rest), BF),
        dma((zs,)),
        dma((zs,)),
        dma((zs,)),
        dma((2, ys, zs)),
        dma((2, ys, zs)),
        dma((2, zs, ys)),
        dma((2, zs, ys)),
        dma((2, zs, 2)),
        dma((2, zs, 2)),
        dma((2, ys, 1)),
        dma((2, ys, 1)),
    ]


def across_scratch(replicas, rows, columns):
    xs = replicas // 2
    wide = columns // 2
    dma = pltpu.SemaphoreType.DMA
    return [
        pltpu.VMEM((xs, rows, wide), BF),
        pltpu.VMEM((2, rows, wide), F32),
        dma((max(xs - 1, 1), 2)),
        dma((xs, 2)),
        dma,
        dma,
    ]


class Across:
    def __init__(self, place, own, scratch):
        self.place, self.own = place, own
        self.in_x, self.fin, self.s_x, self.g_x, self.s_f, self.g_f = scratch
        self.xs = self.in_x.shape[0]
        self.x = place.dp // 2
        self.peers = [(lax.rem(self.x + t, self.xs) * 2 + place.core, place.seq) for t in range(1, self.xs)]

    def columns(self, piece):
        wide = self.own.shape[-1]
        first = first_columns(wide)
        return pl.ds(first, wide - first) if piece else pl.ds(0, first)

    def copy(self, t, there, piece):
        lanes = self.columns(piece)
        return pltpu.make_async_remote_copy(
            src_ref=self.own.at[:, lanes],
            dst_ref=self.in_x.at[there, :, lanes],
            send_sem=self.s_x.at[t, piece],
            recv_sem=self.g_x.at[there, piece],
            device_id=self.peers[t],
            device_id_type=MESH,
        )

    def half(self, c):
        return pltpu.make_async_remote_copy(
            src_ref=self.fin.at[c],
            dst_ref=self.fin.at[c],
            send_sem=self.s_f,
            recv_sem=self.g_f,
            device_id=self.place.sibling(),
            device_id_type=MESH,
        )

    def start(self, piece):
        for t in range(self.xs - 1):
            self.copy(t, self.x, piece).start()
        lanes = self.columns(piece)
        self.in_x[self.x, :, lanes] = self.own[:, lanes]

    def fold(self):
        for t in range(self.xs - 1):
            for piece in range(2):
                self.copy(t, lax.rem(self.x + t + 1, self.xs), piece).wait_recv()
        total = self.in_x[0].astype(F32)
        for t in range(1, self.xs):
            total = total + self.in_x[t].astype(F32)
        self.fin[self.place.core] = total
        self.half(self.place.core).start()

    def finish(self, out_ref):
        self.half(1 - self.place.core).wait_recv()
        squares = 0.0
        for c in range(2):
            value = self.fin[c]
            out_ref[c] = value
            squares = squares + jnp.sum(value * value, axis=(0, 1), keepdims=True)
        return squares

    def drain(self):
        for t in range(self.xs - 1):
            for piece in range(2):
                self.copy(t, self.x, piece).wait_send()
        self.half(self.place.core).wait_send()


class Reduction:
    def __init__(self, place, grad_ref, scratch):
        self.place, self.grad = place, grad_ref
        self.acc, self.in_c, in_ya, in_zb, in_za, in_yb = scratch[:6]
        self.local, self.s_c, self.g_c, s_ya, g_ya, s_zb, g_zb, s_za, g_za, s_yb, g_yb = scratch[6:]
        acc = self.acc
        zs, ys = place.zs, place.ys
        wide = acc.shape[-1]
        first = first_columns(wide)
        a, b = pl.ds(0, first), pl.ds(first, wide - first)
        self.lanes = pl.ds(pl.multiple_of(place.core * wide, LANES), wide)
        self.other = pl.ds(pl.multiple_of((1 - place.core) * wide, LANES), wide)
        self.line_ya = Line(
            place.y, ys, place.along_y, lambda j, k: acc.at[k, j, :, a], lambda s, j, k: in_ya.at[s, j, k], zs, s_ya, g_ya
        )
        self.line_zb = Line(
            place.z, zs, place.along_z, lambda j, k: acc.at[j, k, :, b], lambda s, j, k: in_zb.at[s, j, k], ys, s_zb, g_zb
        )
        pieces = [pl.ds(k * (first // 2), first // 2) for k in range(2)]
        self.line_za = Line(
            place.z,
            zs,
            place.along_z,
            lambda j, k: acc.at[j, place.y, :, pieces[k]],
            lambda s, j, k: in_za.at[s, j, k],
            2,
            s_za,
            g_za,
        )
        self.line_yb = Line(
            place.y, ys, place.along_y, lambda j, k: acc.at[place.z, j, :, b], lambda s, j, k: in_yb.at[s, j, k], 1, s_yb, g_yb
        )
        self.own = acc.at[place.z, place.y]

    def mine(self, z):
        return pltpu.make_async_copy(self.grad.at[z, :, :, self.lanes], self.acc.at[z], self.local.at[z])

    def swap(self, z):
        return pltpu.make_async_remote_copy(
            src_ref=self.grad.at[z, :, :, self.other],
            dst_ref=self.in_c.at[z],
            send_sem=self.s_c.at[z],
            recv_sem=self.g_c.at[z],
            device_id=self.place.sibling(),
            device_id_type=MESH,
        )

    def open(self, greeting):
        for z in range(self.place.zs):
            self.mine(z).start()
        greeting()
        for z in range(self.place.zs):
            self.swap(z).start()

    def fold_cores(self):
        for z in range(self.place.zs):
            self.mine(z).wait()
            self.swap(z).wait_recv()
            for y in range(self.place.ys):
                add_into(self.acc.at[z, y], self.in_c.at[z, y])
            if self.place.ys == 2:
                self.line_ya.send_pair(z)

    def advance(self, slot, last):
        def now(time):
            return slot == jnp.minimum(time, last)

        zs, ys = self.place.zs, self.place.ys
        pl.when(now(0))(lambda: self.open(lambda: greet(self.place)))
        pl.when(now(1))(self.fold_cores)
        if ys != 2:
            self.line_ya.send(now, 1)
        self.line_zb.send(now, 1)
        ready = max(zs, ys + 1)
        pl.when(now(ready))(self.line_zb.finish)
        self.line_yb.send(now, ready)
        pl.when(now(ready))(self.line_ya.finish)
        self.line_za.send(now, ready)

    def finish(self):
        self.line_yb.finish()
        self.line_za.finish()

    def drain(self):
        for line in (self.line_ya, self.line_zb, self.line_za, self.line_yb):
            line.drain()
        for z in range(self.place.zs):
            self.swap(z).wait_send()


def reduce_kernel(parts, grad_ref, band_ref, out_ref, norm_ref, squares, s_n, g_n, *scratch):
    place = Place(parts)
    peers = [(place.dp, lax.rem(place.seq + t, parts)) for t in range(1, parts)]
    reduction = Reduction(place, grad_ref, scratch[:REDUCE_SCRATCH])
    band = Across(place, band_ref, scratch[REDUCE_SCRATCH : REDUCE_SCRATCH + ACROSS_SCRATCH])
    time = Across(place, reduction.own, scratch[REDUCE_SCRATCH + ACROSS_SCRATCH :])

    def greeting():
        barrier = pltpu.get_barrier_semaphore()
        everyone = [place.sibling()] + time.peers + peers
        for to in everyone:
            pl.semaphore_signal(barrier, inc=1, device_id=to, device_id_type=MESH)
        pl.semaphore_wait(barrier, len(everyone))

    def always(time):
        return True

    reduction.open(greeting)
    reduction.fold_cores()
    band.start(0)
    band.start(1)
    if place.ys != 2:
        reduction.line_ya.send(always, 0)
    reduction.line_zb.send(always, 0)
    reduction.line_zb.finish()
    reduction.line_yb.send(always, 0)
    band.fold()
    reduction.line_ya.finish()
    reduction.line_za.send(always, 0)
    reduction.line_yb.finish()
    time.start(1)
    partial_sum = band.finish(out_ref.at[1])
    reduction.line_za.finish()
    time.start(0)
    time.fold()
    partial_sum = partial_sum + time.finish(out_ref.at[0])
    squares[place.seq] = jnp.broadcast_to(partial_sum, squares.shape[1:])

    def tell(t, there):
        return pltpu.make_async_remote_copy(
            src_ref=squares.at[there],
            dst_ref=squares.at[there],
            send_sem=s_n.at[t],
            recv_sem=g_n.at[there],
            device_id=peers[t],
            device_id_type=MESH,
        )

    for t in range(parts - 1):
        tell(t, place.seq).start()
    for t in range(parts - 1):
        tell(t, lax.rem(place.seq + t + 1, parts)).wait_recv()
    norm = squares[0]
    for p in range(1, parts):
        norm = norm + squares[p]
    norm_ref[...] = norm
    for t in range(parts - 1):
        tell(t, place.seq).wait_send()
    reduction.drain()
    band.drain()
    time.drain()


def reduce_gradient(grad, band, parts, replicas):
    zs, ys = seq_sides(parts)
    rows, columns = grad.shape[0] // parts, grad.shape[1]
    dma = pltpu.SemaphoreType.DMA
    in_vmem = pl.BlockSpec(memory_space=pltpu.VMEM)
    return pl.pallas_call(
        partial(reduce_kernel, parts),
        in_specs=[pl.BlockSpec(memory_space=pl.ANY), in_vmem],
        out_specs=[in_vmem, in_vmem],
        out_shape=[
            jax.ShapeDtypeStruct((2, 2, rows, columns // 2), F32),
            jax.ShapeDtypeStruct((8, LANES), F32),
        ],
        scratch_shapes=[pltpu.VMEM((parts, 8, LANES), F32), dma((parts - 1,)), dma((parts,))]
        + reduce_scratch(parts, rows, columns)
        + across_scratch(replicas, rows, columns) * 2,
        compiler_params=params(collective_id=2, has_side_effects=True),
        cost_estimate=pl.CostEstimate(flops=0, bytes_accessed=columns * rows * parts * 60, transcendentals=0),
        name="reduce_gradient",
    )(grad.reshape(zs, ys, rows, columns), band)


def rotary_order(columns):
    lead = columns.shape[:-1]
    split = columns.reshape(lead + (-1, 4, 2, HEAD_DIM // 2))
    return jnp.swapaxes(split, -3, -2).reshape(columns.shape)


def adam_step(master, gradient, first_old, second_old, learn_rate):
    first_new = BETA_ONE * first_old + (1.0 - BETA_ONE) * gradient
    second_new = BETA_TWO * second_old + (1.0 - BETA_TWO) * gradient * gradient
    first_hat = first_new / (1.0 - BETA_ONE**STEP)
    second_hat = second_new / (1.0 - BETA_TWO**STEP)
    updated = master - learn_rate * (first_hat / (jnp.sqrt(second_hat) + ADAM_EPS) + DECAY * master)
    return (updated, first_new, second_new)


def heads_in_order(first, second):
    half = HEAD_DIM // 2
    lane = iota(first.shape, 1) // half

    def turn(t, places):
        return pltpu.roll(t, places % LANES, 1) if places % LANES else t

    results = []
    for low in (0, 2):
        pieces = [turn(first, -low * half), turn(second, half - low * half)]
        pieces += [turn(first, half - low * half), turn(second, 2 * half - low * half)]
        out = pieces[0]
        for place in range(1, 4):
            out = jnp.where(lane == place, pieces[place], out)
        results.append(out)
    return results


def update_kernel(grads_ref, squares_ref, *refs):
    masters, firsts, seconds = refs[0:2], refs[2:4], refs[4:6]
    outs = refs[6:]
    norm = jnp.sqrt(squares_ref[0:1, 0:1])
    factor = jnp.minimum(1.0, CLIP_NORM / (norm + 1e-06))
    half = grads_ref.shape[2]
    width_in, width_out = (ref.shape[1] for ref in masters)

    def gradient(start, size):
        return grads_ref[start // half, :, start % half : start % half + size] * factor

    def update(which, column, size, grad, rate):
        part = slice(column, column + size)
        new = adam_step(
            masters[which][:, part], grad, firsts[which][:, part], seconds[which][:, part], rate
        )
        for k in range(3):
            outs[2 * k + which][:, part] = new[k]
        outs[6 + which][:, part] = new[0].astype(BF)

    for start in range(0, 2 * INNER_WIDTH, GROUP):
        pair = heads_in_order(gradient(start, LANES), gradient(start + LANES, LANES))
        for n in range(2):
            update(0, start + n * LANES, LANES, pair[n], RATE_MATRIX)
    for which, width, base, begin in ((0, width_in, 0, 2 * INNER_WIDTH), (1, width_out, width_in, 0)):
        for column in range(begin, width, LANES):
            update(which, column, LANES, gradient(base + column, LANES), RATE_MATRIX)


def update_weights(grads, squares, masters, firsts, seconds):
    states = [*masters, *firsts, *seconds]

    def by_layer(t):
        return pl.BlockSpec((None,) + t.shape[1:], lambda i: (i, 0, 0))

    return pl.pallas_call(
        update_kernel,
        grid=(2,),
        in_specs=[pl.BlockSpec((None,) + grads.shape[1:], lambda i: (i, 0, 0, 0)), whole(squares.shape)]
        + [by_layer(t) for t in states],
        out_specs=[by_layer(t) for t in states + list(masters)],
        out_shape=[jax.ShapeDtypeStruct(t.shape, F32) for t in states]
        + [jax.ShapeDtypeStruct(t.shape, BF) for t in masters],
        compiler_params=params(),
        name="update_weights",
    )(grads, squares, *states)


def body(
    activations,
    cotangent,
    lengths,
    weight_in,
    weight_out,
    weight_small,
    first_in,
    first_out,
    first_small,
    second_in,
    second_out,
    second_small,
):
    parts = lax.axis_size("seq")
    micro, unused, band_dev, frames, model = activations.shape
    bands, frame_dev = cotangent.shape[2], cotangent.shape[3]
    turned = 2 * INNER_WIDTH
    width_in, width_out = weight_in.shape[2], weight_out.shape[2]
    width_ff = width_in - 3 * INNER_WIDTH
    small_width = weight_small.shape[2]
    packed = [
        jnp.concatenate(
            [
                rotary_order(weight_in[layer, :, :turned].astype(BF)),
                weight_in[layer, :, turned:].astype(BF),
                weight_out[layer].astype(BF),
                jnp.pad(weight_small[layer].astype(BF), ((0, 0), (0, SMALL_LANES - small_width))),
            ],
            axis=1,
        )
        for layer in range(2)
    ]
    time_weights = gather_weights(packed[0], parts)
    time_tables = rotary_tables(frames, sequences(band_dev) * frames)
    band_tables = rotary_tables(bands, min(2 * BLOCK, frame_dev * bands))

    def exchange(tensor):
        return lax.all_to_all(tensor, "seq", split_axis=0, concat_axis=0, tiled=True)

    streams, saves, other = [], [], packed[1]
    for m in range(micro):
        ride = "lines" if m == 0 else "pass" if m == 1 else ""
        out, saved, other = time_forward(
            m, activations, lengths, time_weights, time_tables, ride, other, parts, width_ff
        )
        saves.append(saved)
        streams.append(exchange(out).reshape(bands, frame_dev, model))
    band_weights = other.reshape(model, -1)
    backs, before = [], ()
    for m in range(micro):
        kind = BF if m == micro - 1 else F32
        output, back, grad_band = band_both(
            m, streams[m], cotangent, lengths, band_weights, band_tables, before, kind, width_ff
        )
        before = (grad_band, output)
        backs.append(exchange(back.reshape(parts, band_dev, frame_dev, model)))
    before = ()
    for m in range(micro):
        kind = BF if m == micro - 1 else F32
        part, grad_time, *shard = time_backward(
            m,
            activations,
            backs[m],
            time_weights,
            time_tables,
            saves[m],
            before,
            grad_band if m == micro - 1 else None,
            kind,
            width_ff,
        )
        if m < micro - 1:
            d_input = part
            before = (grad_time, d_input)
        else:
            d_input = lax.dynamic_update_slice(d_input, part, (m, 0, 0, 0, 0))
    grads, squares = reduce_gradient(grad_time, shard[0], parts, lax.axis_size("dp"))
    new = update_weights(grads, squares, (weight_in, weight_out), (first_in, first_out), (second_in, second_out))
    norm = jnp.sqrt(squares[0, 0])
    factor = jnp.minimum(1.0, CLIP_NORM / (norm + 1e-06))
    start = width_in + width_out - grads.shape[3]
    rate = jnp.where(jnp.arange(small_width) < HEAD_COUNT, RATE_GATE, RATE_GAIN)
    small = adam_step(
        weight_small, grads[:, 1, :, start : start + small_width] * factor, first_small, second_small, rate
    )
    return (
        output,
        d_input,
        norm,
        new[0],
        new[1],
        small[0],
        new[2],
        new[3],
        small[1],
        new[4],
        new[5],
        small[2],
        new[6],
        new[7],
        small[0].astype(BF),
    )


def solution(mesh):
    by_seq = P(None, "seq", None)
    by_band = P(None, "dp", "seq", None, None)
    by_frame = P(None, "dp", None, "seq", None)
    return jax.shard_map(
        body,
        mesh=mesh,
        in_specs=(by_band, by_frame, P(None, "dp")) + (by_seq,) * 9,
        out_specs=(by_frame, by_band, P()) + (by_seq,) * 12,
        check_vma=False,
    )
```

```python
from functools import partial
import math

import jax
import jax.numpy as jnp
import numpy as np
from jax import lax
from jax.experimental import pallas as pl
from jax.experimental.pallas import tpu as pltpu
from jax.sharding import PartitionSpec as P

HEAD_COUNT = 8
HEAD_DIM = 64
INNER_WIDTH = 512
STEP = 10
EPS_NORM = 1e-06
BETA_ONE = 0.9
BETA_TWO = 0.999
ADAM_EPS = 1e-08
DECAY = 0.1
RATE_MATRIX = 0.1
RATE_GATE = 0.1
RATE_GAIN = 0.5
CLIP_NORM = 1.0
MASKED = -1e30

BF = jnp.bfloat16
F32 = jnp.float32
GROUP = 256
BLOCK = 256
LANES = 128
SMALL_LANES = 2 * LANES
LOG2E = 1.4426950408889634
SCORE_EXP = LOG2E / math.sqrt(HEAD_DIM)
SQRT_HALF = math.sqrt(0.5)
GAUSS = 1.0 / math.sqrt(2.0 * math.pi)
VMEM_LIMIT = 60 * 2**20


def nn(a, b):
    return lax.dot_general(a, b, (((1,), (0,)), ((), ())), preferred_element_type=F32)


def nt(a, b):
    return lax.dot_general(a, b, (((1,), (1,)), ((), ())), preferred_element_type=F32)


def tn(a, b):
    return lax.dot_general(a, b, (((0,), (0,)), ((), ())), preferred_element_type=F32)


def iota(shape, dim):
    return lax.broadcasted_iota(jnp.int32, shape, dim)


def split_rows(rows):
    high = rows.astype(BF)
    rest = (rows - high.astype(F32)).astype(BF)
    return jnp.concatenate([high, rest], axis=0)


def head_lanes():
    shape = (2 * HEAD_COUNT, INNER_WIDTH)
    return (iota(shape, 1) // HEAD_DIM == iota(shape, 0) % HEAD_COUNT).astype(F32).astype(BF)


def inverse_rms(rows):
    return lax.rsqrt(jnp.mean(rows * rows, axis=-1, keepdims=True) + EPS_NORM)


def norm_back(rows, gain, grad):
    inverse = inverse_rms(rows)
    unit = rows * inverse
    scaled = grad * gain
    d_rows = inverse * (scaled - unit * jnp.mean(scaled * unit, axis=-1, keepdims=True))
    return d_rows, jnp.sum(grad * unit, axis=0, keepdims=True)


def half_lanes(h):
    return (iota((BLOCK, GROUP), 1) % LANES) // (HEAD_DIM // 2) == h


def whole_lanes(h):
    return iota((BLOCK, GROUP), 1) // HEAD_DIM == h


def picked(mask, tensor):
    return jnp.where(mask, tensor, jnp.zeros_like(tensor))


def group_slice(g):
    return slice(g * GROUP, (g + 1) * GROUP)


def forward_block(x, w_ref, small, cos, sin, bias_ref, keep, start, item, width_ff, tick=None):
    gate_weight, gain_attn, gain_ff = small
    size = x.shape[0]
    rows = pl.ds(start, size)
    normed = (x * inverse_rms(x) * gain_attn).astype(BF)
    if "normed" in keep:
        keep["normed"][rows, :] = normed
    gate_rows = jax.nn.sigmoid(nt(gate_weight, normed))
    keep["gate"][:, rows] = gate_rows
    half = GROUP // 2
    for g in range(2):
        for part, name in ((0, "q"), (1, "k")):
            column = part * INNER_WIDTH + g * GROUP
            t = nn(normed, w_ref[:, column : column + GROUP])
            a, b = t[:, :half], t[:, half:]
            keep[name][rows, g * GROUP : g * GROUP + half] = (a * cos - b * sin).astype(BF)
            keep[name][rows, g * GROUP + half : (g + 1) * GROUP] = (b * cos + a * sin).astype(BF)
        column = 2 * INNER_WIDTH + g * GROUP
        keep["v"][rows, group_slice(g)] = nn(normed, w_ref[:, column : column + GROUP]).astype(BF)
    gate = tn(split_rows(gate_rows), head_lanes())
    for n in range(size // BLOCK):
        if tick and n == size // BLOCK - 1:
            tick()
        block = pl.ds(start + n * BLOCK, BLOCK)
        for g in range(2):
            lanes = group_slice(g)
            queries, keys = keep["q"][block, lanes], keep["k"][block, lanes]
            values = keep["v"][block, lanes]
            parts, heads = [], []
            for h in range(4):
                scores = nt(picked(half_lanes(h), keys), queries) + bias_ref[...]
                peak = jnp.max(scores, axis=0, keepdims=True)
                terms = jnp.exp2((scores - peak) * SCORE_EXP)
                probs = (terms * (1.0 / jnp.sum(terms, axis=0, keepdims=True))).astype(BF)
                keep["probs"][item + n, g * 4 + h] = probs
                parts.append(probs)
                heads.append(picked(whole_lanes(h), values))
            attended = tn(jnp.concatenate(parts, axis=0), jnp.concatenate(heads, axis=0))
            keep["gated"][block, lanes] = (attended * gate[n * BLOCK : (n + 1) * BLOCK, lanes]).astype(BF)
    out_start = 3 * INNER_WIDTH + width_ff
    middle = x + nt(keep["gated"][rows, :], w_ref[:, out_start : out_start + INNER_WIDTH])
    keep["middle"][rows, :] = middle
    normed_ff = (middle * inverse_rms(middle) * gain_ff).astype(BF)
    if "normed_ff" in keep:
        keep["normed_ff"][rows, :] = normed_ff
    result = middle
    for c in range(width_ff // GROUP):
        up = 3 * INNER_WIDTH + c * GROUP
        down = out_start + INNER_WIDTH + c * GROUP
        hidden = nn(normed_ff, w_ref[:, up : up + GROUP])
        cumulative = 0.5 + 0.5 * lax.erf(hidden * SQRT_HALF)
        activated = (hidden * cumulative).astype(BF)
        density = jnp.exp2(hidden * hidden * (-0.5 * LOG2E)) * GAUSS
        keep["act"][rows, group_slice(c)] = activated
        keep["slope"][rows, group_slice(c)] = (cumulative + hidden * density).astype(BF)
        result = result + nt(activated, w_ref[:, down : down + GROUP])
    return result


def backward_block(d_out, x, w_ref, small, cos, sin, keep, work, sums, start, item, width_ff, tick=None):
    gate_weight, gain_attn, gain_ff = small
    size = x.shape[0]
    rows = pl.ds(start, size)
    branch = d_out.astype(BF)
    work["branch"][rows, :] = branch
    out_start = 3 * INNER_WIDTH + width_ff
    d_normed_ff = None
    for c in range(width_ff // GROUP):
        up = 3 * INNER_WIDTH + c * GROUP
        down = out_start + INNER_WIDTH + c * GROUP
        d_act = nn(branch, w_ref[:, down : down + GROUP])
        d_hidden = (d_act * keep["slope"][rows, group_slice(c)].astype(F32)).astype(BF)
        work["d_hidden"][rows, group_slice(c)] = d_hidden
    up = 3 * INNER_WIDTH
    d_normed_ff = nt(work["d_hidden"][rows, :], w_ref[:, up : up + width_ff])
    middle = keep["middle"][rows, :]
    d_rows, d_gain_ff = norm_back(middle, gain_ff, d_normed_ff)
    d_middle = d_out + d_rows
    attn_back = d_middle.astype(BF)
    work["attn_back"][rows, :] = attn_back
    gate_rows = keep["gate"][:, rows]
    lanes_of = head_lanes()
    gate = tn(split_rows(gate_rows), lanes_of)
    d_gated = nn(attn_back, w_ref[:, out_start : out_start + INNER_WIDTH])
    product = d_gated * keep["gated"][rows, :].astype(F32)
    high = product.astype(BF)
    rest = (product - high.astype(F32)).astype(BF)
    delta_rows = (nt(lanes_of, high) + nt(lanes_of, rest))[:HEAD_COUNT]
    d_logit = split_rows(delta_rows * (1.0 - gate_rows))
    d_attended = (d_gated * gate).astype(BF)
    half = GROUP // 2
    scale = HEAD_DIM**-0.5
    for n in range(size // BLOCK):
        if tick and n == size // BLOCK - 1:
            tick()
        block = pl.ds(start + n * BLOCK, BLOCK)
        inner = slice(n * BLOCK, (n + 1) * BLOCK)
        for g in range(2):
            lanes = group_slice(g)
            queries, keys = keep["q"][block, lanes], keep["k"][block, lanes]
            values, d_att = keep["v"][block, lanes], d_attended[inner, lanes]
            p_list, s_list, q_list, a_list, k_list = [], [], [], [], []
            for h in range(4):
                halves, wholes = half_lanes(h), whole_lanes(h)
                probs = keep["probs"][item + n, g * 4 + h]
                d_probs = nt(picked(wholes, values), d_att)
                delta = delta_rows[g * 4 + h : g * 4 + h + 1, inner]
                d_scores = (probs.astype(F32) * (d_probs - delta)).astype(BF)
                p_list.append(probs)
                s_list.append(d_scores)
                a_list.append(picked(wholes, d_att))
                q_list.append(picked(halves, queries))
                k_list.append(picked(halves, keys))
            d_values = nn(jnp.concatenate(p_list, axis=1), jnp.concatenate(a_list, axis=0))
            d_keys = nn(jnp.concatenate(s_list, axis=1), jnp.concatenate(q_list, axis=0))
            d_query = tn(jnp.concatenate(s_list, axis=0), jnp.concatenate(k_list, axis=0))
            for column, t in ((0, d_query), (INNER_WIDTH, d_keys)):
                t = t * scale
                a, b = t[:, :half], t[:, half:]
                c, s = cos[inner], sin[inner]
                column = column + g * GROUP
                work["d_proj"][block, column : column + half] = (a * c + b * s).astype(BF)
                work["d_proj"][block, column + half : column + GROUP] = (b * c - a * s).astype(BF)
            column = 2 * INNER_WIDTH + g * GROUP
            work["d_proj"][block, column : column + GROUP] = d_values.astype(BF)
    twice = jnp.concatenate([gate_weight, gate_weight], axis=0)
    d_normed = tn(d_logit, twice)
    for c in range(3 * INNER_WIDTH // INNER_WIDTH):
        part = slice(c * INNER_WIDTH, (c + 1) * INNER_WIDTH)
        d_normed = d_normed + nt(work["d_proj"][rows, part], w_ref[:, part])
    d_rows, d_gain_attn = norm_back(x, gain_attn, d_normed)
    d_gate = nn(d_logit, work["normed"][rows, :])
    sums[0:HEAD_COUNT, :] += d_gate[:HEAD_COUNT] + d_gate[HEAD_COUNT:]
    sums[HEAD_COUNT : HEAD_COUNT + 1, :] += d_gain_attn
    sums[HEAD_COUNT + 1 : HEAD_COUNT + 2, :] += d_gain_ff
    return d_middle + d_rows


def weight_sums(total, work, keep, width_ff, done=None):
    out_start = 3 * INNER_WIDTH + width_ff
    pairs = (
        (work["normed"], work["d_proj"], 0),
        (work["normed_ff"], work["d_hidden"], 3 * INNER_WIDTH),
        (work["attn_back"], keep["gated"], out_start),
        (work["branch"], keep["act"], out_start + INNER_WIDTH),
    )
    for left, right, start in pairs:
        turned = left[...].T
        for c in range(right.shape[-1] // INNER_WIDTH):
            part = slice(start + c * INNER_WIDTH, start + (c + 1) * INNER_WIDTH)
            total[:, part] += nn(turned, right[:, c * INNER_WIDTH : (c + 1) * INNER_WIDTH])
        if done:
            done(start)


def sections(width, width_ff):
    cuts = [0, 3 * INNER_WIDTH, 3 * INNER_WIDTH + width_ff, 4 * INNER_WIDTH + width_ff, 4 * INNER_WIDTH + 2 * width_ff, width]
    return [slice(a, b) for a, b in zip(cuts[:-1], cuts[1:])]


def masked_keys(valid):
    return jnp.where(valid, 0.0, MASKED).astype(F32)


def turn_small(w_ref, small_ref):
    width = w_ref.shape[1] - SMALL_LANES
    rows = w_ref[:, width : width + LANES].astype(F32).T
    small_ref[...] = rows[: small_ref.shape[0]]


def small_parts(small_ref):
    gate_weight = small_ref[0:HEAD_COUNT, :].astype(BF)
    return (
        gate_weight,
        small_ref[HEAD_COUNT : HEAD_COUNT + 1, :],
        small_ref[HEAD_COUNT + 1 : HEAD_COUNT + 2, :],
    )


class Outgoing:
    def __init__(self, total, out_ref, sems, width_ff, last):
        self.total, self.out, self.sems, self.last = total, out_ref, sems, last
        self.parts = sections(total.shape[1], width_ff)

    def copy(self, n):
        part = self.parts[n]
        return pltpu.make_async_copy(self.total.at[:, part], self.out.at[:, part], self.sems.at[n])

    def done(self, start):
        number = [part.start for part in self.parts].index(start)
        pl.when(self.last)(lambda: self.copy(number).start())


def finish_sums(total, sums, out_ref, outgoing):
    width = total.shape[1] - SMALL_LANES
    model = total.shape[0]
    tall = jnp.concatenate([sums[...], jnp.zeros((SMALL_LANES - sums.shape[0], model), F32)], axis=0)
    if outgoing:
        total[:, width:] = tall.T
        outgoing.copy(4).start()
        for n in range(5):
            outgoing.copy(n).wait()
    else:
        out_ref[:, :width] = total[:, :width].astype(out_ref.dtype)
        out_ref[:, width:] = tall.T.astype(out_ref.dtype)


def start_sums(total, sums, before_ref, arrival):
    sums[...] = jnp.zeros_like(sums)
    if before_ref is None:
        total[...] = jnp.zeros_like(total)
    else:
        pltpu.make_async_copy(before_ref, total, arrival).start()


def await_sums(total, sums, before_ref, arrival):
    if before_ref is not None:
        width = total.shape[1] - SMALL_LANES
        pltpu.make_async_copy(before_ref, total, arrival).wait()
        sums[...] += total[:, width:].T[: sums.shape[0]]


SAVED = ("q", "k", "v", "gate", "probs", "gated", "middle", "act", "slope")


def time_forward_kernel(parts, width_ff, ride, m, x_ref, w_ref, cos_ref, sin_ref, len_ref, *refs):
    step, steps = pl.program_id(0), pl.num_programs(0)
    tick, gather = None, None
    if ride:
        shard_ref, out_ref, refs, full_ref = refs[0], refs[1], refs[2:], refs[11]
        sems = refs[-GATHER_SCRATCH:]
        small_ref, bias_ref = refs[-GATHER_SCRATCH - 2 : -GATHER_SCRATCH]
        if ride == "lines":
            gather = Gather(Place(parts), shard_ref, full_ref, *sems, at_once=False)
            pl.when(step == 0)(gather.start)
            gather.advance(2 * step, 2 * steps)
            tick = partial(gather.advance, 2 * step + 1, 2 * steps)
        else:
            gather = Gather(Place(parts), None, full_ref, *sems)
            pl.when(step == 0)(gather.open_passing)
            pl.when(step == steps - 1)(gather.pass_taken)
    else:
        out_ref, refs = refs[0], refs[1:]
        small_ref, bias_ref = refs[-2:]
    keep = dict(zip(SAVED, refs))

    @pl.when(step == 0)
    def _():
        turn_small(w_ref, small_ref)
        bias_ref[...] = masked_keys(iota((BLOCK, BLOCK), 0) < len_ref[:, m : m + 1])

    per_step, whole_frames, model = x_ref.shape
    x = x_ref[...].astype(F32).reshape(per_step * whole_frames, model)
    out = forward_block(
        x, w_ref, small_parts(small_ref), cos_ref[...], sin_ref[...], bias_ref, keep, 0, 0, width_ff, tick
    )
    frames = out_ref.shape[2]
    for n in range(per_step):
        out_ref[:, n] = out[n * whole_frames : (n + 1) * whole_frames].reshape(parts, frames, model).astype(BF)

    @pl.when(step == steps - 1)
    def _():
        if ride == "lines":
            gather.other_lines()
            gather.finish_lines()
        elif ride:
            gather.finish_passing()


def time_backward_kernel(parts, width_ff, chained, ride, per_step, *refs):
    x_ref, d_ref, w_ref, cos_ref, sin_ref = refs[:5]
    keep = dict(zip(SAVED, refs[5:14]))
    refs = refs[14:]
    before = refs[0] if chained else None
    refs = refs[2 - ride :] if chained else refs
    step, steps = pl.program_id(0), pl.num_programs(0)
    if ride:
        other_ref, dx_ref, grad_ref, shard_ref = refs[:4]
        reduction = Reduction(Place(parts), other_ref, refs[-REDUCE_SCRATCH:])
        refs = refs[:-REDUCE_SCRATCH]
    else:
        dx_ref, grad_ref = refs[:2]
    total, sums, normed, normed_ff, d_hidden, attn_back, branch, d_proj, arrival, small_ref, o_sems = refs[-11:]
    outgoing = Outgoing(total, grad_ref, o_sems, width_ff, step == steps - 1) if grad_ref.dtype == F32 else None
    work = dict(
        normed=normed, normed_ff=normed_ff, d_hidden=d_hidden, attn_back=attn_back, branch=branch, d_proj=d_proj
    )

    @pl.when(step == 0)
    def _():
        start_sums(total, sums, before, arrival)
        turn_small(w_ref, small_ref)

    small = small_parts(small_ref)
    if ride:
        reduction.advance(2 * step, 2 * steps - 1)
    model = x_ref.shape[2]
    x = x_ref[...].astype(F32).reshape(per_step * BLOCK, model)
    work["normed"][...] = (x * inverse_rms(x) * small[1]).astype(BF)
    middle = keep["middle"][...]
    work["normed_ff"][...] = (middle * inverse_rms(middle) * small[2]).astype(BF)
    d_out = jnp.concatenate([d_ref[:, i].astype(F32).reshape(BLOCK, model) for i in range(per_step)], axis=0)
    d_x = backward_block(
        d_out, x, w_ref, small, cos_ref[...], sin_ref[...], keep, work, sums, 0, 0, width_ff,
        partial(reduction.advance, 2 * step + 1, 2 * steps - 1) if ride else None,
    )
    dx_ref[...] = d_x.reshape(dx_ref.shape)
    if chained:

        @pl.when(step == 0)
        def _():
            await_sums(total, sums, before, arrival)

    weight_sums(total, work, keep, width_ff, outgoing.done if outgoing else None)

    @pl.when(step == steps - 1)
    def _():
        finish_sums(total, sums, grad_ref, outgoing)
        if ride:
            reduction.finish()
            shard_ref[...] = reduction.own[...]
            reduction.drain()


def gather_rows(ref, strides, factors):
    return jnp.concatenate(
        [
            jnp.concatenate([ref[p, s, :] * f for p in range(ref.shape[0])], axis=1)
            for s, f in zip(strides, factors)
        ],
        axis=0,
    )


def band_kernel(width_ff, chained, m, len_ref, *refs):
    x_ref, d_ref, w_ref, cos_ref, sin_ref = refs[:5]
    refs = refs[5:]
    before = refs[0] if chained else None
    out_ref, back_ref, grad_ref = refs[2:5] if chained else refs[:3]
    scratch = refs[-23:]
    keep = dict(zip(SAVED, scratch[:9]))
    total, sums, normed, normed_ff, d_hidden, attn_back, branch, d_proj, arrival, small_ref, o_sems, rows_a, rows_b, bias_ref = scratch[9:]
    work = dict(
        normed=normed, normed_ff=normed_ff, d_hidden=d_hidden, attn_back=attn_back, branch=branch, d_proj=d_proj
    )
    keep.update(normed=normed, normed_ff=normed_ff)
    step = pl.program_id(0)
    bands, frames, model = x_ref.shape
    pieces = model // LANES
    last = step == pl.num_programs(0) - 1
    outgoing = Outgoing(total, grad_ref, o_sems, width_ff, last) if grad_ref.dtype == F32 else None

    @pl.when(step == 0)
    def _():
        start_sums(total, sums, before, arrival)
        turn_small(w_ref, small_ref)
        same = iota((BLOCK, BLOCK), 0) // bands == iota((BLOCK, BLOCK), 1) // bands
        bias_ref[...] = masked_keys(same)

    small = small_parts(small_ref)
    for p in range(pieces):
        lanes = slice(p * LANES, (p + 1) * LANES)
        rows_a[p] = x_ref[:, :, lanes].astype(F32).reshape(bands * frames, LANES)
        rows_b[p] = d_ref[:, :, lanes].astype(F32).reshape(bands * frames, LANES)
    first = (lax.axis_index("seq") * pl.num_programs(0) + step) * frames

    size = cos_ref.shape[0]
    spread = size // bands

    def one(j, carry):
        start = pl.multiple_of(j * size, size)
        item = j * (size // BLOCK)
        strides = [pl.ds(j * spread + f, bands, stride=frames) for f in range(spread)]
        valid = [(first + j * spread + f < len_ref[0, m]).astype(F32) for f in range(spread)]
        x = gather_rows(rows_a, strides, [1.0] * spread)
        d_out = gather_rows(rows_b, strides, valid)
        out = forward_block(
            x, w_ref, small, cos_ref[...], sin_ref[...], bias_ref, keep, start, item, width_ff
        )
        for f in range(spread):
            for p in range(pieces):
                part = out[f * bands : (f + 1) * bands, p * LANES : (p + 1) * LANES]
                rows_a[p, strides[f], :] = part * valid[f]
        back = backward_block(
            d_out, x, w_ref, small, cos_ref[...], sin_ref[...], keep, work, sums, start, item, width_ff
        )
        for f in range(spread):
            for p in range(pieces):
                part = back[f * bands : (f + 1) * bands, p * LANES : (p + 1) * LANES]
                rows_b[p, strides[f], :] = part
        return carry

    lax.fori_loop(0, bands * frames // size, one, 0)
    for p in range(pieces):
        lanes = slice(p * LANES, (p + 1) * LANES)
        out_ref[:, :, lanes] = rows_a[p].reshape(bands, frames, LANES).astype(BF)
        back_ref[:, :, lanes] = rows_b[p].reshape(bands, frames, LANES).astype(BF)
    if chained:

        @pl.when(step == 0)
        def _():
            await_sums(total, sums, before, arrival)

    weight_sums(total, work, keep, width_ff, outgoing.done if outgoing else None)

    @pl.when(step == pl.num_programs(0) - 1)
    def _():
        finish_sums(total, sums, grad_ref, outgoing)


def whole(shape):
    return pl.BlockSpec(shape, lambda *i: (0,) * len(shape), pipeline_mode=pl.Buffered(1))


def params(**more):
    return pltpu.CompilerParams(vmem_limit_bytes=VMEM_LIMIT, **more)


def rotary_tables(positions, rows):
    half_width = HEAD_DIM // 2
    inverse = np.float32(10000.0) ** (-(np.arange(half_width, dtype=np.float32) * np.float32(2.0 / HEAD_DIM)))
    angles = np.arange(positions, dtype=np.float32)[:, None] * inverse[None, :].astype(np.float32)
    angles = np.tile(angles, (rows // positions, LANES // half_width))
    return (jnp.asarray(np.cos(angles), F32), jnp.asarray(np.sin(angles), F32))


def saved_shapes(tokens, items, model, width_ff):
    return (
        ((tokens, INNER_WIDTH), BF),
        ((tokens, INNER_WIDTH), BF),
        ((tokens, INNER_WIDTH), BF),
        ((HEAD_COUNT, tokens), F32),
        ((items, HEAD_COUNT, BLOCK, BLOCK), BF),
        ((tokens, INNER_WIDTH), BF),
        ((tokens, model), F32),
        ((tokens, width_ff), BF),
        ((tokens, width_ff), BF),
    )


def saved_specs(tokens, items, model, width_ff):
    def place(shape):
        if shape[0] == HEAD_COUNT:
            return pl.BlockSpec(shape, lambda i, *s: (0, i))
        return pl.BlockSpec(shape, lambda i, *s: (i,) + (0,) * (len(shape) - 1))

    return [place(shape) for shape, kind in saved_shapes(tokens, items, model, width_ff)]


def work_shapes(tokens, model, width_ff, columns):
    return [
        pltpu.VMEM((model, columns), F32),
        pltpu.VMEM((2 * HEAD_COUNT, model), F32),
        pltpu.VMEM((tokens, model), BF),
        pltpu.VMEM((tokens, model), BF),
        pltpu.VMEM((tokens, width_ff), BF),
        pltpu.VMEM((tokens, model), BF),
        pltpu.VMEM((tokens, model), BF),
        pltpu.VMEM((tokens, 3 * INNER_WIDTH), BF),
        pltpu.SemaphoreType.DMA,
        pltpu.VMEM((2 * HEAD_COUNT, model), F32),
        pltpu.SemaphoreType.DMA((5,)),
    ]


def at_micro(m, shape, place):
    return pl.BlockSpec((None, None) + shape, lambda i, *s: (m, 0) + place(i))


def sequences(seqs):
    return 2 if seqs % 2 == 0 else 1


def time_forward(m, x, lengths, weights, tables, ride, other, parts, width_ff):
    seqs, frames, model = x.shape[2:]
    tokens = seqs * frames
    shapes = saved_shapes(tokens, seqs, model, width_ff)
    out = jax.ShapeDtypeStruct((parts, seqs, frames // parts, model), BF)
    per_step = sequences(seqs)
    any_space = pl.BlockSpec(memory_space=pl.ANY)
    riding = 1 if ride else 0
    full = [jax.ShapeDtypeStruct((parts,) + other.shape[-2:], BF)] * riding
    aliases = {5: 1 + len(SAVED)} if ride == "pass" else {}
    results = pl.pallas_call(
        partial(time_forward_kernel, parts, width_ff, ride, m),
        grid=(seqs // per_step,),
        in_specs=[
            at_micro(m, (per_step, frames, model), lambda i: (i, 0, 0)),
            whole(weights.shape),
            whole(tables[0].shape),
            whole(tables[1].shape),
            whole(lengths.shape),
        ]
        + [any_space] * riding,
        out_specs=[
            pl.BlockSpec((parts, per_step, frames // parts, model), lambda i: (0, i, 0, 0)),
            *saved_specs(per_step * frames, per_step, model, width_ff),
        ]
        + [any_space] * riding,
        scratch_shapes=[pltpu.VMEM((2 * HEAD_COUNT, model), F32), pltpu.VMEM((BLOCK, BLOCK), F32)]
        + (gather_scratch(parts) if ride else []),
        out_shape=[out, *(jax.ShapeDtypeStruct(s, k) for s, k in shapes)] + full,
        input_output_aliases=aliases,
        compiler_params=params(collective_id=3 if ride == "lines" else 5, has_side_effects=True) if ride else params(),
        cost_estimate=pl.CostEstimate(
            flops=int(tokens * 5e6), bytes_accessed=tokens * 15000, transcendentals=tokens * 5000
        ),
        name="time_forward_" + ride if ride else "time_forward",
    )(x, weights, *tables, lengths, *([other] if ride else []))
    saved = results[1 : 1 + len(SAVED)]
    return results[0], saved, (results[-1] if ride else other)


def time_backward(m, x, d_out, weights, tables, saved, before, other, kind, width_ff):
    seqs, frames, model = x.shape[2:]
    tokens = seqs * frames
    parts, unused, part_frames, unused_model = d_out.shape
    per_step = sequences(seqs)
    columns = weights.shape[1]
    ride = other is not None
    if ride:
        before = before[:1]
    ins = [x, d_out, weights, *tables, *saved, *before]
    aliases = {len(ins) - 1: 0} if len(before) == 2 else {}
    target = (1, 1) + x.shape[2:] if ride else x.shape
    more_specs, more_shapes, scratch = [], [], []
    any_space = pl.BlockSpec(memory_space=pl.ANY)
    if ride:
        zs, ys = seq_sides(parts)
        part = model // parts
        ins.append(other.reshape(zs, ys, part, columns))
        more_shapes = [jax.ShapeDtypeStruct((part, columns // 2), BF)]
        more_specs = [whole(more_shapes[0].shape)]
        scratch = reduce_scratch(parts, part, columns)
    rows = at_micro(m, (per_step, frames, model), lambda i: (i, 0, 0))
    return pl.pallas_call(
        partial(time_backward_kernel, parts, width_ff, bool(before), ride, per_step),
        grid=(seqs // per_step,),
        in_specs=[
            rows,
            pl.BlockSpec((parts, per_step, part_frames, model), lambda i: (0, i, 0, 0)),
            whole(weights.shape),
            whole(tables[0].shape),
            whole(tables[1].shape),
            *saved_specs(per_step * frames, per_step, model, width_ff),
        ]
        + [any_space] * (len(before) + ride),
        out_specs=[
            at_micro(0 if ride else m, (per_step, frames, model), lambda i: (i, 0, 0)),
            any_space if kind == F32 else whole((model, columns)),
        ]
        + more_specs,
        out_shape=[
            jax.ShapeDtypeStruct(target, F32),
            jax.ShapeDtypeStruct((model, columns), kind),
        ]
        + more_shapes,
        input_output_aliases=aliases,
        scratch_shapes=work_shapes(per_step * frames, model, width_ff, columns) + scratch,
        compiler_params=params(collective_id=4, has_side_effects=True) if ride else params(),
        cost_estimate=pl.CostEstimate(
            flops=int(tokens * 9e6), bytes_accessed=tokens * 18000, transcendentals=0
        ),
        name="time_backward_reduce" if ride else "time_backward",
    )(*ins)


def band_both(m, x, d_out, lengths, weights, tables, before, kind, width_ff):
    bands, frames, model = x.shape
    tokens = bands * frames
    chunk = math.gcd(frames, 16)
    step_tokens = bands * chunk
    columns = weights.shape[1]
    ins = [lengths, x, d_out, weights, *tables, *before]
    rows = pl.BlockSpec((bands, chunk, model), lambda i, s: (0, i, 0))
    rows_m = at_micro(m, (bands, chunk, model), lambda i: (0, i, 0))
    any_space = pl.BlockSpec(memory_space=pl.ANY)
    saved = [
        pltpu.VMEM(s, k) for s, k in saved_shapes(step_tokens, step_tokens // BLOCK, model, width_ff)
    ]
    return pl.pallas_call(
        partial(band_kernel, width_ff, bool(before), m),
        grid_spec=pltpu.PrefetchScalarGridSpec(
            num_scalar_prefetch=1,
            grid=(frames // chunk,),
            in_specs=[
                rows,
                rows_m,
                whole(weights.shape),
                whole(tables[0].shape),
                whole(tables[1].shape),
            ]
            + [any_space] * len(before),
            out_specs=[rows_m, rows, any_space if kind == F32 else whole((model, columns))],
            scratch_shapes=saved
            + work_shapes(step_tokens, model, width_ff, columns)
            + [pltpu.VMEM((model // LANES, step_tokens, LANES), F32)] * 2
            + [pltpu.VMEM((BLOCK, BLOCK), F32)],
        ),
        out_shape=[
            jax.ShapeDtypeStruct(d_out.shape, BF),
            jax.ShapeDtypeStruct(x.shape, BF),
            jax.ShapeDtypeStruct((model, columns), kind),
        ],
        input_output_aliases={len(ins) - 1: 0} if before else {},
        compiler_params=params(),
        cost_estimate=pl.CostEstimate(
            flops=int(tokens * 14e6), bytes_accessed=tokens * 8000, transcendentals=tokens * 5000
        ),
        name="band_both",
    )(*ins)


MESH = pl.DeviceIdType.MESH


def seq_sides(parts):
    side = 1
    while 4 * side * side <= parts:
        side *= 2
    return parts // side, side


class Place:
    def __init__(self, parts):
        self.dp, self.seq = lax.axis_index("dp"), lax.axis_index("seq")
        self.core = self.dp % 2
        self.zs, self.ys = seq_sides(parts)
        self.z, self.y = self.seq // self.ys, self.seq % self.ys

    def sibling(self):
        return (self.dp + 1 - 2 * self.core, self.seq)

    def along_z(self, step):
        return (self.dp, self.seq + step * self.ys)

    def along_y(self, step):
        return (self.dp, self.seq + step)

    def has_z(self, step):
        return self.z + step < self.zs if step > 0 else self.z + step >= 0

    def has_y(self, step):
        return self.y + step < self.ys if step > 0 else self.y + step >= 0


def greet(place, others=()):
    barrier = pltpu.get_barrier_semaphore()
    pl.semaphore_signal(barrier, inc=1, device_id=place.sibling(), device_id_type=MESH)
    for other in others:
        pl.semaphore_signal(barrier, inc=1, device_id=other, device_id_type=MESH)
    for step in (1, -1):
        for has, to in ((place.has_z, place.along_z), (place.has_y, place.along_y)):

            @pl.when(has(step))
            def _(to=to, step=step):
                pl.semaphore_signal(barrier, inc=1, device_id=to(step), device_id_type=MESH)

    count = 1 + len(others)
    for has in (place.has_z, place.has_y):
        count = count + has(1).astype(jnp.int32) + has(-1).astype(jnp.int32)
    pl.semaphore_wait(barrier, count)


GATHER_SCRATCH = 9


class Gather:
    def __init__(
        self, place, shard_ref, out_ref, send_z, send_y, send_c, got, got_c, local, send_x, got_x, send_cx, at_once=True
    ):
        self.place, self.shard, self.out, self.at_once = place, shard_ref, out_ref, at_once
        self.send_z, self.send_y, self.send_c, self.got, self.got_c, self.local = send_z, send_y, send_c, got, got_c, local
        self.send_x, self.got_x, self.send_cx = send_x, got_x, send_cx
        wide = out_ref.shape[2] // 2
        self.blocks = place.zs * place.ys
        self.crossing = lax.axis_size("dp") == 4 and wide % (3 * LANES) == 0
        third = wide // 3
        x = place.dp // 2

        def columns(core, start, size):
            return pl.ds(pl.multiple_of(core * wide + start, LANES), size)

        if self.crossing:
            self.lanes = columns(place.core, x * third, 2 * third)
            self.other_lanes = columns(1 - place.core, x * third, 2 * third)
            self.given = columns(place.core, x * 2 * third, third)
            self.taken = columns(place.core, (1 - x) * 2 * third, third)
            self.other_taken = columns(1 - place.core, (1 - x) * 2 * third, third)
            self.across = (lax.rem(place.dp + 2, 4), place.seq)
            self.pieces = [columns(place.core, (x + k) * third, third) for k in range(2)]
        else:
            self.lanes = columns(place.core, 0, wide)
            self.other_lanes = columns(1 - place.core, 0, wide)
            self.pieces = [self.lanes]
        self.hops = place.zs
        self.others = [lax.rem(place.seq + turn, self.blocks) for turn in range(1, self.blocks)]

    def index(self, z, y):
        return z * self.place.ys + y

    def held(self, p, k):
        return self.out.at[p, :, self.pieces[k]]

    def mine(self, k):
        return self.shard.at[:, self.pieces[k]]

    def push(self, source, p, k, to, send, receive):
        return pltpu.make_async_remote_copy(
            src_ref=source, dst_ref=self.held(p, k), send_sem=send, recv_sem=receive, device_id=to, device_id_type=MESH
        )

    def same(self, p, lanes, to, send, receive):
        there = self.out.at[p, :, lanes]
        return pltpu.make_async_remote_copy(
            src_ref=there, dst_ref=there, send_sem=send, recv_sem=receive, device_id=to, device_id_type=MESH
        )

    def to_sibling(self, p):
        return self.same(p, self.lanes, self.place.sibling(), self.send_c.at[p], self.got_c.at[0, p])

    def from_sibling(self, p):
        return self.same(p, self.other_lanes, self.place.sibling(), self.send_c.at[p], self.got_c.at[0, p])

    def give(self, p):
        return self.same(p, self.given, self.across, self.send_x.at[p], self.got_x.at[p])

    def take(self, p):
        return self.same(p, self.taken, self.across, self.send_x.at[p], self.got_x.at[p])

    def taken_to_sibling(self, p):
        return self.same(p, self.taken, self.place.sibling(), self.send_cx.at[p], self.got_c.at[1, p])

    def taken_from_sibling(self, p):
        return self.same(p, self.other_taken, self.place.sibling(), self.send_cx.at[p], self.got_c.at[1, p])

    def along_z(self, source, p, k, step, t):
        side = (step + 1) // 2
        return self.push(source, p, k, self.place.along_z(step), self.send_z.at[side, t, k], self.got.at[p, k])

    def along_y(self, source, p, k, step):
        side = (step + 1) // 2
        return self.push(source, p, k, self.place.along_y(step), self.send_y.at[side, p, k], self.got.at[p, k])

    def await_block(self, p, k):
        self.push(self.held(p, k), p, k, self.place.sibling(), self.send_c.at[p], self.got.at[p, k]).wait_recv()

    def hand_on(self, p):
        if self.at_once:
            self.pass_on(p)

    def pass_on(self, p):
        if self.crossing:
            self.give(p).start()
        self.to_sibling(p).start()

    def open_passing(self):
        barrier = pltpu.get_barrier_semaphore()
        peers = [self.place.sibling()] + ([self.across] if self.crossing else [])
        for to in peers:
            pl.semaphore_signal(barrier, inc=1, device_id=to, device_id_type=MESH)
        pl.semaphore_wait(barrier, len(peers))
        for p in self.others:
            self.pass_on(p)

    def own(self):
        return pltpu.make_async_copy(self.shard, self.out.at[self.place.seq], self.local)

    def start(self):
        place = self.place
        greet(place, [self.across] if self.crossing else [])
        self.own().start()
        for k in range(len(self.pieces)):
            for step in (1, -1):

                @pl.when(place.has_z(step))
                def _(k=k, step=step):
                    self.along_z(self.mine(k), place.seq, k, step, 0).start()

                @pl.when(place.has_y(step))
                def _(k=k, step=step):
                    self.along_y(self.mine(k), place.seq, k, step).start()

    def advance(self, slot, slots):
        for hop in range(1, self.hops):
            due = (hop * (slots - 2) + self.hops - 2) // (self.hops - 1) if self.hops > 1 else 0
            pl.when(slot == due)(partial(self.hop, hop))

    def hop(self, t):
        if t == self.place.zs:
            return self.other_lines()
        place = self.place
        for step in (1, -1):
            z = place.z - step * t
            here = (z >= 0) if step > 0 else (z < place.zs)

            @pl.when(here)
            def _(step=step, z=z):
                p = self.index(z, place.y)
                for k in range(len(self.pieces)):
                    self.await_block(p, k)
                    if t < place.zs - 1:
                        pl.when(place.has_z(step))(
                            lambda k=k: self.along_z(self.held(p, k), p, k, step, t).start()
                        )
                    for side in (1, -1):
                        pl.when(place.has_y(side))(
                            lambda k=k, side=side: self.along_y(self.held(p, k), p, k, side).start()
                        )
                self.hand_on(p)

    def other_lines(self):
        place = self.place
        for t in range(1, place.ys):
            for step in (1, -1):
                y = place.y - step * t
                here = (y >= 0) if step > 0 else (y < place.ys)

                @pl.when(here)
                def _(t=t, step=step, y=y):
                    for turn in range(place.zs):
                        p = self.index(lax.rem(place.z + turn, place.zs), y)
                        for k in range(len(self.pieces)):
                            self.await_block(p, k)
                            if t < place.ys - 1:
                                pl.when(place.has_y(step))(
                                    lambda p=p, k=k: self.along_y(self.held(p, k), p, k, step).start()
                                )
                        self.hand_on(p)

    def pass_taken(self):
        if self.crossing:
            for p in self.others:
                self.take(p).wait_recv()
                self.taken_to_sibling(p).start()

    def finish_passing(self):
        for p in self.others:
            self.to_sibling(p).wait_send()
            self.from_sibling(p).wait_recv()
        if self.crossing:
            for p in self.others:
                self.give(p).wait_send()
                self.taken_to_sibling(p).wait_send()
                self.taken_from_sibling(p).wait_recv()

    def finish_lines(self):
        place = self.place
        self.own().wait()
        for step in (1, -1):
            for t in range(place.zs - 1):
                z = place.z - step * t
                sent = jnp.logical_and((z >= 0) if step > 0 else (z < place.zs), place.has_z(step))

                @pl.when(sent)
                def _(step=step, t=t):
                    for k in range(len(self.pieces)):
                        self.along_z(self.mine(k), place.seq, k, step, t).wait_send()

            for t in range(place.ys - 1):
                y = place.y - step * t
                sent = jnp.logical_and((y >= 0) if step > 0 else (y < place.ys), place.has_y(step))

                @pl.when(sent)
                def _(step=step, y=y):
                    for z in range(place.zs):
                        for k in range(len(self.pieces)):
                            self.along_y(self.mine(k), self.index(z, y), k, step).wait_send()


def gather_kernel(parts, shard_ref, out_ref, *sems):
    gather = Gather(Place(parts), shard_ref, out_ref, *sems)
    gather.start()
    for hop in range(1, gather.hops + 1):
        gather.hop(hop)
    gather.pass_taken()
    gather.finish_passing()
    gather.finish_lines()


def gather_scratch(parts):
    zs, ys = seq_sides(parts)
    dma = pltpu.SemaphoreType.DMA
    each = dma((parts,))
    return [dma((2, zs, 2)), dma((2, parts, 2)), each, dma((parts, 2)), dma((2, parts)), dma, each, each, each]


def gather_weights(shard, parts):
    rows, columns = shard.shape
    out = pl.pallas_call(
        partial(gather_kernel, parts),
        in_specs=[pl.BlockSpec(memory_space=pl.ANY)],
        out_specs=pl.BlockSpec(memory_space=pl.ANY),
        out_shape=jax.ShapeDtypeStruct((parts, rows, columns), shard.dtype),
        scratch_shapes=gather_scratch(parts),
        compiler_params=params(collective_id=1, has_side_effects=True),
        cost_estimate=pl.CostEstimate(flops=0, bytes_accessed=parts * rows * columns * 40, transcendentals=0),
        name="gather_weights",
    )(shard)
    return out.reshape(parts * rows, columns)


def add_into(acc, other):
    acc[...] = (acc[...].astype(F32) + other[...].astype(F32)).astype(acc.dtype)


class Line:
    def __init__(self, i, n, to, acc, slot, count, sends, receives):
        self.i, self.n, self.to, self.acc, self.slot, self.count = i, n, to, acc, slot, count
        self.sends, self.receives = sends, receives

    def copy(self, side, j, k):
        return pltpu.make_async_remote_copy(
            src_ref=self.acc(j, k),
            dst_ref=self.slot(side, j, k),
            send_sem=self.sends.at[side, j, k],
            recv_sem=self.receives.at[side, j, k],
            device_id=self.to(1 - 2 * side),
            device_id_type=MESH,
        )

    def take(self, side, j, k):
        self.copy(side, j, k).wait_recv()
        add_into(self.acc(j, k), self.slot(side, j, k))

    def send_pair(self, k):
        pl.when(self.i == 0)(lambda: self.copy(0, 1, k).start())
        pl.when(self.i == 1)(lambda: self.copy(1, 0, k).start())

    def send(self, now, base):
        for t in range(self.n - 1):
            for side, j, passed in ((0, self.n - 1 - t, self.i), (1, t, self.n - 1 - self.i)):
                beyond = self.i < j if side == 0 else self.i > j
                inner = self.i > 0 if side == 0 else self.i < self.n - 1

                @pl.when(jnp.logical_and(beyond, now(base + passed + t)))
                def _(side=side, j=j, inner=inner):
                    for k in range(self.count):
                        if self.n > 2:
                            pl.when(inner)(lambda k=k: self.take(side, j, k))
                        self.copy(side, j, k).start()

    def finish(self):
        for side, inner in ((0, self.i > 0), (1, self.i < self.n - 1)):

            @pl.when(inner)
            def _(side=side):
                for k in range(self.count):
                    self.take(side, self.i, k)

    def drain(self):
        for j in range(self.n):
            for side, beyond in ((0, self.i < j), (1, self.i > j)):

                @pl.when(beyond)
                def _(side=side, j=j):
                    for k in range(self.count):
                        self.copy(side, j, k).wait_send()


def first_columns(wide):
    return wide // LANES // 3 * 2 * LANES


REDUCE_SCRATCH = 17
ACROSS_SCRATCH = 6


def reduce_scratch(parts, rows, columns):
    zs, ys = seq_sides(parts)
    wide = columns // 2
    first = first_columns(wide)
    rest = wide - first
    dma = pltpu.SemaphoreType.DMA
    return [
        pltpu.VMEM((zs, ys, rows, wide), BF),
        pltpu.VMEM((zs, ys, rows, wide), BF),
        pltpu.VMEM((2, ys, zs, rows, first), BF),
        pltpu.VMEM((2, zs, ys, rows, rest), BF),
        pltpu.VMEM((2, zs, 2, rows, first // 2), BF),
        pltpu.VMEM((2, ys, 1, rows, rest), BF),
        dma((zs,)),
        dma((zs,)),
        dma((zs,)),
        dma((2, ys, zs)),
        dma((2, ys, zs)),
        dma((2, zs, ys)),
        dma((2, zs, ys)),
        dma((2, zs, 2)),
        dma((2, zs, 2)),
        dma((2, ys, 1)),
        dma((2, ys, 1)),
    ]


def across_scratch(replicas, rows, columns):
    xs = replicas // 2
    wide = columns // 2
    dma = pltpu.SemaphoreType.DMA
    return [
        pltpu.VMEM((xs, rows, wide), BF),
        pltpu.VMEM((2, rows, wide), F32),
        dma((max(xs - 1, 1), 2)),
        dma((xs, 2)),
        dma,
        dma,
    ]


class Across:
    def __init__(self, place, own, scratch):
        self.place, self.own = place, own
        self.in_x, self.fin, self.s_x, self.g_x, self.s_f, self.g_f = scratch
        self.xs = self.in_x.shape[0]
        self.x = place.dp // 2
        self.peers = [(lax.rem(self.x + t, self.xs) * 2 + place.core, place.seq) for t in range(1, self.xs)]

    def columns(self, piece):
        wide = self.own.shape[-1]
        first = first_columns(wide)
        return pl.ds(first, wide - first) if piece else pl.ds(0, first)

    def copy(self, t, there, piece):
        lanes = self.columns(piece)
        return pltpu.make_async_remote_copy(
            src_ref=self.own.at[:, lanes],
            dst_ref=self.in_x.at[there, :, lanes],
            send_sem=self.s_x.at[t, piece],
            recv_sem=self.g_x.at[there, piece],
            device_id=self.peers[t],
            device_id_type=MESH,
        )

    def half(self, c):
        return pltpu.make_async_remote_copy(
            src_ref=self.fin.at[c],
            dst_ref=self.fin.at[c],
            send_sem=self.s_f,
            recv_sem=self.g_f,
            device_id=self.place.sibling(),
            device_id_type=MESH,
        )

    def start(self, piece):
        for t in range(self.xs - 1):
            self.copy(t, self.x, piece).start()
        lanes = self.columns(piece)
        self.in_x[self.x, :, lanes] = self.own[:, lanes]

    def fold(self):
        for t in range(self.xs - 1):
            for piece in range(2):
                self.copy(t, lax.rem(self.x + t + 1, self.xs), piece).wait_recv()
        total = self.in_x[0].astype(F32)
        for t in range(1, self.xs):
            total = total + self.in_x[t].astype(F32)
        self.fin[self.place.core] = total
        self.half(self.place.core).start()

    def finish(self, out_ref):
        self.half(1 - self.place.core).wait_recv()
        squares = 0.0
        for c in range(2):
            value = self.fin[c]
            out_ref[c] = value
            squares = squares + jnp.sum(value * value, axis=(0, 1), keepdims=True)
        return squares

    def drain(self):
        for t in range(self.xs - 1):
            for piece in range(2):
                self.copy(t, self.x, piece).wait_send()
        self.half(self.place.core).wait_send()


class Reduction:
    def __init__(self, place, grad_ref, scratch):
        self.place, self.grad = place, grad_ref
        self.acc, self.in_c, in_ya, in_zb, in_za, in_yb = scratch[:6]
        self.local, self.s_c, self.g_c, s_ya, g_ya, s_zb, g_zb, s_za, g_za, s_yb, g_yb = scratch[6:]
        acc = self.acc
        zs, ys = place.zs, place.ys
        wide = acc.shape[-1]
        first = first_columns(wide)
        a, b = pl.ds(0, first), pl.ds(first, wide - first)
        self.lanes = pl.ds(pl.multiple_of(place.core * wide, LANES), wide)
        self.other = pl.ds(pl.multiple_of((1 - place.core) * wide, LANES), wide)
        self.line_ya = Line(
            place.y, ys, place.along_y, lambda j, k: acc.at[k, j, :, a], lambda s, j, k: in_ya.at[s, j, k], zs, s_ya, g_ya
        )
        self.line_zb = Line(
            place.z, zs, place.along_z, lambda j, k: acc.at[j, k, :, b], lambda s, j, k: in_zb.at[s, j, k], ys, s_zb, g_zb
        )
        pieces = [pl.ds(k * (first // 2), first // 2) for k in range(2)]
        self.line_za = Line(
            place.z,
            zs,
            place.along_z,
            lambda j, k: acc.at[j, place.y, :, pieces[k]],
            lambda s, j, k: in_za.at[s, j, k],
            2,
            s_za,
            g_za,
        )
        self.line_yb = Line(
            place.y, ys, place.along_y, lambda j, k: acc.at[place.z, j, :, b], lambda s, j, k: in_yb.at[s, j, k], 1, s_yb, g_yb
        )
        self.own = acc.at[place.z, place.y]

    def mine(self, z):
        return pltpu.make_async_copy(self.grad.at[z, :, :, self.lanes], self.acc.at[z], self.local.at[z])

    def swap(self, z):
        return pltpu.make_async_remote_copy(
            src_ref=self.grad.at[z, :, :, self.other],
            dst_ref=self.in_c.at[z],
            send_sem=self.s_c.at[z],
            recv_sem=self.g_c.at[z],
            device_id=self.place.sibling(),
            device_id_type=MESH,
        )

    def open(self, greeting):
        for z in range(self.place.zs):
            self.mine(z).start()
        greeting()
        for z in range(self.place.zs):
            self.swap(z).start()

    def fold_cores(self):
        for z in range(self.place.zs):
            self.mine(z).wait()
            self.swap(z).wait_recv()
            for y in range(self.place.ys):
                add_into(self.acc.at[z, y], self.in_c.at[z, y])
            if self.place.ys == 2:
                self.line_ya.send_pair(z)

    def advance(self, slot, last):
        def now(time):
            return slot == jnp.minimum(time, last)

        zs, ys = self.place.zs, self.place.ys
        pl.when(now(0))(lambda: self.open(lambda: greet(self.place)))
        pl.when(now(1))(self.fold_cores)
        if ys != 2:
            self.line_ya.send(now, 1)
        self.line_zb.send(now, 1)
        ready = max(zs, ys + 1)
        pl.when(now(ready))(self.line_zb.finish)
        self.line_yb.send(now, ready)
        pl.when(now(ready))(self.line_ya.finish)
        self.line_za.send(now, ready)

    def finish(self):
        self.line_yb.finish()
        self.line_za.finish()

    def drain(self):
        for line in (self.line_ya, self.line_zb, self.line_za, self.line_yb):
            line.drain()
        for z in range(self.place.zs):
            self.swap(z).wait_send()


def reduce_kernel(parts, grad_ref, band_ref, out_ref, norm_ref, squares, s_n, g_n, *scratch):
    place = Place(parts)
    peers = [(place.dp, lax.rem(place.seq + t, parts)) for t in range(1, parts)]
    reduction = Reduction(place, grad_ref, scratch[:REDUCE_SCRATCH])
    band = Across(place, band_ref, scratch[REDUCE_SCRATCH : REDUCE_SCRATCH + ACROSS_SCRATCH])
    time = Across(place, reduction.own, scratch[REDUCE_SCRATCH + ACROSS_SCRATCH :])

    def greeting():
        barrier = pltpu.get_barrier_semaphore()
        everyone = [place.sibling()] + time.peers + peers
        for to in everyone:
            pl.semaphore_signal(barrier, inc=1, device_id=to, device_id_type=MESH)
        pl.semaphore_wait(barrier, len(everyone))

    def always(time):
        return True

    reduction.open(greeting)
    reduction.fold_cores()
    band.start(0)
    band.start(1)
    if place.ys != 2:
        reduction.line_ya.send(always, 0)
    reduction.line_zb.send(always, 0)
    reduction.line_zb.finish()
    reduction.line_yb.send(always, 0)
    band.fold()
    reduction.line_ya.finish()
    reduction.line_za.send(always, 0)
    reduction.line_yb.finish()
    time.start(1)
    partial_sum = band.finish(out_ref.at[1])
    reduction.line_za.finish()
    time.start(0)
    time.fold()
    partial_sum = partial_sum + time.finish(out_ref.at[0])
    squares[place.seq] = jnp.broadcast_to(partial_sum, squares.shape[1:])

    def tell(t, there):
        return pltpu.make_async_remote_copy(
            src_ref=squares.at[there],
            dst_ref=squares.at[there],
            send_sem=s_n.at[t],
            recv_sem=g_n.at[there],
            device_id=peers[t],
            device_id_type=MESH,
        )

    for t in range(parts - 1):
        tell(t, place.seq).start()
    for t in range(parts - 1):
        tell(t, lax.rem(place.seq + t + 1, parts)).wait_recv()
    norm = squares[0]
    for p in range(1, parts):
        norm = norm + squares[p]
    norm_ref[...] = norm
    for t in range(parts - 1):
        tell(t, place.seq).wait_send()
    reduction.drain()
    band.drain()
    time.drain()


def reduce_gradient(grad, band, parts, replicas):
    zs, ys = seq_sides(parts)
    rows, columns = grad.shape[0] // parts, grad.shape[1]
    dma = pltpu.SemaphoreType.DMA
    in_vmem = pl.BlockSpec(memory_space=pltpu.VMEM)
    return pl.pallas_call(
        partial(reduce_kernel, parts),
        in_specs=[pl.BlockSpec(memory_space=pl.ANY), in_vmem],
        out_specs=[in_vmem, in_vmem],
        out_shape=[
            jax.ShapeDtypeStruct((2, 2, rows, columns // 2), F32),
            jax.ShapeDtypeStruct((8, LANES), F32),
        ],
        scratch_shapes=[pltpu.VMEM((parts, 8, LANES), F32), dma((parts - 1,)), dma((parts,))]
        + reduce_scratch(parts, rows, columns)
        + across_scratch(replicas, rows, columns) * 2,
        compiler_params=params(collective_id=2, has_side_effects=True),
        cost_estimate=pl.CostEstimate(flops=0, bytes_accessed=columns * rows * parts * 60, transcendentals=0),
        name="reduce_gradient",
    )(grad.reshape(zs, ys, rows, columns), band)


def rotary_order(columns):
    lead = columns.shape[:-1]
    split = columns.reshape(lead + (-1, 4, 2, HEAD_DIM // 2))
    return jnp.swapaxes(split, -3, -2).reshape(columns.shape)


def adam_step(master, gradient, first_old, second_old, learn_rate):
    first_new = BETA_ONE * first_old + (1.0 - BETA_ONE) * gradient
    second_new = BETA_TWO * second_old + (1.0 - BETA_TWO) * gradient * gradient
    first_hat = first_new / (1.0 - BETA_ONE**STEP)
    second_hat = second_new / (1.0 - BETA_TWO**STEP)
    updated = master - learn_rate * (first_hat / (jnp.sqrt(second_hat) + ADAM_EPS) + DECAY * master)
    return (updated, first_new, second_new)


def heads_in_order(first, second):
    half = HEAD_DIM // 2
    lane = iota(first.shape, 1) // half

    def turn(t, places):
        return pltpu.roll(t, places % LANES, 1) if places % LANES else t

    results = []
    for low in (0, 2):
        pieces = [turn(first, -low * half), turn(second, half - low * half)]
        pieces += [turn(first, half - low * half), turn(second, 2 * half - low * half)]
        out = pieces[0]
        for place in range(1, 4):
            out = jnp.where(lane == place, pieces[place], out)
        results.append(out)
    return results


def update_kernel(grads_ref, squares_ref, *refs):
    masters, firsts, seconds = refs[0:2], refs[2:4], refs[4:6]
    outs = refs[6:]
    norm = jnp.sqrt(squares_ref[0:1, 0:1])
    factor = jnp.minimum(1.0, CLIP_NORM / (norm + 1e-06))
    half = grads_ref.shape[2]
    width_in, width_out = (ref.shape[1] for ref in masters)

    def gradient(start, size):
        return grads_ref[start // half, :, start % half : start % half + size] * factor

    def update(which, column, size, grad, rate):
        part = slice(column, column + size)
        new = adam_step(
            masters[which][:, part], grad, firsts[which][:, part], seconds[which][:, part], rate
        )
        for k in range(3):
            outs[2 * k + which][:, part] = new[k]
        outs[6 + which][:, part] = new[0].astype(BF)

    for start in range(0, 2 * INNER_WIDTH, GROUP):
        pair = heads_in_order(gradient(start, LANES), gradient(start + LANES, LANES))
        for n in range(2):
            update(0, start + n * LANES, LANES, pair[n], RATE_MATRIX)
    for which, width, base, begin in ((0, width_in, 0, 2 * INNER_WIDTH), (1, width_out, width_in, 0)):
        for column in range(begin, width, LANES):
            update(which, column, LANES, gradient(base + column, LANES), RATE_MATRIX)


def update_weights(grads, squares, masters, firsts, seconds):
    states = [*masters, *firsts, *seconds]

    def by_layer(t):
        return pl.BlockSpec((None,) + t.shape[1:], lambda i: (i, 0, 0))

    return pl.pallas_call(
        update_kernel,
        grid=(2,),
        in_specs=[pl.BlockSpec((None,) + grads.shape[1:], lambda i: (i, 0, 0, 0)), whole(squares.shape)]
        + [by_layer(t) for t in states],
        out_specs=[by_layer(t) for t in states + list(masters)],
        out_shape=[jax.ShapeDtypeStruct(t.shape, F32) for t in states]
        + [jax.ShapeDtypeStruct(t.shape, BF) for t in masters],
        compiler_params=params(),
        name="update_weights",
    )(grads, squares, *states)


def body(
    activations,
    cotangent,
    lengths,
    weight_in,
    weight_out,
    weight_small,
    first_in,
    first_out,
    first_small,
    second_in,
    second_out,
    second_small,
):
    parts = lax.axis_size("seq")
    lengths = lengths.reshape(1, -1)
    micro, unused, band_dev, frames, model = activations.shape
    bands, frame_dev = cotangent.shape[2], cotangent.shape[3]
    turned = 2 * INNER_WIDTH
    width_in, width_out = weight_in.shape[2], weight_out.shape[2]
    width_ff = width_in - 3 * INNER_WIDTH
    small_width = weight_small.shape[2]
    packed = [
        jnp.concatenate(
            [
                rotary_order(weight_in[layer, :, :turned].astype(BF)),
                weight_in[layer, :, turned:].astype(BF),
                weight_out[layer].astype(BF),
                jnp.pad(weight_small[layer].astype(BF), ((0, 0), (0, SMALL_LANES - small_width))),
            ],
            axis=1,
        )
        for layer in range(2)
    ]
    time_weights = gather_weights(packed[0], parts)
    time_tables = rotary_tables(frames, sequences(band_dev) * frames)
    band_tables = rotary_tables(bands, min(2 * BLOCK, frame_dev * bands))

    def exchange(tensor):
        return lax.all_to_all(tensor, "seq", split_axis=0, concat_axis=0, tiled=True)

    streams, saves, other = [], [], packed[1]
    for m in range(micro):
        ride = "lines" if m == 0 else "pass" if m == 1 else ""
        out, saved, other = time_forward(
            m, activations, lengths, time_weights, time_tables, ride, other, parts, width_ff
        )
        saves.append(saved)
        streams.append(exchange(out).reshape(bands, frame_dev, model))
    band_weights = other.reshape(model, -1)
    backs, before = [], ()
    for m in range(micro):
        kind = BF if m == micro - 1 else F32
        output, back, grad_band = band_both(
            m, streams[m], cotangent, lengths, band_weights, band_tables, before, kind, width_ff
        )
        before = (grad_band, output)
        backs.append(exchange(back.reshape(parts, band_dev, frame_dev, model)))
    before = ()
    for m in range(micro):
        kind = BF if m == micro - 1 else F32
        part, grad_time, *shard = time_backward(
            m,
            activations,
            backs[m],
            time_weights,
            time_tables,
            saves[m],
            before,
            grad_band if m == micro - 1 else None,
            kind,
            width_ff,
        )
        if m < micro - 1:
            d_input = part
            before = (grad_time, d_input)
        else:
            d_input = lax.dynamic_update_slice(d_input, part, (m, 0, 0, 0, 0))
    grads, squares = reduce_gradient(grad_time, shard[0], parts, lax.axis_size("dp"))
    new = update_weights(grads, squares, (weight_in, weight_out), (first_in, first_out), (second_in, second_out))
    norm = jnp.sqrt(squares[0, 0])
    factor = jnp.minimum(1.0, CLIP_NORM / (norm + 1e-06))
    start = width_in + width_out - grads.shape[3]
    rate = jnp.where(jnp.arange(small_width) < HEAD_COUNT, RATE_GATE, RATE_GAIN)

    def columns_first(t):
        return jnp.transpose(t, (2, 0, 1))

    small = adam_step(
        columns_first(weight_small),
        columns_first(grads[:, 1, :, start : start + small_width]) * factor,
        columns_first(first_small),
        columns_first(second_small),
        rate[:, None, None],
    )
    small = [jnp.transpose(t, (1, 2, 0)) for t in small]
    return (
        output,
        d_input,
        norm,
        new[0],
        new[1],
        small[0],
        new[2],
        new[3],
        small[1],
        new[4],
        new[5],
        small[2],
        new[6],
        new[7],
        small[0].astype(BF),
    )


def solution(mesh):
    by_seq = P(None, "seq", None)
    by_band = P(None, "dp", "seq", None, None)
    by_frame = P(None, "dp", None, "seq", None)
    return jax.shard_map(
        body,
        mesh=mesh,
        in_specs=(by_band, by_frame, P(None, "dp")) + (by_seq,) * 9,
        out_specs=(by_frame, by_band, P()) + (by_seq,) * 12,
        check_vma=False,
    )
```

```python
from functools import partial
import math

import jax
import jax.numpy as jnp
import numpy as np
from jax import lax
from jax.experimental import pallas as pl
from jax.experimental.pallas import tpu as pltpu
from jax.sharding import PartitionSpec as P

HEAD_COUNT = 8
HEAD_DIM = 64
INNER_WIDTH = 512
STEP = 10
EPS_NORM = 1e-06
BETA_ONE = 0.9
BETA_TWO = 0.999
ADAM_EPS = 1e-08
DECAY = 0.1
RATE_MATRIX = 0.1
RATE_GATE = 0.1
RATE_GAIN = 0.5
CLIP_NORM = 1.0
MASKED = -1e30

BF = jnp.bfloat16
F32 = jnp.float32
GROUP = 256
BLOCK = 256
LANES = 128
SMALL_LANES = 2 * LANES
LOG2E = 1.4426950408889634
SCORE_EXP = LOG2E / math.sqrt(HEAD_DIM)
SQRT_HALF = math.sqrt(0.5)
GAUSS = 1.0 / math.sqrt(2.0 * math.pi)
VMEM_LIMIT = 60 * 2**20


def nn(a, b):
    return lax.dot_general(a, b, (((1,), (0,)), ((), ())), preferred_element_type=F32)


def nt(a, b):
    return lax.dot_general(a, b, (((1,), (1,)), ((), ())), preferred_element_type=F32)


def tn(a, b):
    return lax.dot_general(a, b, (((0,), (0,)), ((), ())), preferred_element_type=F32)


def iota(shape, dim):
    return lax.broadcasted_iota(jnp.int32, shape, dim)


def split_rows(rows):
    high = rows.astype(BF)
    rest = (rows - high.astype(F32)).astype(BF)
    return jnp.concatenate([high, rest], axis=0)


def head_lanes():
    shape = (2 * HEAD_COUNT, INNER_WIDTH)
    return (iota(shape, 1) // HEAD_DIM == iota(shape, 0) % HEAD_COUNT).astype(F32).astype(BF)


def inverse_rms(rows):
    return lax.rsqrt(jnp.mean(rows * rows, axis=-1, keepdims=True) + EPS_NORM)


def norm_back(rows, gain, grad):
    inverse = inverse_rms(rows)
    unit = rows * inverse
    scaled = grad * gain
    d_rows = inverse * (scaled - unit * jnp.mean(scaled * unit, axis=-1, keepdims=True))
    return d_rows, jnp.sum(grad * unit, axis=0, keepdims=True)


def half_lanes(h):
    return (iota((BLOCK, GROUP), 1) % LANES) // (HEAD_DIM // 2) == h


def whole_lanes(h):
    return iota((BLOCK, GROUP), 1) // HEAD_DIM == h


def picked(mask, tensor):
    return jnp.where(mask, tensor, jnp.zeros_like(tensor))


def group_slice(g):
    return slice(g * GROUP, (g + 1) * GROUP)


def forward_block(x, w_ref, small, cos, sin, bias_ref, keep, start, item, width_ff, tick=None):
    gate_weight, gain_attn, gain_ff = small
    size = x.shape[0]
    rows = pl.ds(start, size)
    normed = (x * inverse_rms(x) * gain_attn).astype(BF)
    if "normed" in keep:
        keep["normed"][rows, :] = normed
    gate_rows = jax.nn.sigmoid(nt(gate_weight, normed))
    keep["gate"][:, rows] = gate_rows
    half = GROUP // 2
    for g in range(2):
        for part, name in ((0, "q"), (1, "k")):
            column = part * INNER_WIDTH + g * GROUP
            t = nn(normed, w_ref[:, column : column + GROUP])
            a, b = t[:, :half], t[:, half:]
            keep[name][rows, g * GROUP : g * GROUP + half] = (a * cos - b * sin).astype(BF)
            keep[name][rows, g * GROUP + half : (g + 1) * GROUP] = (b * cos + a * sin).astype(BF)
        column = 2 * INNER_WIDTH + g * GROUP
        keep["v"][rows, group_slice(g)] = nn(normed, w_ref[:, column : column + GROUP]).astype(BF)
    gate = tn(split_rows(gate_rows), head_lanes())
    for n in range(size // BLOCK):
        if tick and n == size // BLOCK - 1:
            tick()
        block = pl.ds(start + n * BLOCK, BLOCK)
        for g in range(2):
            lanes = group_slice(g)
            queries, keys = keep["q"][block, lanes], keep["k"][block, lanes]
            values = keep["v"][block, lanes]
            parts, heads = [], []
            for h in range(4):
                scores = nt(picked(half_lanes(h), keys), queries) + bias_ref[...]
                peak = jnp.max(scores, axis=0, keepdims=True)
                terms = jnp.exp2((scores - peak) * SCORE_EXP)
                probs = (terms * (1.0 / jnp.sum(terms, axis=0, keepdims=True))).astype(BF)
                keep["probs"][item + n, g * 4 + h] = probs
                parts.append(probs)
                heads.append(picked(whole_lanes(h), values))
            attended = tn(jnp.concatenate(parts, axis=0), jnp.concatenate(heads, axis=0))
            keep["gated"][block, lanes] = (attended * gate[n * BLOCK : (n + 1) * BLOCK, lanes]).astype(BF)
    out_start = 3 * INNER_WIDTH + width_ff
    middle = x + nt(keep["gated"][rows, :], w_ref[:, out_start : out_start + INNER_WIDTH])
    keep["middle"][rows, :] = middle
    normed_ff = (middle * inverse_rms(middle) * gain_ff).astype(BF)
    if "normed_ff" in keep:
        keep["normed_ff"][rows, :] = normed_ff
    result = middle
    for c in range(width_ff // GROUP):
        up = 3 * INNER_WIDTH + c * GROUP
        down = out_start + INNER_WIDTH + c * GROUP
        hidden = nn(normed_ff, w_ref[:, up : up + GROUP])
        cumulative = 0.5 + 0.5 * lax.erf(hidden * SQRT_HALF)
        activated = (hidden * cumulative).astype(BF)
        density = jnp.exp2(hidden * hidden * (-0.5 * LOG2E)) * GAUSS
        keep["act"][rows, group_slice(c)] = activated
        keep["slope"][rows, group_slice(c)] = (cumulative + hidden * density).astype(BF)
        result = result + nt(activated, w_ref[:, down : down + GROUP])
    return result


def backward_block(d_out, x, w_ref, small, cos, sin, keep, work, sums, start, item, width_ff, tick=None):
    gate_weight, gain_attn, gain_ff = small
    size = x.shape[0]
    rows = pl.ds(start, size)
    branch = d_out.astype(BF)
    work["branch"][rows, :] = branch
    out_start = 3 * INNER_WIDTH + width_ff
    d_normed_ff = None
    for c in range(width_ff // GROUP):
        up = 3 * INNER_WIDTH + c * GROUP
        down = out_start + INNER_WIDTH + c * GROUP
        d_act = nn(branch, w_ref[:, down : down + GROUP])
        d_hidden = (d_act * keep["slope"][rows, group_slice(c)].astype(F32)).astype(BF)
        work["d_hidden"][rows, group_slice(c)] = d_hidden
    up = 3 * INNER_WIDTH
    d_normed_ff = nt(work["d_hidden"][rows, :], w_ref[:, up : up + width_ff])
    middle = keep["middle"][rows, :]
    d_rows, d_gain_ff = norm_back(middle, gain_ff, d_normed_ff)
    d_middle = d_out + d_rows
    attn_back = d_middle.astype(BF)
    work["attn_back"][rows, :] = attn_back
    gate_rows = keep["gate"][:, rows]
    lanes_of = head_lanes()
    gate = tn(split_rows(gate_rows), lanes_of)
    d_gated = nn(attn_back, w_ref[:, out_start : out_start + INNER_WIDTH])
    product = d_gated * keep["gated"][rows, :].astype(F32)
    high = product.astype(BF)
    rest = (product - high.astype(F32)).astype(BF)
    delta_rows = (nt(lanes_of, high) + nt(lanes_of, rest))[:HEAD_COUNT]
    d_logit = split_rows(delta_rows * (1.0 - gate_rows))
    d_attended = (d_gated * gate).astype(BF)
    half = GROUP // 2
    scale = HEAD_DIM**-0.5
    for n in range(size // BLOCK):
        if tick and n == size // BLOCK - 1:
            tick()
        block = pl.ds(start + n * BLOCK, BLOCK)
        inner = slice(n * BLOCK, (n + 1) * BLOCK)
        for g in range(2):
            lanes = group_slice(g)
            queries, keys = keep["q"][block, lanes], keep["k"][block, lanes]
            values, d_att = keep["v"][block, lanes], d_attended[inner, lanes]
            p_list, s_list, q_list, a_list, k_list = [], [], [], [], []
            for h in range(4):
                halves, wholes = half_lanes(h), whole_lanes(h)
                probs = keep["probs"][item + n, g * 4 + h]
                d_probs = nt(picked(wholes, values), d_att)
                delta = delta_rows[g * 4 + h : g * 4 + h + 1, inner]
                d_scores = (probs.astype(F32) * (d_probs - delta)).astype(BF)
                p_list.append(probs)
                s_list.append(d_scores)
                a_list.append(picked(wholes, d_att))
                q_list.append(picked(halves, queries))
                k_list.append(picked(halves, keys))
            d_values = nn(jnp.concatenate(p_list, axis=1), jnp.concatenate(a_list, axis=0))
            d_keys = nn(jnp.concatenate(s_list, axis=1), jnp.concatenate(q_list, axis=0))
            d_query = tn(jnp.concatenate(s_list, axis=0), jnp.concatenate(k_list, axis=0))
            for column, t in ((0, d_query), (INNER_WIDTH, d_keys)):
                t = t * scale
                a, b = t[:, :half], t[:, half:]
                c, s = cos[inner], sin[inner]
                column = column + g * GROUP
                work["d_proj"][block, column : column + half] = (a * c + b * s).astype(BF)
                work["d_proj"][block, column + half : column + GROUP] = (b * c - a * s).astype(BF)
            column = 2 * INNER_WIDTH + g * GROUP
            work["d_proj"][block, column : column + GROUP] = d_values.astype(BF)
    twice = jnp.concatenate([gate_weight, gate_weight], axis=0)
    d_normed = tn(d_logit, twice)
    for c in range(3 * INNER_WIDTH // INNER_WIDTH):
        part = slice(c * INNER_WIDTH, (c + 1) * INNER_WIDTH)
        d_normed = d_normed + nt(work["d_proj"][rows, part], w_ref[:, part])
    d_rows, d_gain_attn = norm_back(x, gain_attn, d_normed)
    d_gate = nn(d_logit, work["normed"][rows, :])
    sums[0:HEAD_COUNT, :] += d_gate[:HEAD_COUNT] + d_gate[HEAD_COUNT:]
    sums[HEAD_COUNT : HEAD_COUNT + 1, :] += d_gain_attn
    sums[HEAD_COUNT + 1 : HEAD_COUNT + 2, :] += d_gain_ff
    return d_middle + d_rows


def weight_sums(total, work, keep, width_ff, done=None):
    out_start = 3 * INNER_WIDTH + width_ff
    pairs = (
        (work["normed"], work["d_proj"], 0),
        (work["normed_ff"], work["d_hidden"], 3 * INNER_WIDTH),
        (work["attn_back"], keep["gated"], out_start),
        (work["branch"], keep["act"], out_start + INNER_WIDTH),
    )
    for left, right, start in pairs:
        turned = left[...].T
        for c in range(right.shape[-1] // INNER_WIDTH):
            part = slice(start + c * INNER_WIDTH, start + (c + 1) * INNER_WIDTH)
            total[:, part] += nn(turned, right[:, c * INNER_WIDTH : (c + 1) * INNER_WIDTH])
        if done:
            done(start)


def sections(width, width_ff):
    cuts = [0, 3 * INNER_WIDTH, 3 * INNER_WIDTH + width_ff, 4 * INNER_WIDTH + width_ff, 4 * INNER_WIDTH + 2 * width_ff, width]
    return [slice(a, b) for a, b in zip(cuts[:-1], cuts[1:])]


def masked_keys(valid):
    return jnp.where(valid, 0.0, MASKED).astype(F32)


def turn_small(w_ref, small_ref):
    width = w_ref.shape[1] - SMALL_LANES
    rows = w_ref[:, width : width + LANES].astype(F32).T
    small_ref[...] = rows[: small_ref.shape[0]]


def small_parts(small_ref):
    gate_weight = small_ref[0:HEAD_COUNT, :].astype(BF)
    return (
        gate_weight,
        small_ref[HEAD_COUNT : HEAD_COUNT + 1, :],
        small_ref[HEAD_COUNT + 1 : HEAD_COUNT + 2, :],
    )


class Outgoing:
    def __init__(self, total, out_ref, sems, width_ff, last):
        self.total, self.out, self.sems, self.last = total, out_ref, sems, last
        self.parts = sections(total.shape[1], width_ff)

    def copy(self, n):
        part = self.parts[n]
        return pltpu.make_async_copy(self.total.at[:, part], self.out.at[:, part], self.sems.at[n])

    def done(self, start):
        number = [part.start for part in self.parts].index(start)
        pl.when(self.last)(lambda: self.copy(number).start())


def finish_sums(total, sums, out_ref, outgoing, arrival):
    width = total.shape[1] - SMALL_LANES
    model = total.shape[0]
    tall = jnp.concatenate([sums[...], jnp.zeros((SMALL_LANES - sums.shape[0], model), F32)], axis=0)
    if outgoing:
        total[:, width:] = tall.T
        outgoing.copy(4).start()
        for n in range(5):
            outgoing.copy(n).wait()
    elif out_ref.dtype == F32:
        total[:, width:] = tall.T
        copy = pltpu.make_async_copy(total, out_ref, arrival)
        copy.start()
        copy.wait()
    else:
        out_ref[:, :width] = total[:, :width].astype(out_ref.dtype)
        out_ref[:, width:] = tall.T.astype(out_ref.dtype)


def start_sums(total, sums, before_ref, arrival):
    sums[...] = jnp.zeros_like(sums)
    if before_ref is None:
        total[...] = jnp.zeros_like(total)
    else:
        pltpu.make_async_copy(before_ref, total, arrival).start()


def await_sums(total, sums, before_ref, arrival):
    if before_ref is not None:
        width = total.shape[1] - SMALL_LANES
        pltpu.make_async_copy(before_ref, total, arrival).wait()
        sums[...] += total[:, width:].T[: sums.shape[0]]


SAVED = ("q", "k", "v", "gate", "probs", "gated", "middle", "act", "slope")


def time_forward_kernel(parts, width_ff, ride, m, x_ref, w_ref, cos_ref, sin_ref, len_ref, *refs):
    step, steps = pl.program_id(0), pl.num_programs(0)
    tick, gather = None, None
    if ride:
        shard_ref, out_ref, refs, full_ref = refs[0], refs[1], refs[2:], refs[11]
        sems = refs[-GATHER_SCRATCH:]
        small_ref, bias_ref = refs[-GATHER_SCRATCH - 2 : -GATHER_SCRATCH]
        if ride == "lines":
            gather = Gather(Place(parts), shard_ref, full_ref, *sems, at_once=False)
            pl.when(step == 0)(gather.start)
            gather.advance(2 * step, 2 * steps)
            tick = partial(gather.advance, 2 * step + 1, 2 * steps)
        else:
            gather = Gather(Place(parts), None, full_ref, *sems)
            pl.when(step == 0)(gather.open_passing)
            pl.when(step == steps - 1)(gather.pass_taken)
    else:
        out_ref, refs = refs[0], refs[1:]
        small_ref, bias_ref = refs[-2:]
    keep = dict(zip(SAVED, refs))

    @pl.when(step == 0)
    def _():
        turn_small(w_ref, small_ref)
        bias_ref[...] = masked_keys(iota((BLOCK, BLOCK), 0) < len_ref[:, m : m + 1])

    per_step, whole_frames, model = x_ref.shape
    x = x_ref[...].astype(F32).reshape(per_step * whole_frames, model)
    out = forward_block(
        x, w_ref, small_parts(small_ref), cos_ref[...], sin_ref[...], bias_ref, keep, 0, 0, width_ff, tick
    )
    frames = out_ref.shape[2]
    for n in range(per_step):
        out_ref[:, n] = out[n * whole_frames : (n + 1) * whole_frames].reshape(parts, frames, model).astype(BF)

    @pl.when(step == steps - 1)
    def _():
        if ride == "lines":
            gather.other_lines()
            gather.finish_lines()
        elif ride:
            gather.finish_passing()


def time_backward_kernel(parts, width_ff, chained, ride, per_step, *refs):
    x_ref, d_ref, w_ref, cos_ref, sin_ref = refs[:5]
    keep = dict(zip(SAVED, refs[5:14]))
    refs = refs[14:]
    before = refs[0] if chained else None
    refs = refs[2 - ride :] if chained else refs
    step, steps = pl.program_id(0), pl.num_programs(0)
    if ride:
        other_ref, dx_ref, grad_ref, shard_ref = refs[:4]
        reduction = Reduction(Place(parts), other_ref, refs[-REDUCE_SCRATCH:])
        refs = refs[:-REDUCE_SCRATCH]
    else:
        dx_ref, grad_ref = refs[:2]
    total, sums, normed, normed_ff, d_hidden, attn_back, branch, d_proj, arrival, small_ref, o_sems = refs[-11:]
    outgoing = Outgoing(total, grad_ref, o_sems, width_ff, step == steps - 1) if grad_ref.dtype == F32 else None
    work = dict(
        normed=normed, normed_ff=normed_ff, d_hidden=d_hidden, attn_back=attn_back, branch=branch, d_proj=d_proj
    )

    @pl.when(step == 0)
    def _():
        start_sums(total, sums, before, arrival)
        turn_small(w_ref, small_ref)

    small = small_parts(small_ref)
    if ride:
        reduction.advance(2 * step, 2 * steps - 1)
    model = x_ref.shape[2]
    x = x_ref[...].astype(F32).reshape(per_step * BLOCK, model)
    work["normed"][...] = (x * inverse_rms(x) * small[1]).astype(BF)
    middle = keep["middle"][...]
    work["normed_ff"][...] = (middle * inverse_rms(middle) * small[2]).astype(BF)
    d_out = jnp.concatenate([d_ref[:, i].astype(F32).reshape(BLOCK, model) for i in range(per_step)], axis=0)
    d_x = backward_block(
        d_out, x, w_ref, small, cos_ref[...], sin_ref[...], keep, work, sums, 0, 0, width_ff,
        partial(reduction.advance, 2 * step + 1, 2 * steps - 1) if ride else None,
    )
    dx_ref[...] = d_x.reshape(dx_ref.shape)
    if chained:

        @pl.when(step == 0)
        def _():
            await_sums(total, sums, before, arrival)

    weight_sums(total, work, keep, width_ff, outgoing.done if outgoing else None)

    @pl.when(step == steps - 1)
    def _():
        finish_sums(total, sums, grad_ref, outgoing, arrival)
        if ride:
            reduction.finish()
            shard_ref[...] = reduction.own[...]
            reduction.drain()


def gather_rows(ref, strides, factors):
    return jnp.concatenate(
        [
            jnp.concatenate([ref[p, s, :] * f for p in range(ref.shape[0])], axis=1)
            for s, f in zip(strides, factors)
        ],
        axis=0,
    )


def band_kernel(width_ff, chained, m, len_ref, *refs):
    x_ref, d_ref, w_ref, cos_ref, sin_ref = refs[:5]
    refs = refs[5:]
    before = refs[0] if chained else None
    out_ref, back_ref, grad_ref = refs[2:5] if chained else refs[:3]
    scratch = refs[-23:]
    keep = dict(zip(SAVED, scratch[:9]))
    total, sums, normed, normed_ff, d_hidden, attn_back, branch, d_proj, arrival, small_ref, o_sems, rows_a, rows_b, bias_ref = scratch[9:]
    work = dict(
        normed=normed, normed_ff=normed_ff, d_hidden=d_hidden, attn_back=attn_back, branch=branch, d_proj=d_proj
    )
    keep.update(normed=normed, normed_ff=normed_ff)
    step = pl.program_id(0)
    bands, frames, model = x_ref.shape
    pieces = model // LANES

    @pl.when(step == 0)
    def _():
        start_sums(total, sums, before, arrival)
        turn_small(w_ref, small_ref)
        same = iota((BLOCK, BLOCK), 0) // bands == iota((BLOCK, BLOCK), 1) // bands
        bias_ref[...] = masked_keys(same)

    small = small_parts(small_ref)
    for p in range(pieces):
        lanes = slice(p * LANES, (p + 1) * LANES)
        rows_a[p] = x_ref[:, :, lanes].astype(F32).reshape(bands * frames, LANES)
        rows_b[p] = d_ref[:, :, lanes].astype(F32).reshape(bands * frames, LANES)
    first = (lax.axis_index("seq") * pl.num_programs(0) + step) * frames

    size = cos_ref.shape[0]
    spread = size // bands

    def one(j, carry):
        start = pl.multiple_of(j * size, size)
        item = j * (size // BLOCK)
        strides = [pl.ds(j * spread + f, bands, stride=frames) for f in range(spread)]
        valid = [(first + j * spread + f < len_ref[0, m]).astype(F32) for f in range(spread)]
        x = gather_rows(rows_a, strides, [1.0] * spread)
        d_out = gather_rows(rows_b, strides, valid)
        out = forward_block(
            x, w_ref, small, cos_ref[...], sin_ref[...], bias_ref, keep, start, item, width_ff
        )
        for f in range(spread):
            for p in range(pieces):
                part = out[f * bands : (f + 1) * bands, p * LANES : (p + 1) * LANES]
                rows_a[p, strides[f], :] = part * valid[f]
        back = backward_block(
            d_out, x, w_ref, small, cos_ref[...], sin_ref[...], keep, work, sums, start, item, width_ff
        )
        for f in range(spread):
            for p in range(pieces):
                part = back[f * bands : (f + 1) * bands, p * LANES : (p + 1) * LANES]
                rows_b[p, strides[f], :] = part
        return carry

    lax.fori_loop(0, bands * frames // size, one, 0)
    for p in range(pieces):
        lanes = slice(p * LANES, (p + 1) * LANES)
        out_ref[:, :, lanes] = rows_a[p].reshape(bands, frames, LANES).astype(BF)
        back_ref[:, :, lanes] = rows_b[p].reshape(bands, frames, LANES).astype(BF)
    if chained:

        @pl.when(step == 0)
        def _():
            await_sums(total, sums, before, arrival)

    weight_sums(total, work, keep, width_ff)

    @pl.when(step == pl.num_programs(0) - 1)
    def _():
        finish_sums(total, sums, grad_ref, None, arrival)


def whole(shape):
    return pl.BlockSpec(shape, lambda *i: (0,) * len(shape), pipeline_mode=pl.Buffered(1))


def params(**more):
    return pltpu.CompilerParams(vmem_limit_bytes=VMEM_LIMIT, **more)


def rotary_tables(positions, rows):
    half_width = HEAD_DIM // 2
    inverse = np.float32(10000.0) ** (-(np.arange(half_width, dtype=np.float32) * np.float32(2.0 / HEAD_DIM)))
    angles = np.arange(positions, dtype=np.float32)[:, None] * inverse[None, :].astype(np.float32)
    angles = np.tile(angles, (rows // positions, LANES // half_width))
    return (jnp.asarray(np.cos(angles), F32), jnp.asarray(np.sin(angles), F32))


def saved_shapes(tokens, items, model, width_ff):
    return (
        ((tokens, INNER_WIDTH), BF),
        ((tokens, INNER_WIDTH), BF),
        ((tokens, INNER_WIDTH), BF),
        ((HEAD_COUNT, tokens), F32),
        ((items, HEAD_COUNT, BLOCK, BLOCK), BF),
        ((tokens, INNER_WIDTH), BF),
        ((tokens, model), F32),
        ((tokens, width_ff), BF),
        ((tokens, width_ff), BF),
    )


def saved_specs(tokens, items, model, width_ff):
    def place(shape):
        if shape[0] == HEAD_COUNT:
            return pl.BlockSpec(shape, lambda i, *s: (0, i))
        return pl.BlockSpec(shape, lambda i, *s: (i,) + (0,) * (len(shape) - 1))

    return [place(shape) for shape, kind in saved_shapes(tokens, items, model, width_ff)]


def work_shapes(tokens, model, width_ff, columns):
    return [
        pltpu.VMEM((model, columns), F32),
        pltpu.VMEM((2 * HEAD_COUNT, model), F32),
        pltpu.VMEM((tokens, model), BF),
        pltpu.VMEM((tokens, model), BF),
        pltpu.VMEM((tokens, width_ff), BF),
        pltpu.VMEM((tokens, model), BF),
        pltpu.VMEM((tokens, model), BF),
        pltpu.VMEM((tokens, 3 * INNER_WIDTH), BF),
        pltpu.SemaphoreType.DMA,
        pltpu.VMEM((2 * HEAD_COUNT, model), F32),
        pltpu.SemaphoreType.DMA((5,)),
    ]


def at_micro(m, shape, place):
    return pl.BlockSpec((None, None) + shape, lambda i, *s: (m, 0) + place(i))


def sequences(seqs):
    return 2 if seqs % 2 == 0 else 1


def time_forward(m, x, lengths, weights, tables, ride, other, parts, width_ff):
    seqs, frames, model = x.shape[2:]
    tokens = seqs * frames
    shapes = saved_shapes(tokens, seqs, model, width_ff)
    out = jax.ShapeDtypeStruct((parts, seqs, frames // parts, model), BF)
    per_step = sequences(seqs)
    any_space = pl.BlockSpec(memory_space=pl.ANY)
    riding = 1 if ride else 0
    full = [jax.ShapeDtypeStruct((parts,) + other.shape[-2:], BF)] * riding
    aliases = {5: 1 + len(SAVED)} if ride == "pass" else {}
    results = pl.pallas_call(
        partial(time_forward_kernel, parts, width_ff, ride, m),
        grid=(seqs // per_step,),
        in_specs=[
            at_micro(m, (per_step, frames, model), lambda i: (i, 0, 0)),
            whole(weights.shape),
            whole(tables[0].shape),
            whole(tables[1].shape),
            whole(lengths.shape),
        ]
        + [any_space] * riding,
        out_specs=[
            pl.BlockSpec((parts, per_step, frames // parts, model), lambda i: (0, i, 0, 0)),
            *saved_specs(per_step * frames, per_step, model, width_ff),
        ]
        + [any_space] * riding,
        scratch_shapes=[pltpu.VMEM((2 * HEAD_COUNT, model), F32), pltpu.VMEM((BLOCK, BLOCK), F32)]
        + (gather_scratch(parts) if ride else []),
        out_shape=[out, *(jax.ShapeDtypeStruct(s, k) for s, k in shapes)] + full,
        input_output_aliases=aliases,
        compiler_params=params(collective_id=3 if ride == "lines" else 5, has_side_effects=True) if ride else params(),
        cost_estimate=pl.CostEstimate(
            flops=int(tokens * 5e6), bytes_accessed=tokens * 15000, transcendentals=tokens * 5000
        ),
        name="time_forward_" + ride if ride else "time_forward",
    )(x, weights, *tables, lengths, *([other] if ride else []))
    saved = results[1 : 1 + len(SAVED)]
    return results[0], saved, (results[-1] if ride else other)


def time_backward(m, x, d_out, weights, tables, saved, before, other, kind, width_ff):
    seqs, frames, model = x.shape[2:]
    tokens = seqs * frames
    parts, unused, part_frames, unused_model = d_out.shape
    per_step = sequences(seqs)
    columns = weights.shape[1]
    ride = other is not None
    if ride:
        before = before[:1]
    ins = [x, d_out, weights, *tables, *saved, *before]
    aliases = {len(ins) - 1: 0} if len(before) == 2 else {}
    target = (1, 1) + x.shape[2:] if ride else x.shape
    more_specs, more_shapes, scratch = [], [], []
    any_space = pl.BlockSpec(memory_space=pl.ANY)
    if ride:
        zs, ys = seq_sides(parts)
        part = model // parts
        ins.append(other.reshape(zs, ys, part, columns))
        more_shapes = [jax.ShapeDtypeStruct((part, columns // 2), BF)]
        more_specs = [whole(more_shapes[0].shape)]
        scratch = reduce_scratch(parts, part, columns)
    rows = at_micro(m, (per_step, frames, model), lambda i: (i, 0, 0))
    return pl.pallas_call(
        partial(time_backward_kernel, parts, width_ff, bool(before), ride, per_step),
        grid=(seqs // per_step,),
        in_specs=[
            rows,
            pl.BlockSpec((parts, per_step, part_frames, model), lambda i: (0, i, 0, 0)),
            whole(weights.shape),
            whole(tables[0].shape),
            whole(tables[1].shape),
            *saved_specs(per_step * frames, per_step, model, width_ff),
        ]
        + [any_space] * (len(before) + ride),
        out_specs=[
            at_micro(0 if ride else m, (per_step, frames, model), lambda i: (i, 0, 0)),
            any_space if kind == F32 else whole((model, columns)),
        ]
        + more_specs,
        out_shape=[
            jax.ShapeDtypeStruct(target, F32),
            jax.ShapeDtypeStruct((model, columns), kind),
        ]
        + more_shapes,
        input_output_aliases=aliases,
        scratch_shapes=work_shapes(per_step * frames, model, width_ff, columns) + scratch,
        compiler_params=params(collective_id=4, has_side_effects=True) if ride else params(),
        cost_estimate=pl.CostEstimate(
            flops=int(tokens * 9e6), bytes_accessed=tokens * 18000, transcendentals=0
        ),
        name="time_backward_reduce" if ride else "time_backward",
    )(*ins)


def band_both(m, x, d_out, lengths, weights, tables, before, kind, width_ff):
    bands, frames, model = x.shape
    tokens = bands * frames
    chunk = math.gcd(frames, 16)
    step_tokens = bands * chunk
    columns = weights.shape[1]
    ins = [lengths, x, d_out, weights, *tables, *before]
    rows = pl.BlockSpec((bands, chunk, model), lambda i, s: (0, i, 0))
    rows_m = at_micro(m, (bands, chunk, model), lambda i: (0, i, 0))
    any_space = pl.BlockSpec(memory_space=pl.ANY)
    saved = [
        pltpu.VMEM(s, k) for s, k in saved_shapes(step_tokens, step_tokens // BLOCK, model, width_ff)
    ]
    return pl.pallas_call(
        partial(band_kernel, width_ff, bool(before), m),
        grid_spec=pltpu.PrefetchScalarGridSpec(
            num_scalar_prefetch=1,
            grid=(frames // chunk,),
            in_specs=[
                rows,
                rows_m,
                whole(weights.shape),
                whole(tables[0].shape),
                whole(tables[1].shape),
            ]
            + [any_space] * len(before),
            out_specs=[rows_m, rows, any_space if kind == F32 else whole((model, columns))],
            scratch_shapes=saved
            + work_shapes(step_tokens, model, width_ff, columns)
            + [pltpu.VMEM((model // LANES, step_tokens, LANES), F32)] * 2
            + [pltpu.VMEM((BLOCK, BLOCK), F32)],
        ),
        out_shape=[
            jax.ShapeDtypeStruct(d_out.shape, BF),
            jax.ShapeDtypeStruct(x.shape, BF),
            jax.ShapeDtypeStruct((model, columns), kind),
        ],
        input_output_aliases={len(ins) - 1: 0} if before else {},
        compiler_params=params(),
        cost_estimate=pl.CostEstimate(
            flops=int(tokens * 14e6), bytes_accessed=tokens * 8000, transcendentals=tokens * 5000
        ),
        name="band_both",
    )(*ins)


MESH = pl.DeviceIdType.MESH


def seq_sides(parts):
    side = 1
    while 4 * side * side <= parts:
        side *= 2
    return parts // side, side


class Place:
    def __init__(self, parts):
        self.dp, self.seq = lax.axis_index("dp"), lax.axis_index("seq")
        self.core = self.dp % 2
        self.zs, self.ys = seq_sides(parts)
        self.z, self.y = self.seq // self.ys, self.seq % self.ys

    def sibling(self):
        return (self.dp + 1 - 2 * self.core, self.seq)

    def along_z(self, step):
        return (self.dp, self.seq + step * self.ys)

    def along_y(self, step):
        return (self.dp, self.seq + step)

    def has_z(self, step):
        return self.z + step < self.zs if step > 0 else self.z + step >= 0

    def has_y(self, step):
        return self.y + step < self.ys if step > 0 else self.y + step >= 0


def greet(place, others=()):
    barrier = pltpu.get_barrier_semaphore()
    pl.semaphore_signal(barrier, inc=1, device_id=place.sibling(), device_id_type=MESH)
    for other in others:
        pl.semaphore_signal(barrier, inc=1, device_id=other, device_id_type=MESH)
    for step in (1, -1):
        for has, to in ((place.has_z, place.along_z), (place.has_y, place.along_y)):

            @pl.when(has(step))
            def _(to=to, step=step):
                pl.semaphore_signal(barrier, inc=1, device_id=to(step), device_id_type=MESH)

    count = 1 + len(others)
    for has in (place.has_z, place.has_y):
        count = count + has(1).astype(jnp.int32) + has(-1).astype(jnp.int32)
    pl.semaphore_wait(barrier, count)


GATHER_SCRATCH = 9


class Gather:
    def __init__(
        self, place, shard_ref, out_ref, send_z, send_y, send_c, got, got_c, local, send_x, got_x, send_cx, at_once=True
    ):
        self.place, self.shard, self.out, self.at_once = place, shard_ref, out_ref, at_once
        self.send_z, self.send_y, self.send_c, self.got, self.got_c, self.local = send_z, send_y, send_c, got, got_c, local
        self.send_x, self.got_x, self.send_cx = send_x, got_x, send_cx
        wide = out_ref.shape[2] // 2
        self.blocks = place.zs * place.ys
        self.crossing = lax.axis_size("dp") == 4 and wide % (3 * LANES) == 0
        third = wide // 3
        x = place.dp // 2

        def columns(core, start, size):
            return pl.ds(pl.multiple_of(core * wide + start, LANES), size)

        if self.crossing:
            self.lanes = columns(place.core, x * third, 2 * third)
            self.other_lanes = columns(1 - place.core, x * third, 2 * third)
            self.given = columns(place.core, x * 2 * third, third)
            self.taken = columns(place.core, (1 - x) * 2 * third, third)
            self.other_taken = columns(1 - place.core, (1 - x) * 2 * third, third)
            self.across = (lax.rem(place.dp + 2, 4), place.seq)
            self.pieces = [self.lanes]
        else:
            self.lanes = columns(place.core, 0, wide)
            self.other_lanes = columns(1 - place.core, 0, wide)
            self.pieces = [self.lanes]
        self.hops = place.zs
        self.others = [lax.rem(place.seq + turn, self.blocks) for turn in range(1, self.blocks)]

    def index(self, z, y):
        return z * self.place.ys + y

    def held(self, p, k):
        return self.out.at[p, :, self.pieces[k]]

    def mine(self, k):
        return self.shard.at[:, self.pieces[k]]

    def push(self, source, p, k, to, send, receive):
        return pltpu.make_async_remote_copy(
            src_ref=source, dst_ref=self.held(p, k), send_sem=send, recv_sem=receive, device_id=to, device_id_type=MESH
        )

    def same(self, p, lanes, to, send, receive):
        there = self.out.at[p, :, lanes]
        return pltpu.make_async_remote_copy(
            src_ref=there, dst_ref=there, send_sem=send, recv_sem=receive, device_id=to, device_id_type=MESH
        )

    def to_sibling(self, p):
        return self.same(p, self.lanes, self.place.sibling(), self.send_c.at[p], self.got_c.at[0, p])

    def from_sibling(self, p):
        return self.same(p, self.other_lanes, self.place.sibling(), self.send_c.at[p], self.got_c.at[0, p])

    def give(self, p):
        return self.same(p, self.given, self.across, self.send_x.at[p], self.got_x.at[p])

    def take(self, p):
        return self.same(p, self.taken, self.across, self.send_x.at[p], self.got_x.at[p])

    def taken_to_sibling(self, p):
        return self.same(p, self.taken, self.place.sibling(), self.send_cx.at[p], self.got_c.at[1, p])

    def taken_from_sibling(self, p):
        return self.same(p, self.other_taken, self.place.sibling(), self.send_cx.at[p], self.got_c.at[1, p])

    def along_z(self, source, p, k, step, t):
        side = (step + 1) // 2
        return self.push(source, p, k, self.place.along_z(step), self.send_z.at[side, t, k], self.got.at[p, k])

    def along_y(self, source, p, k, step):
        side = (step + 1) // 2
        return self.push(source, p, k, self.place.along_y(step), self.send_y.at[side, p, k], self.got.at[p, k])

    def await_block(self, p, k):
        self.push(self.held(p, k), p, k, self.place.sibling(), self.send_c.at[p], self.got.at[p, k]).wait_recv()

    def hand_on(self, p):
        if self.at_once:
            self.pass_on(p)

    def pass_on(self, p):
        if self.crossing:
            self.give(p).start()
        self.to_sibling(p).start()

    def open_passing(self):
        barrier = pltpu.get_barrier_semaphore()
        peers = [self.place.sibling()] + ([self.across] if self.crossing else [])
        for to in peers:
            pl.semaphore_signal(barrier, inc=1, device_id=to, device_id_type=MESH)
        pl.semaphore_wait(barrier, len(peers))
        for p in self.others:
            self.pass_on(p)

    def own(self):
        return pltpu.make_async_copy(self.shard, self.out.at[self.place.seq], self.local)

    def start(self):
        place = self.place
        greet(place, [self.across] if self.crossing else [])
        self.own().start()
        for k in range(len(self.pieces)):
            for step in (1, -1):

                @pl.when(place.has_z(step))
                def _(k=k, step=step):
                    self.along_z(self.mine(k), place.seq, k, step, 0).start()

                @pl.when(place.has_y(step))
                def _(k=k, step=step):
                    self.along_y(self.mine(k), place.seq, k, step).start()

    def advance(self, slot, slots):
        for hop in range(1, self.hops):
            due = (hop * (slots - 2) + self.hops - 2) // (self.hops - 1) if self.hops > 1 else 0
            pl.when(slot == due)(partial(self.hop, hop))

    def hop(self, t):
        if t == self.place.zs:
            return self.other_lines()
        place = self.place
        for step in (1, -1):
            z = place.z - step * t
            here = (z >= 0) if step > 0 else (z < place.zs)

            @pl.when(here)
            def _(step=step, z=z):
                p = self.index(z, place.y)
                for k in range(len(self.pieces)):
                    self.await_block(p, k)
                    if t < place.zs - 1:
                        pl.when(place.has_z(step))(
                            lambda k=k: self.along_z(self.held(p, k), p, k, step, t).start()
                        )
                    for side in (1, -1):
                        pl.when(place.has_y(side))(
                            lambda k=k, side=side: self.along_y(self.held(p, k), p, k, side).start()
                        )
                self.hand_on(p)

    def other_lines(self):
        place = self.place
        for t in range(1, place.ys):
            for step in (1, -1):
                y = place.y - step * t
                here = (y >= 0) if step > 0 else (y < place.ys)

                @pl.when(here)
                def _(t=t, step=step, y=y):
                    for turn in range(place.zs):
                        p = self.index(lax.rem(place.z + turn, place.zs), y)
                        for k in range(len(self.pieces)):
                            self.await_block(p, k)
                            if t < place.ys - 1:
                                pl.when(place.has_y(step))(
                                    lambda p=p, k=k: self.along_y(self.held(p, k), p, k, step).start()
                                )
                        self.hand_on(p)

    def pass_taken(self):
        if self.crossing:
            for p in self.others:
                self.take(p).wait_recv()
                self.taken_to_sibling(p).start()

    def finish_passing(self):
        for p in self.others:
            self.to_sibling(p).wait_send()
            self.from_sibling(p).wait_recv()
        if self.crossing:
            for p in self.others:
                self.give(p).wait_send()
                self.taken_to_sibling(p).wait_send()
                self.taken_from_sibling(p).wait_recv()

    def finish_lines(self):
        place = self.place
        self.own().wait()
        for step in (1, -1):
            for t in range(place.zs - 1):
                z = place.z - step * t
                sent = jnp.logical_and((z >= 0) if step > 0 else (z < place.zs), place.has_z(step))

                @pl.when(sent)
                def _(step=step, t=t):
                    for k in range(len(self.pieces)):
                        self.along_z(self.mine(k), place.seq, k, step, t).wait_send()

            for t in range(place.ys - 1):
                y = place.y - step * t
                sent = jnp.logical_and((y >= 0) if step > 0 else (y < place.ys), place.has_y(step))

                @pl.when(sent)
                def _(step=step, y=y):
                    for z in range(place.zs):
                        for k in range(len(self.pieces)):
                            self.along_y(self.mine(k), self.index(z, y), k, step).wait_send()


def gather_kernel(parts, shard_ref, out_ref, *sems):
    gather = Gather(Place(parts), shard_ref, out_ref, *sems)
    gather.start()
    for hop in range(1, gather.hops + 1):
        gather.hop(hop)
    gather.pass_taken()
    gather.finish_passing()
    gather.finish_lines()


def gather_scratch(parts):
    zs, ys = seq_sides(parts)
    dma = pltpu.SemaphoreType.DMA
    each = dma((parts,))
    return [dma((2, zs, 2)), dma((2, parts, 2)), each, dma((parts, 2)), dma((2, parts)), dma, each, each, each]


def gather_weights(shard, parts):
    rows, columns = shard.shape
    out = pl.pallas_call(
        partial(gather_kernel, parts),
        in_specs=[pl.BlockSpec(memory_space=pl.ANY)],
        out_specs=pl.BlockSpec(memory_space=pl.ANY),
        out_shape=jax.ShapeDtypeStruct((parts, rows, columns), shard.dtype),
        scratch_shapes=gather_scratch(parts),
        compiler_params=params(collective_id=1, has_side_effects=True),
        cost_estimate=pl.CostEstimate(flops=0, bytes_accessed=parts * rows * columns * 40, transcendentals=0),
        name="gather_weights",
    )(shard)
    return out.reshape(parts * rows, columns)


def add_into(acc, other):
    acc[...] = (acc[...].astype(F32) + other[...].astype(F32)).astype(acc.dtype)


class Line:
    def __init__(self, i, n, to, acc, slot, count, sends, receives):
        self.i, self.n, self.to, self.acc, self.slot, self.count = i, n, to, acc, slot, count
        self.sends, self.receives = sends, receives

    def copy(self, side, j, k):
        return pltpu.make_async_remote_copy(
            src_ref=self.acc(j, k),
            dst_ref=self.slot(side, j, k),
            send_sem=self.sends.at[side, j, k],
            recv_sem=self.receives.at[side, j, k],
            device_id=self.to(1 - 2 * side),
            device_id_type=MESH,
        )

    def take(self, side, j, k):
        self.copy(side, j, k).wait_recv()
        add_into(self.acc(j, k), self.slot(side, j, k))

    def send_pair(self, k):
        pl.when(self.i == 0)(lambda: self.copy(0, 1, k).start())
        pl.when(self.i == 1)(lambda: self.copy(1, 0, k).start())

    def send(self, now, base):
        for t in range(self.n - 1):
            for side, j, passed in ((0, self.n - 1 - t, self.i), (1, t, self.n - 1 - self.i)):
                beyond = self.i < j if side == 0 else self.i > j
                inner = self.i > 0 if side == 0 else self.i < self.n - 1

                @pl.when(jnp.logical_and(beyond, now(base + passed + t)))
                def _(side=side, j=j, inner=inner):
                    for k in range(self.count):
                        if self.n > 2:
                            pl.when(inner)(lambda k=k: self.take(side, j, k))
                        self.copy(side, j, k).start()

    def finish(self):
        for side, inner in ((0, self.i > 0), (1, self.i < self.n - 1)):

            @pl.when(inner)
            def _(side=side):
                for k in range(self.count):
                    self.take(side, self.i, k)

    def drain(self):
        for j in range(self.n):
            for side, beyond in ((0, self.i < j), (1, self.i > j)):

                @pl.when(beyond)
                def _(side=side, j=j):
                    for k in range(self.count):
                        self.copy(side, j, k).wait_send()


def first_columns(wide):
    return wide // LANES // 3 * 2 * LANES


REDUCE_SCRATCH = 17
ACROSS_SCRATCH = 6


def reduce_scratch(parts, rows, columns):
    zs, ys = seq_sides(parts)
    wide = columns // 2
    first = first_columns(wide)
    rest = wide - first
    dma = pltpu.SemaphoreType.DMA
    return [
        pltpu.VMEM((zs, ys, rows, wide), BF),
        pltpu.VMEM((zs, ys, rows, wide), BF),
        pltpu.VMEM((2, ys, zs, rows, first), BF),
        pltpu.VMEM((2, zs, ys, rows, rest), BF),
        pltpu.VMEM((2, zs, 2, rows, first // 2), BF),
        pltpu.VMEM((2, ys, 1, rows, rest), BF),
        dma((zs,)),
        dma((zs,)),
        dma((zs,)),
        dma((2, ys, zs)),
        dma((2, ys, zs)),
        dma((2, zs, ys)),
        dma((2, zs, ys)),
        dma((2, zs, 2)),
        dma((2, zs, 2)),
        dma((2, ys, 1)),
        dma((2, ys, 1)),
    ]


def across_scratch(replicas, rows, columns):
    xs = replicas // 2
    wide = columns // 2
    dma = pltpu.SemaphoreType.DMA
    return [
        pltpu.VMEM((xs, rows, wide), BF),
        pltpu.VMEM((2, rows, wide), F32),
        dma((max(xs - 1, 1), 2)),
        dma((xs, 2)),
        dma,
        dma,
    ]


class Across:
    def __init__(self, place, own, scratch):
        self.place, self.own = place, own
        self.in_x, self.fin, self.s_x, self.g_x, self.s_f, self.g_f = scratch
        self.xs = self.in_x.shape[0]
        self.x = place.dp // 2
        self.peers = [(lax.rem(self.x + t, self.xs) * 2 + place.core, place.seq) for t in range(1, self.xs)]

    def columns(self, piece):
        wide = self.own.shape[-1]
        first = first_columns(wide)
        return pl.ds(first, wide - first) if piece else pl.ds(0, first)

    def copy(self, t, there, piece):
        lanes = self.columns(piece)
        return pltpu.make_async_remote_copy(
            src_ref=self.own.at[:, lanes],
            dst_ref=self.in_x.at[there, :, lanes],
            send_sem=self.s_x.at[t, piece],
            recv_sem=self.g_x.at[there, piece],
            device_id=self.peers[t],
            device_id_type=MESH,
        )

    def half(self, c):
        return pltpu.make_async_remote_copy(
            src_ref=self.fin.at[c],
            dst_ref=self.fin.at[c],
            send_sem=self.s_f,
            recv_sem=self.g_f,
            device_id=self.place.sibling(),
            device_id_type=MESH,
        )

    def start(self, piece):
        for t in range(self.xs - 1):
            self.copy(t, self.x, piece).start()
        lanes = self.columns(piece)
        self.in_x[self.x, :, lanes] = self.own[:, lanes]

    def fold(self):
        for t in range(self.xs - 1):
            for piece in range(2):
                self.copy(t, lax.rem(self.x + t + 1, self.xs), piece).wait_recv()
        total = self.in_x[0].astype(F32)
        for t in range(1, self.xs):
            total = total + self.in_x[t].astype(F32)
        self.fin[self.place.core] = total
        self.half(self.place.core).start()

    def finish(self, out_ref):
        self.half(1 - self.place.core).wait_recv()
        squares = 0.0
        for c in range(2):
            value = self.fin[c]
            out_ref[c] = value
            squares = squares + jnp.sum(value * value, axis=(0, 1), keepdims=True)
        return squares

    def drain(self):
        for t in range(self.xs - 1):
            for piece in range(2):
                self.copy(t, self.x, piece).wait_send()
        self.half(self.place.core).wait_send()


class Reduction:
    def __init__(self, place, grad_ref, scratch):
        self.place, self.grad = place, grad_ref
        self.acc, self.in_c, in_ya, in_zb, in_za, in_yb = scratch[:6]
        self.local, self.s_c, self.g_c, s_ya, g_ya, s_zb, g_zb, s_za, g_za, s_yb, g_yb = scratch[6:]
        acc = self.acc
        zs, ys = place.zs, place.ys
        wide = acc.shape[-1]
        first = first_columns(wide)
        a, b = pl.ds(0, first), pl.ds(first, wide - first)
        self.lanes = pl.ds(pl.multiple_of(place.core * wide, LANES), wide)
        self.other = pl.ds(pl.multiple_of((1 - place.core) * wide, LANES), wide)
        self.line_ya = Line(
            place.y, ys, place.along_y, lambda j, k: acc.at[k, j, :, a], lambda s, j, k: in_ya.at[s, j, k], zs, s_ya, g_ya
        )
        self.line_zb = Line(
            place.z, zs, place.along_z, lambda j, k: acc.at[j, k, :, b], lambda s, j, k: in_zb.at[s, j, k], ys, s_zb, g_zb
        )
        pieces = [pl.ds(k * (first // 2), first // 2) for k in range(2)]
        self.line_za = Line(
            place.z,
            zs,
            place.along_z,
            lambda j, k: acc.at[j, place.y, :, pieces[k]],
            lambda s, j, k: in_za.at[s, j, k],
            2,
            s_za,
            g_za,
        )
        self.line_yb = Line(
            place.y, ys, place.along_y, lambda j, k: acc.at[place.z, j, :, b], lambda s, j, k: in_yb.at[s, j, k], 1, s_yb, g_yb
        )
        self.own = acc.at[place.z, place.y]

    def mine(self, z):
        return pltpu.make_async_copy(self.grad.at[z, :, :, self.lanes], self.acc.at[z], self.local.at[z])

    def swap(self, z):
        return pltpu.make_async_remote_copy(
            src_ref=self.grad.at[z, :, :, self.other],
            dst_ref=self.in_c.at[z],
            send_sem=self.s_c.at[z],
            recv_sem=self.g_c.at[z],
            device_id=self.place.sibling(),
            device_id_type=MESH,
        )

    def open(self, greeting):
        for z in range(self.place.zs):
            self.mine(z).start()
        greeting()
        for z in range(self.place.zs):
            self.swap(z).start()

    def fold_cores(self):
        for z in range(self.place.zs):
            self.mine(z).wait()
            self.swap(z).wait_recv()
            for y in range(self.place.ys):
                add_into(self.acc.at[z, y], self.in_c.at[z, y])
            if self.place.ys == 2:
                self.line_ya.send_pair(z)

    def advance(self, slot, last):
        def now(time):
            return slot == jnp.minimum(time, last)

        zs, ys = self.place.zs, self.place.ys
        pl.when(now(0))(lambda: self.open(lambda: greet(self.place)))
        pl.when(now(1))(self.fold_cores)
        if ys != 2:
            self.line_ya.send(now, 1)
        self.line_zb.send(now, 1)
        ready = max(zs, ys + 1)
        pl.when(now(ready))(self.line_zb.finish)
        self.line_yb.send(now, ready)
        pl.when(now(ready))(self.line_ya.finish)
        self.line_za.send(now, ready)

    def finish(self):
        self.line_yb.finish()
        self.line_za.finish()

    def drain(self):
        for line in (self.line_ya, self.line_zb, self.line_za, self.line_yb):
            line.drain()
        for z in range(self.place.zs):
            self.swap(z).wait_send()


def reduce_kernel(parts, grad_ref, band_ref, out_ref, norm_ref, squares, s_n, g_n, *scratch):
    place = Place(parts)
    peers = [(place.dp, lax.rem(place.seq + t, parts)) for t in range(1, parts)]
    reduction = Reduction(place, grad_ref, scratch[:REDUCE_SCRATCH])
    band = Across(place, band_ref, scratch[REDUCE_SCRATCH : REDUCE_SCRATCH + ACROSS_SCRATCH])
    time = Across(place, reduction.own, scratch[REDUCE_SCRATCH + ACROSS_SCRATCH :])

    def greeting():
        barrier = pltpu.get_barrier_semaphore()
        everyone = [place.sibling()] + time.peers + peers
        for to in everyone:
            pl.semaphore_signal(barrier, inc=1, device_id=to, device_id_type=MESH)
        pl.semaphore_wait(barrier, len(everyone))

    def always(time):
        return True

    reduction.open(greeting)
    reduction.fold_cores()
    band.start(0)
    band.start(1)
    if place.ys != 2:
        reduction.line_ya.send(always, 0)
    reduction.line_zb.send(always, 0)
    reduction.line_zb.finish()
    reduction.line_yb.send(always, 0)
    band.fold()
    reduction.line_ya.finish()
    reduction.line_za.send(always, 0)
    reduction.line_yb.finish()
    time.start(1)
    partial_sum = band.finish(out_ref.at[1])
    reduction.line_za.finish()
    time.start(0)
    time.fold()
    partial_sum = partial_sum + time.finish(out_ref.at[0])
    squares[place.seq] = jnp.broadcast_to(partial_sum, squares.shape[1:])

    def tell(t, there):
        return pltpu.make_async_remote_copy(
            src_ref=squares.at[there],
            dst_ref=squares.at[there],
            send_sem=s_n.at[t],
            recv_sem=g_n.at[there],
            device_id=peers[t],
            device_id_type=MESH,
        )

    for t in range(parts - 1):
        tell(t, place.seq).start()
    for t in range(parts - 1):
        tell(t, lax.rem(place.seq + t + 1, parts)).wait_recv()
    norm = squares[0]
    for p in range(1, parts):
        norm = norm + squares[p]
    norm_ref[...] = norm
    for t in range(parts - 1):
        tell(t, place.seq).wait_send()
    reduction.drain()
    band.drain()
    time.drain()


def reduce_gradient(grad, band, parts, replicas):
    zs, ys = seq_sides(parts)
    rows, columns = grad.shape[0] // parts, grad.shape[1]
    dma = pltpu.SemaphoreType.DMA
    in_vmem = pl.BlockSpec(memory_space=pltpu.VMEM)
    return pl.pallas_call(
        partial(reduce_kernel, parts),
        in_specs=[pl.BlockSpec(memory_space=pl.ANY), in_vmem],
        out_specs=[in_vmem, in_vmem],
        out_shape=[
            jax.ShapeDtypeStruct((2, 2, rows, columns // 2), F32),
            jax.ShapeDtypeStruct((8, LANES), F32),
        ],
        scratch_shapes=[pltpu.VMEM((parts, 8, LANES), F32), dma((parts - 1,)), dma((parts,))]
        + reduce_scratch(parts, rows, columns)
        + across_scratch(replicas, rows, columns) * 2,
        compiler_params=params(collective_id=2, has_side_effects=True),
        cost_estimate=pl.CostEstimate(flops=0, bytes_accessed=columns * rows * parts * 60, transcendentals=0),
        name="reduce_gradient",
    )(grad.reshape(zs, ys, rows, columns), band)


def rotary_order(columns):
    lead = columns.shape[:-1]
    split = columns.reshape(lead + (-1, 4, 2, HEAD_DIM // 2))
    return jnp.swapaxes(split, -3, -2).reshape(columns.shape)


def adam_step(master, gradient, first_old, second_old, learn_rate):
    first_new = BETA_ONE * first_old + (1.0 - BETA_ONE) * gradient
    second_new = BETA_TWO * second_old + (1.0 - BETA_TWO) * gradient * gradient
    first_hat = first_new / (1.0 - BETA_ONE**STEP)
    second_hat = second_new / (1.0 - BETA_TWO**STEP)
    updated = master - learn_rate * (first_hat / (jnp.sqrt(second_hat) + ADAM_EPS) + DECAY * master)
    return (updated, first_new, second_new)


def heads_in_order(first, second):
    half = HEAD_DIM // 2
    lane = iota(first.shape, 1) // half

    def turn(t, places):
        return pltpu.roll(t, places % LANES, 1) if places % LANES else t

    results = []
    for low in (0, 2):
        pieces = [turn(first, -low * half), turn(second, half - low * half)]
        pieces += [turn(first, half - low * half), turn(second, 2 * half - low * half)]
        out = pieces[0]
        for place in range(1, 4):
            out = jnp.where(lane == place, pieces[place], out)
        results.append(out)
    return results


def update_kernel(grads_ref, squares_ref, *refs):
    masters, firsts, seconds = refs[0:2], refs[2:4], refs[4:6]
    outs = refs[6:]
    norm = jnp.sqrt(squares_ref[0:1, 0:1])
    factor = jnp.minimum(1.0, CLIP_NORM / (norm + 1e-06))
    half = grads_ref.shape[2]
    width_in, width_out = (ref.shape[1] for ref in masters)

    def gradient(start, size):
        return grads_ref[start // half, :, start % half : start % half + size] * factor

    def update(which, column, size, grad, rate):
        part = slice(column, column + size)
        new = adam_step(
            masters[which][:, part], grad, firsts[which][:, part], seconds[which][:, part], rate
        )
        for k in range(3):
            outs[2 * k + which][:, part] = new[k]
        outs[6 + which][:, part] = new[0].astype(BF)

    for start in range(0, 2 * INNER_WIDTH, GROUP):
        pair = heads_in_order(gradient(start, LANES), gradient(start + LANES, LANES))
        for n in range(2):
            update(0, start + n * LANES, LANES, pair[n], RATE_MATRIX)
    for which, width, base, begin in ((0, width_in, 0, 2 * INNER_WIDTH), (1, width_out, width_in, 0)):
        for column in range(begin, width, LANES):
            update(which, column, LANES, gradient(base + column, LANES), RATE_MATRIX)


def update_weights(grads, squares, masters, firsts, seconds):
    states = [*masters, *firsts, *seconds]

    def by_layer(t):
        return pl.BlockSpec((None,) + t.shape[1:], lambda i: (i, 0, 0))

    return pl.pallas_call(
        update_kernel,
        grid=(2,),
        in_specs=[pl.BlockSpec((None,) + grads.shape[1:], lambda i: (i, 0, 0, 0)), whole(squares.shape)]
        + [by_layer(t) for t in states],
        out_specs=[by_layer(t) for t in states + list(masters)],
        out_shape=[jax.ShapeDtypeStruct(t.shape, F32) for t in states]
        + [jax.ShapeDtypeStruct(t.shape, BF) for t in masters],
        compiler_params=params(),
        name="update_weights",
    )(grads, squares, *states)


def body(
    activations,
    cotangent,
    lengths,
    weight_in,
    weight_out,
    weight_small,
    first_in,
    first_out,
    first_small,
    second_in,
    second_out,
    second_small,
):
    parts = lax.axis_size("seq")
    lengths = lengths.reshape(1, -1)
    micro, unused, band_dev, frames, model = activations.shape
    bands, frame_dev = cotangent.shape[2], cotangent.shape[3]
    turned = 2 * INNER_WIDTH
    width_in, width_out = weight_in.shape[2], weight_out.shape[2]
    width_ff = width_in - 3 * INNER_WIDTH
    small_width = weight_small.shape[2]
    packed = [
        jnp.concatenate(
            [
                rotary_order(weight_in[layer, :, :turned].astype(BF)),
                weight_in[layer, :, turned:].astype(BF),
                weight_out[layer].astype(BF),
                jnp.pad(weight_small[layer].astype(BF), ((0, 0), (0, SMALL_LANES - small_width))),
            ],
            axis=1,
        )
        for layer in range(2)
    ]
    time_weights = gather_weights(packed[0], parts)
    time_tables = rotary_tables(frames, sequences(band_dev) * frames)
    band_tables = rotary_tables(bands, min(2 * BLOCK, frame_dev * bands))

    def exchange(tensor):
        return lax.all_to_all(tensor, "seq", split_axis=0, concat_axis=0, tiled=True)

    streams, saves, other = [], [], packed[1]
    for m in range(micro):
        ride = "lines" if m == 0 else "pass" if m == 1 else ""
        out, saved, other = time_forward(
            m, activations, lengths, time_weights, time_tables, ride, other, parts, width_ff
        )
        saves.append(saved)
        streams.append(exchange(out).reshape(bands, frame_dev, model))
    band_weights = other.reshape(model, -1)
    backs, before = [], ()
    for m in range(micro):
        kind = BF if m == micro - 1 else F32
        output, back, grad_band = band_both(
            m, streams[m], cotangent, lengths, band_weights, band_tables, before, kind, width_ff
        )
        before = (grad_band, output)
        backs.append(exchange(back.reshape(parts, band_dev, frame_dev, model)))
    before = ()
    for m in range(micro):
        kind = BF if m == micro - 1 else F32
        part, grad_time, *shard = time_backward(
            m,
            activations,
            backs[m],
            time_weights,
            time_tables,
            saves[m],
            before,
            grad_band if m == micro - 1 else None,
            kind,
            width_ff,
        )
        if m < micro - 1:
            d_input = part
            before = (grad_time, d_input)
        else:
            d_input = lax.dynamic_update_slice(d_input, part, (m, 0, 0, 0, 0))
    grads, squares = reduce_gradient(grad_time, shard[0], parts, lax.axis_size("dp"))
    new = update_weights(grads, squares, (weight_in, weight_out), (first_in, first_out), (second_in, second_out))
    norm = jnp.sqrt(squares[0, 0])
    factor = jnp.minimum(1.0, CLIP_NORM / (norm + 1e-06))
    start = width_in + width_out - grads.shape[3]
    rate = jnp.where(jnp.arange(small_width) < HEAD_COUNT, RATE_GATE, RATE_GAIN)

    def columns_first(t):
        return jnp.transpose(t, (2, 0, 1))

    small = adam_step(
        columns_first(weight_small),
        columns_first(grads[:, 1, :, start : start + small_width]) * factor,
        columns_first(first_small),
        columns_first(second_small),
        rate[:, None, None],
    )
    small = [jnp.transpose(t, (1, 2, 0)) for t in small]
    return (
        output,
        d_input,
        norm,
        new[0],
        new[1],
        small[0],
        new[2],
        new[3],
        small[1],
        new[4],
        new[5],
        small[2],
        new[6],
        new[7],
        small[0].astype(BF),
    )


def solution(mesh):
    by_seq = P(None, "seq", None)
    by_band = P(None, "dp", "seq", None, None)
    by_frame = P(None, "dp", None, "seq", None)
    return jax.shard_map(
        body,
        mesh=mesh,
        in_specs=(by_band, by_frame, P(None, "dp")) + (by_seq,) * 9,
        out_specs=(by_frame, by_band, P()) + (by_seq,) * 12,
        check_vma=False,
    )
```
